128 devices in a mesh: group: 16 (over x, z), owner: 8 (over y, core).
Axes of the slice: x: 4, y: 4, z: 4, core: 2. Of those that a mesh axis runs over, the one named last changes fastest.
Arguments:
- embeddings: bfloat16 [131072, 1024], P(('group', 'owner')), may hold values from -2 to 2
- home_pairs: int32 [16, 8, 5, 64, 2], P('group', 'owner'), may hold values from 0 to 7, as said below
- home_count: int32 [16, 8, 5], P('group', 'owner'), may hold values from 0 to 20
- surplus_pairs: int32 [16, 8, 16, 3], P('group', 'owner'), may hold values from 0 to 7, as said below
Outputs:
- centered: bfloat16 [131072, 1024], P(('group', 'owner'))
- log_density: float32 [131072], P(('group', 'owner'))
The draws below stay inside these ranges and needn't reach their ends.
Inputs may be any that keep to these rules, and one draw needn't show every extreme that they name: `home_pairs`: for owner o of group g and distance s, the first home_count[g, o, s] slots hold distinct pairs (a, b) of block a of owner o and block b of owner (o + s) mod 8 that lie in one cluster; at distance 0 a <= b and every pair (a, a) is listed; at twice s equal to 8 only owners below 4 list pairs; later slots are ignored. `surplus_pairs`: A live entry (a, b, 1) names two blocks of the same owner in one cluster with a < b; no pair is live twice or also listed in home_pairs; dead entries are ignored.
All inputs are finite; a program needn't handle non-finite values.
Results may differ from the reference program's by a relative error of at most 0.0057.
Values may be sent and summed in bfloat16 or wider, within the bound.
No kernel may reach another device: no remote copies, remote signals or barrier semaphores. Data moves between devices by JAX's collectives and lax.ppermute only.
A program may use at most 128 MiB of HBM per device.

```python
import jax
import jax.numpy as jnp
from jax import lax

D = 1024
BLOCK = 128
BPD = 8
SHIFTS = 5
SLOTS = 64
ROWS = 131072
N_GROUP = 16
N_OWNER = 8


topic_count = 16


def offset_ranks(group_total):
    half_way = group_total // 2
    leading = [half_way, 1, group_total - 1, half_way + 1, half_way - 1, 2]
    others = [offset for offset in range(1, group_total) if offset not in leading]
    ordered = leading + others + [0]
    table = [0] * group_total
    for place in range(group_total):
        table[ordered[place]] = place
    return jnp.array(table, dtype=jnp.int32)


def pair_plan(base_key):
    sub_keys = jax.random.split(jax.random.fold_in(base_key, 7), 2)
    heavy_owner = jax.random.randint(sub_keys[0], (N_GROUP, 1, 1), 0, N_OWNER, jnp.int32)
    light_ids = jax.random.randint(sub_keys[1], (N_GROUP, N_OWNER, BPD), 1, 1 + 6 * BPD, jnp.int32)
    owner_ids = jnp.arange(N_OWNER, dtype=jnp.int32)
    cluster = jnp.where(owner_ids[None, :, None] == heavy_owner, 0, light_ids).astype(jnp.int32)
    distance = jnp.arange(SHIFTS, dtype=jnp.int32)
    partner = (owner_ids[:, None] + distance[None, :]) % N_OWNER
    partner_cluster = cluster[:, partner]
    same_cluster = cluster[:, :, None, :, None] == partner_cluster[:, :, :, None, :]
    block_ids = jnp.arange(BPD, dtype=jnp.int32)
    upper_tri = block_ids[:, None] <= block_ids[None, :]
    strict_upper = block_ids[:, None] < block_ids[None, :]
    at_zero = (distance == 0)[None, None, :, None, None]
    at_half = (2 * distance == N_OWNER)[None, None, :, None, None]
    low_owner = (owner_ids < N_OWNER // 2)[None, :, None, None, None]
    allowed = jnp.where(at_zero, upper_tri[None, None, None], True) & (jnp.logical_not(at_half) | low_owner)
    candidate = (same_cluster & allowed).reshape(N_GROUP, N_OWNER, SHIFTS, SLOTS)
    off_pairs = (same_cluster[:, :, 0] & strict_upper).reshape(N_GROUP, N_OWNER, SLOTS)
    rank = jnp.cumsum(off_pairs.astype(jnp.int32), axis=-1) - 1
    shipped = off_pairs & (rank < N_GROUP)
    home_zero = candidate[:, :, 0] & jnp.logical_not(shipped)
    home = candidate.at[:, :, 0].set(home_zero)
    positions = jnp.arange(SLOTS, dtype=jnp.int32)
    home_key = (1 - home.astype(jnp.int32)) * SLOTS + positions
    home_order = jnp.argsort(home_key, axis=-1, stable=True).astype(jnp.int32)
    home_pairs = jnp.stack([home_order // BPD, home_order % BPD], axis=-1).astype(jnp.int32)
    home_count = jnp.sum(home.astype(jnp.int32), axis=-1, dtype=jnp.int32)
    off_key = (1 - off_pairs.astype(jnp.int32)) * SLOTS + positions
    off_order = jnp.argsort(off_key, axis=-1, stable=True).astype(jnp.int32)
    off_count = jnp.sum(off_pairs.astype(jnp.int32), axis=-1, dtype=jnp.int32)
    group_ids = jnp.arange(N_GROUP, dtype=jnp.int32)
    rank_table_small = offset_ranks(N_GROUP)
    slot_rank = rank_table_small[(group_ids[None, :] - group_ids[:, None]) % N_GROUP]
    rank_table = jnp.broadcast_to(slot_rank[:, None, :], (N_GROUP, N_OWNER, N_GROUP))
    picked = jnp.take_along_axis(off_order, rank_table, axis=-1)
    live_flag = (rank_table < off_count[..., None]).astype(jnp.int32)
    surplus = jnp.stack([picked // BPD, picked % BPD, live_flag], axis=-1).astype(jnp.int32)
    return (home_pairs, home_count, surplus)


def draw_home_pairs(key, part):
    return pair_plan(key)[0]


def draw_home_count(key, part):
    return pair_plan(key)[1]


def draw_surplus_pairs(key, part):
    return pair_plan(key)[2]


def draw_embeddings(key, part):
    sub_keys = jax.random.split(jax.random.fold_in(key, 3), 4)
    centers = jax.random.normal(sub_keys[0], (topic_count, D), jnp.float32)
    topics = jax.random.randint(sub_keys[1], (ROWS,), 0, topic_count, jnp.int32)
    noise = jax.random.normal(sub_keys[2], (ROWS, D), jnp.float32)
    spread = jax.random.uniform(sub_keys[3], (ROWS, 1), jnp.float32, 0.4, 1.6)
    vectors = centers[topics] + spread * noise
    return jnp.clip(0.25 * vectors, -2.0, 2.0).astype(jnp.bfloat16)


def setup_inputs(seed: int = 0) -> dict:
    seeds = jax.random.split(jax.random.key(seed), 5)
    return {
        "embeddings": draw_embeddings(jax.random.fold_in(seeds[4], 71), 0),
        "home_pairs": draw_home_pairs(jax.random.fold_in(seeds[4], 71), 0),
        "home_count": draw_home_count(jax.random.fold_in(seeds[4], 71), 0),
        "surplus_pairs": draw_surplus_pairs(jax.random.fold_in(seeds[4], 71), 0),
    }


sharpness = 4.0
epsilon = 1e-06
batch_pairs = 16

def unit_rows(embeddings):
    widened = embeddings.astype(jnp.float32)
    inv_rms = lax.rsqrt(lax.optimization_barrier(jnp.mean(widened * widened, axis=-1, keepdims=True)) + epsilon)
    return (widened * inv_rms).astype(jnp.bfloat16)

def round_half(value):
    return lax.optimization_barrier(value.astype(jnp.bfloat16)).astype(jnp.float32)

def pair_terms(first_block, second_block):
    first_wide = first_block.astype(jnp.float32)
    second_wide = second_block.astype(jnp.float32)
    embed_width = first_block.shape[-1]
    similarity = jnp.einsum('nid,njd->nij', first_wide, second_wide) * (1.0 / embed_width)
    kernel = jnp.exp(sharpness * (similarity - 1.0))
    kernel_low = round_half(kernel)
    to_first = jnp.einsum('nij,njd->nid', kernel_low, second_wide)
    to_second = jnp.einsum('nij,nid->njd', kernel_low, first_wide)
    return (to_first, to_second, lax.optimization_barrier(jnp.sum(kernel, axis=2)), lax.optimization_barrier(jnp.sum(kernel, axis=1)))

def add_pairs(blocks, first_ids, second_ids, live_mask, second_scale, round_terms, totals):
    pad_ids = jnp.zeros((batch_pairs,), jnp.int32)
    first_ids = jnp.concatenate([first_ids.astype(jnp.int32), pad_ids])
    second_ids = jnp.concatenate([second_ids.astype(jnp.int32), pad_ids])
    live_mask = jnp.concatenate([live_mask.astype(jnp.int32), pad_ids])
    second_scale = jnp.concatenate([second_scale.astype(jnp.float32), jnp.zeros((batch_pairs,), jnp.float32)])
    live_first = jnp.argsort(1 - live_mask, stable=True).astype(jnp.int32)
    live_count = jnp.sum(live_mask, dtype=jnp.int32)

    def step(turn_index, carry):
        near_sums, near_dens, far_sums, far_dens = carry
        picked = lax.dynamic_slice_in_dim(live_first, turn_index * batch_pairs, batch_pairs, 0)
        positions = turn_index * batch_pairs + jnp.arange(batch_pairs, dtype=jnp.int32)
        keep_mask = (positions < live_count).astype(jnp.float32)
        first_pick = first_ids[picked]
        second_pick = second_ids[picked]
        to_first, to_second, dens_first, dens_second = pair_terms(blocks[first_pick], blocks[second_pick])
        if round_terms:
            to_first = round_half(to_first)
            to_second = round_half(to_second)
            dens_first = round_half(dens_first)
            dens_second = round_half(dens_second)
        other_mask = keep_mask * second_scale[picked]
        near_sums = near_sums.at[first_pick].add(to_first * keep_mask[:, None, None])
        near_dens = near_dens.at[first_pick].add(dens_first * keep_mask[:, None])
        far_sums = far_sums.at[second_pick].add(to_second * other_mask[:, None, None])
        far_dens = far_dens.at[second_pick].add(dens_second * other_mask[:, None])
        return (near_sums, near_dens, far_sums, far_dens)
    turn_count = (live_count + batch_pairs - 1) // batch_pairs
    return lax.fori_loop(0, turn_count, step, totals)

def reference(embeddings, home_pairs, home_count, surplus_pairs):
    normed = unit_rows(embeddings)
    embed_width = normed.shape[1]
    blocks = normed.reshape(-1, BLOCK, embed_width)
    block_count = blocks.shape[0]
    near_sums = jnp.zeros((block_count, BLOCK, embed_width), jnp.float32)
    near_dens = jnp.zeros((block_count, BLOCK), jnp.float32)
    groups = jnp.arange(N_GROUP, dtype=jnp.int32)[:, None, None]
    owners = jnp.arange(N_OWNER, dtype=jnp.int32)[None, :, None]
    slot_ids = jnp.arange(SLOTS, dtype=jnp.int32)[None, None, :]
    for distance in range(N_OWNER // 2 + 1):
        pair_list = home_pairs[:, :, distance]
        partner = (owners + distance) % N_OWNER
        first_ids = ((groups * N_OWNER + owners) * BPD + pair_list[..., 0]).reshape(-1)
        second_ids = ((groups * N_OWNER + partner) * BPD + pair_list[..., 1]).reshape(-1)
        live_mask = (slot_ids < home_count[:, :, distance][..., None]).astype(jnp.int32).reshape(-1)
        if distance == 0:
            second_scale = (first_ids != second_ids).astype(jnp.float32)
        else:
            second_scale = jnp.ones(first_ids.shape, jnp.float32)
        far_sums = jnp.zeros_like(near_sums)
        far_dens = jnp.zeros_like(near_dens)
        near_sums, near_dens, far_sums, far_dens = add_pairs(blocks, first_ids, second_ids, live_mask, second_scale, False, (near_sums, near_dens, far_sums, far_dens))
        if distance == 0:
            near_sums = near_sums + far_sums
            near_dens = near_dens + far_dens
        else:
            near_sums = near_sums + round_half(far_sums)
            near_dens = near_dens + round_half(far_dens)
    first_ids = ((groups * N_OWNER + owners) * BPD + surplus_pairs[..., 0]).reshape(-1)
    second_ids = ((groups * N_OWNER + owners) * BPD + surplus_pairs[..., 1]).reshape(-1)
    live_mask = surplus_pairs[..., 2].reshape(-1)
    second_scale = jnp.ones(first_ids.shape, jnp.float32)
    far_sums = jnp.zeros_like(near_sums)
    far_dens = jnp.zeros_like(near_dens)
    near_sums, near_dens, far_sums, far_dens = add_pairs(blocks, first_ids, second_ids, live_mask, second_scale, True, (near_sums, near_dens, far_sums, far_dens))
    near_sums = near_sums + far_sums
    near_dens = near_dens + far_dens
    log_density = jnp.log(near_dens).reshape(-1)
    centered = (blocks.astype(jnp.float32) - near_sums / near_dens[..., None]).astype(jnp.bfloat16)
    return (centered.reshape(-1, embed_width), log_density)
```

```python
import functools

import jax
import jax.numpy as jnp
from jax import lax
from jax.experimental import pallas as pl
from jax.experimental.pallas import tpu as pltpu
from jax.sharding import PartitionSpec as P

BLOCK = 128
sharpness = 4.0
epsilon = 1e-06
VMEM_BYTES = 56 * 2**20
CHIPS = 4


def along_chips(x, hops):
    route = [(o, ((o // 2 + hops) % CHIPS) * 2 + o % 2) for o in range(2 * CHIPS)]
    return lax.ppermute(x, "owner", route)


def to_sibling(x):
    return lax.ppermute(x, "owner", [(o, o ^ 1) for o in range(2 * CHIPS)])


def normalize_kernel(x_ref, u_ref):
    wide = x_ref[...].astype(jnp.float32)
    mean = jnp.mean(wide * wide, axis=-1, keepdims=True)
    u_ref[...] = (wide * lax.rsqrt(mean + epsilon)).astype(jnp.bfloat16)


def normalize(x):
    rows, width = x.shape
    step = 256
    return pl.pallas_call(
        normalize_kernel,
        grid=(rows // step,),
        in_specs=[pl.BlockSpec((step, width), lambda i: (i, 0))],
        out_specs=pl.BlockSpec((step, width), lambda i: (i, 0)),
        out_shape=jax.ShapeDtypeStruct(x.shape, jnp.bfloat16),
        compiler_params=pltpu.CompilerParams(vmem_limit_bytes=VMEM_BYTES),
        name="normalize",
    )(x)


def rows_of(block):
    return pl.ds(pl.multiple_of(block * BLOCK, BLOCK), BLOCK)


def add_terms(u_ref, q_ref, acc_ref, kacc_ref, mine, other):
    p = u_ref[rows_of(mine), :]
    q = q_ref[rows_of(other), :]
    dots = lax.dot_general(p, q, (((1,), (1,)), ((), ())), preferred_element_type=jnp.float32)
    kernel = jnp.exp(sharpness * (dots * (1.0 / q.shape[1]) - 1.0))
    kacc_ref[rows_of(mine), :] += kernel
    acc_ref[rows_of(mine), :] += jnp.dot(
        kernel.astype(jnp.bfloat16), q, preferred_element_type=jnp.float32
    )


def own_kernel(list_ref, surplus_ref, u_ref, acc_ref, kacc_ref):
    acc_ref[...] = jnp.zeros_like(acc_ref)
    kacc_ref[...] = jnp.zeros_like(kacc_ref)

    def both(a, b):
        add_terms(u_ref, u_ref, acc_ref, kacc_ref, a, b)

        @pl.when(a != b)
        def _():
            add_terms(u_ref, u_ref, acc_ref, kacc_ref, b, a)

    def home(t, carry):
        both(list_ref[0, 2 * t], list_ref[0, 2 * t + 1])
        return carry

    lax.fori_loop(0, list_ref[0, 128], home, 0)

    def surplus(t, carry):
        @pl.when(surplus_ref[t, 2] == 1)
        def _():
            both(surplus_ref[t, 0], surplus_ref[t, 1])

        return carry

    lax.fori_loop(0, surplus_ref.shape[0], surplus, 0)


def run_lists(core_ref, list_ref, rows, buffers, u_ref, acc_ref, kacc_ref):
    for (row0, row1), q_ref in zip(rows, buffers):
        row = jnp.where(core_ref[0] == 0, row0, row1)

        def step(t, carry):
            add_terms(u_ref, q_ref, acc_ref, kacc_ref, list_ref[row, 2 * t], list_ref[row, 2 * t + 1])
            return carry

        lax.fori_loop(0, list_ref[row, 128], step, 0)


def far_kernel(rows, core_ref, list_ref, u_ref, acc_in, kacc_in, *refs):
    buffers, (acc_ref, kacc_ref) = refs[:-2], refs[-2:]
    acc_ref[...] = acc_in[...]
    kacc_ref[...] = kacc_in[...]
    run_lists(core_ref, list_ref, rows, buffers, u_ref, acc_ref, kacc_ref)


def last_kernel(rows, core_ref, list_ref, u_ref, acc_in, kacc_in, *refs):
    buffers, (out_ref, log_ref, acc_ref, kacc_ref) = refs[:-4], refs[-4:]
    acc_ref[...] = acc_in[...]
    kacc_ref[...] = kacc_in[...]
    run_lists(core_ref, list_ref, rows, buffers, u_ref, acc_ref, kacc_ref)
    for block in range(out_ref.shape[0] // BLOCK):
        here = slice(block * BLOCK, (block + 1) * BLOCK)
        kernel = kacc_ref[here, :]
        density = jnp.sum(kernel, axis=1, keepdims=True)
        out_ref[here, :] = (
            u_ref[here, :].astype(jnp.float32) - acc_ref[here, :] / density
        ).astype(jnp.bfloat16)
        log_ref[block : block + 1, :] = jnp.log(jnp.sum(kernel.T, axis=0, keepdims=True))


SMEM = pl.BlockSpec(memory_space=pltpu.SMEM)
VMEM = pl.BlockSpec(memory_space=pltpu.VMEM)


def params():
    return pltpu.CompilerParams(vmem_limit_bytes=VMEM_BYTES)


def cost(pairs, width):
    return pl.CostEstimate(
        flops=pairs * 4 * BLOCK * BLOCK * width, bytes_accessed=8 * 2**20, transcendentals=pairs * BLOCK * BLOCK
    )


def shards(embeddings, home_pairs, home_count, surplus_pairs):
    rows, width = embeddings.shape
    pairs, count = home_pairs[0, 0], home_count[0, 0]
    shifts = pairs.shape[0]

    def table(listed):
        return jnp.concatenate(
            [listed.reshape(shifts, -1), count[:, None], jnp.zeros((shifts, 7), jnp.int32)], axis=1
        )

    mine = table(pairs)
    turned = table(pairs[:, :, ::-1])
    owners = 2 * CHIPS
    theirs = [
        lax.ppermute(turned[s : s + 1], "owner", [(o, (o + s) % owners) for o in range(owners)])
        for s in range(1, shifts)
    ]
    lists = jnp.concatenate([mine] + theirs, axis=0)
    core = (lax.axis_index("owner") % 2).astype(jnp.int32).reshape(1)

    unit = normalize(embeddings)
    half = rows // 2
    low, high = unit[:half], unit[half:]
    b_low, a_high = along_chips(low, 1), along_chips(high, -1)
    b_high, a_low = along_chips(high, 1), along_chips(low, -1)
    sib = to_sibling(unit)
    o_low, o_high = along_chips(b_low, 1), along_chips(a_high, -1)

    below = jnp.concatenate([b_low, b_high], axis=0)
    above = jnp.concatenate([a_low, a_high], axis=0)
    below_x, above_x = to_sibling(below), to_sibling(above)
    opposite = jnp.concatenate([o_low, o_high], axis=0)
    opposite_x = to_sibling(opposite)

    sums = (
        jax.ShapeDtypeStruct((rows, width), jnp.float32),
        jax.ShapeDtypeStruct((rows, BLOCK), jnp.float32),
    )
    acc, kacc = pl.pallas_call(
        own_kernel,
        in_specs=[SMEM, SMEM, VMEM],
        out_specs=(VMEM, VMEM),
        out_shape=sums,
        compiler_params=params(),
        cost_estimate=cost(64, width),
        name="own_pairs",
    )(mine, surplus_pairs[0, 0], unit)

    acc, kacc = pl.pallas_call(
        functools.partial(far_kernel, ((1, 5), (2, 2), (3, 1), (6, 6), (5, 7))),
        in_specs=[SMEM, SMEM] + [VMEM] * 8,
        out_specs=(VMEM, VMEM),
        out_shape=sums,
        compiler_params=params(),
        cost_estimate=cost(12, width),
        name="near_pairs",
    )(core, lists, unit, acc, kacc, sib, above, above_x, below, below_x)

    centered, log_density = pl.pallas_call(
        functools.partial(last_kernel, ((4, 4), (8, 8), (7, 3))),
        in_specs=[SMEM, SMEM] + [VMEM] * 6,
        out_specs=(VMEM, VMEM),
        out_shape=(
            jax.ShapeDtypeStruct((rows, width), jnp.bfloat16),
            jax.ShapeDtypeStruct((rows // BLOCK, BLOCK), jnp.float32),
        ),
        scratch_shapes=[pltpu.VMEM((rows, width), jnp.float32), pltpu.VMEM((rows, BLOCK), jnp.float32)],
        compiler_params=params(),
        cost_estimate=cost(8, width),
        name="opposite_pairs",
    )(core, lists, unit, acc, kacc, opposite, opposite, opposite_x)
    return centered, log_density.reshape(rows)


def solution(mesh):
    return jax.shard_map(
        shards,
        mesh=mesh,
        in_specs=(
            P(("group", "owner"), None),
            P("group", "owner", None, None, None),
            P("group", "owner", None),
            P("group", "owner", None, None),
        ),
        out_specs=(P(("group", "owner"), None), P(("group", "owner"))),
        check_vma=False,
    )
```

```python
import functools

import jax
import jax.numpy as jnp
from jax import lax
from jax.experimental import pallas as pl
from jax.experimental.pallas import tpu as pltpu
from jax.sharding import PartitionSpec as P

BLOCK = 128
BPD = 8
CHIPS = 4
OWNERS = 8
BLOCKS = OWNERS * BPD
ON_CHIP = 2 * BPD
sharpness = 4.0
epsilon = 1e-06
VMEM_BYTES = 56 * 2**20
SIZES = ((2, 1), (2, 2), (3, 2), (3, 3), (4, 3), (4, 4), (8, 8))
COUNT = 64

TASK, TASKS, F_COUNT, D_COUNT, F_LIST, D_LIST, NEED, PLACE, LOAD, CLASS = (
    0, 1024, 1040, 1048, 1056, 1184, 1312, 1376, 1440, 1448
)
PLAN = 1536


def along_chips(x, hops):
    route = [(o, ((o // 2 + hops) % CHIPS) * 2 + o % 2) for o in range(OWNERS)]
    return lax.ppermute(x, "owner", route)


def to_sibling(x):
    return lax.ppermute(x, "owner", [(o, o ^ 1) for o in range(OWNERS)])


def normalize_kernel(x_ref, u_ref):
    wide = x_ref[...].astype(jnp.float32)
    mean = jnp.mean(wide * wide, axis=-1, keepdims=True)
    u_ref[...] = (wide * lax.rsqrt(mean + epsilon)).astype(jnp.bfloat16)


def rows_of(block):
    return pl.ds(pl.multiple_of(block * BLOCK, BLOCK), BLOCK)


def kernel_values(p, q):
    dots = lax.dot_general(p, q, (((1,), (1,)), ((), ())), preferred_element_type=jnp.float32)
    return jnp.exp(sharpness * (dots * (1.0 / q.shape[1]) - 1.0))


def add_terms(u_ref, q_ref, acc_ref, kacc_ref, mine, other):
    q = q_ref[rows_of(other), :]
    kernel = kernel_values(u_ref[rows_of(mine), :], q)
    kacc_ref[rows_of(mine), :] += kernel
    acc_ref[rows_of(mine), :] += jnp.dot(
        kernel.astype(jnp.bfloat16), q, preferred_element_type=jnp.float32
    )


def plan_kernel(pos_ref, tab_ref, plan_ref, class_ref):
    y, core = pos_ref[0], pos_ref[1]
    me = 2 * y + core

    def loop(count, body):
        def step(i, carry):
            body(i)
            return carry

        lax.fori_loop(0, count, step, 0)

    def clear(start, count):
        @functools.partial(loop, count)
        def _(i):
            plan_ref[start + i] = 0

    def bump(index, by):
        plan_ref[index] = plan_ref[index] + by

    clear(TASKS, 32)
    clear(NEED, 64)
    clear(LOAD, 8)

    @functools.partial(loop, OWNERS)
    def _(o):
        for s in range(1, 5):
            q = lax.rem(o + s, OWNERS)

            @functools.partial(loop, tab_ref[o * 8 + s, COUNT])
            def _(t):
                pair = tab_ref[o * 8 + s, t]
                first, second = NEED + o * BPD + pair // 8, NEED + q * BPD + lax.rem(pair, 8)
                plan_ref[first] = plan_ref[first] | lax.shift_left(1, q // 2)
                plan_ref[second] = plan_ref[second] | lax.shift_left(1, o // 2)

    def needs(block):
        chip = block // ON_CHIP
        mask = plan_ref[NEED + block]
        bit = lambda hop: lax.shift_right_logical(mask, lax.rem(chip + hop, CHIPS)) & 1
        return chip, bit(1), bit(3), bit(2)

    def append(count, table, chip, way, block):
        at = count + 2 * chip + way
        plan_ref[table + (2 * chip + way) * 16 + plan_ref[at]] = block
        plan_ref[at] = plan_ref[at] + 1

    @functools.partial(loop, BLOCKS)
    def _(block):
        chip, up, down, far = needs(block)

        @pl.when((up + down) > 0)
        def _():
            bump(LOAD + 2 * chip, up)
            bump(LOAD + 2 * chip + 1, down)

            @pl.when(far == 0)
            def _():
                @pl.when(up == 1)
                def _():
                    append(D_COUNT, D_LIST, chip, 0, block)

                @pl.when(down == 1)
                def _():
                    append(D_COUNT, D_LIST, chip, 1, block)

    @functools.partial(loop, BLOCKS)
    def _(block):
        chip, up, down, far = needs(block)

        @pl.when(far == 1)
        def _():
            a0, a1 = LOAD + 2 * chip, LOAD + 2 * lax.rem(chip + 1, CHIPS)
            b0, b1 = LOAD + 2 * chip + 1, LOAD + 2 * lax.rem(chip + 3, CHIPS) + 1
            up0, up1 = plan_ref[a0] + 1 - up, plan_ref[a1] + 1
            down0, down1 = plan_ref[b0] + 1 - down, plan_ref[b1] + 1
            up_cost = jnp.maximum(up0, up1) * 64 + up0 + up1 + 32 * (1 - up)
            down_cost = jnp.maximum(down0, down1) * 64 + down0 + down1 + 32 * (1 - down)
            goes_up = up_cost <= down_cost

            @pl.when(goes_up)
            def _():
                plan_ref[a0] = up0
                plan_ref[a1] = up1
                append(F_COUNT, F_LIST, chip, 0, block)

                @pl.when(down == 1)
                def _():
                    append(D_COUNT, D_LIST, chip, 1, block)

            @pl.when(jnp.logical_not(goes_up))
            def _():
                plan_ref[b0] = down0
                plan_ref[b1] = down1
                append(F_COUNT, F_LIST, chip, 1, block)

                @pl.when(up == 1)
                def _():
                    append(D_COUNT, D_LIST, chip, 0, block)

    chosen, first_size = len(SIZES) - 1, 2 * SIZES[-1][0]
    for k in range(len(SIZES) - 2, -1, -1):
        first, second = 2 * SIZES[k][0], 2 * SIZES[k][1]
        fits = None
        for chip in range(CHIPS):
            for way in (0, 1):
                before = (chip + (3 if way == 0 else 1)) % CHIPS
                twice, once = plan_ref[F_COUNT + 2 * chip + way], plan_ref[D_COUNT + 2 * chip + way]
                passing = plan_ref[F_COUNT + 2 * before + way]
                fit = (twice <= first) & (passing + jnp.maximum(twice + once - first, 0) <= second)
                fits = fit if fits is None else fits & fit
        chosen = jnp.where(fits, k, chosen)
        first_size = jnp.where(fits, first, first_size)
    class_ref[0] = chosen

    def put(block, stage, way, position):
        other = (lax.rem(position, 2) != core).astype(jnp.int32)
        plan_ref[PLACE + block] = stage * 65536 + (way * 2 + other) * 256 + position // 2

    for way in (0, 1):
        near = 2 * lax.rem(y + (3 if way == 0 else 1), CHIPS) + way
        far = 2 * lax.rem(y + 2, CHIPS) + way
        twice = plan_ref[F_COUNT + near]

        @functools.partial(loop, twice)
        def _(i):
            put(plan_ref[F_LIST + near * 16 + i], 0, way, i)

        passing = plan_ref[F_COUNT + far]

        @functools.partial(loop, plan_ref[D_COUNT + near])
        def _(i):
            late = (twice + i >= first_size).astype(jnp.int32)
            put(
                plan_ref[D_LIST + near * 16 + i],
                late,
                way,
                twice + i + late * (passing - first_size),
            )

        @functools.partial(loop, passing)
        def _(i):
            put(plan_ref[F_LIST + far * 16 + i], 1, way, i)

    def add_task(own, block):
        place = plan_ref[PLACE + block]
        row = (place // 65536) * BPD + own
        count = plan_ref[TASKS + row]
        plan_ref[TASK + row * 64 + count] = lax.rem(place, 65536)
        plan_ref[TASKS + row] = count + 1

    for s in range(1, 5):
        above, below = lax.rem(me + s, OWNERS), lax.rem(me + OWNERS - s, OWNERS)

        @pl.when(above // 2 != y)
        def _():
            @functools.partial(loop, tab_ref[me * 8 + s, COUNT])
            def _(t):
                pair = tab_ref[me * 8 + s, t]
                add_task(pair // 8, above * BPD + lax.rem(pair, 8))

        @pl.when(below // 2 != y)
        def _():
            @functools.partial(loop, tab_ref[below * 8 + s, COUNT])
            def _(t):
                pair = tab_ref[below * 8 + s, t]
                add_task(lax.rem(pair, 8), below * BPD + pair // 8)


def start_from(id_, core, unit_ref, sib_ref, dst, sem):
    here = rows_of(lax.rem(id_, BPD))
    mine = lax.rem(id_ // BPD, 2) == core

    @pl.when(mine)
    def _():
        pltpu.make_async_copy(unit_ref.at[here, :], dst, sem).start()

    @pl.when(jnp.logical_not(mine))
    def _():
        pltpu.make_async_copy(sib_ref.at[here, :], dst, sem).start()


def listed(plan_ref, row, i, chip):
    twice, once = plan_ref[F_COUNT + row], plan_ref[D_COUNT + row]
    from_f = plan_ref[F_LIST + row * 16 + jnp.clip(i, 0, 15)]
    from_d = plan_ref[D_LIST + row * 16 + jnp.clip(i - twice, 0, 15)]
    found = jnp.where(i < twice, from_f, from_d)
    return jnp.where(i < twice + once, found, chip * ON_CHIP)


def first_pack_kernel(size, pos_ref, plan_ref, unit_ref, sib_ref, up_ref, down_ref, sems):
    y, core = pos_ref[0], pos_ref[1]
    slots = [(way, j, out) for way, out in ((0, up_ref), (1, down_ref)) for j in range(size)]
    for n, (way, j, out) in enumerate(slots):
        block = listed(plan_ref, 2 * y + way, 2 * j + core, y)
        start_from(block, core, unit_ref, sib_ref, out.at[j * BLOCK : (j + 1) * BLOCK, :], sems.at[n])
    for n, (way, j, out) in enumerate(slots):
        pltpu.make_async_copy(
            unit_ref.at[0:BLOCK, :], out.at[j * BLOCK : (j + 1) * BLOCK, :], sems.at[n]
        ).wait()


def second_pack_kernel(
    first, size, pos_ref, plan_ref, unit_ref, sib_ref, got_up, got_down, acc_ref, up_ref, down_ref, sems
):
    y, core = pos_ref[0], pos_ref[1]
    slots = [
        (way, j, out, got)
        for way, out, got in ((0, up_ref, got_up), (1, down_ref, got_down))
        for j in range(size)
    ]
    for n, (way, j, out, got) in enumerate(slots):
        dst = out.at[j * BLOCK : (j + 1) * BLOCK, :]
        position = 2 * j + core
        passing = plan_ref[F_COUNT + 2 * lax.rem(y + (3 if way == 0 else 1), CHIPS) + way]
        passes = (position < passing) if j < first else (position < 0)
        if j < first:

            @pl.when(passes)
            def _():
                pltpu.make_async_copy(got.at[j * BLOCK : (j + 1) * BLOCK, :], dst, sems.at[n]).start()

        @pl.when(jnp.logical_not(passes))
        def _():
            block = listed(plan_ref, 2 * y + way, position - passing + 2 * first, y)
            start_from(block, core, unit_ref, sib_ref, dst, sems.at[n])

    for n, (way, j, out, got) in enumerate(slots):
        pltpu.make_async_copy(
            unit_ref.at[0:BLOCK, :], out.at[j * BLOCK : (j + 1) * BLOCK, :], sems.at[n]
        ).wait()


def own_kernel(pos_ref, tab_ref, surplus_ref, u_ref, sib_ref, acc_ref, kacc_ref, live_ref):
    y, core = pos_ref[0], pos_ref[1]
    me = 2 * y + core

    def loop(count, body):
        def step(i, carry):
            body(i)
            return carry

        lax.fori_loop(0, count, step, 0)

    @functools.partial(loop, BPD * BPD)
    def _(i):
        live_ref[i] = 0.0

    def mark(a, b):
        live_ref[a * BPD + b] = 1.0
        live_ref[b * BPD + a] = 1.0

    @functools.partial(loop, tab_ref[me * 8, COUNT])
    def _(t):
        pair = tab_ref[me * 8, t]
        mark(pair // 8, lax.rem(pair, 8))

    @functools.partial(loop, surplus_ref.shape[0])
    def _(t):
        @pl.when(surplus_ref[t, 2] == 1)
        def _():
            mark(surplus_ref[t, 0], surplus_ref[t, 1])

    step = 2

    @functools.partial(loop, BPD // step)
    def _(part):
        here = pl.ds(pl.multiple_of(part * step * BLOCK, step * BLOCK), step * BLOCK)
        kernel = kernel_values(u_ref[here, :], u_ref[...])
        rows = []
        for i in range(step):
            parts = [
                kernel[i * BLOCK : (i + 1) * BLOCK, j * BLOCK : (j + 1) * BLOCK]
                * live_ref[(part * step + i) * BPD + j]
                for j in range(BPD)
            ]
            kacc_ref[rows_of(part * step + i), :] = sum(parts)
            rows.append(jnp.concatenate(parts, axis=1).astype(jnp.bfloat16))
        acc_ref[here, :] = jnp.dot(
            jnp.concatenate(rows, axis=0), u_ref[...], preferred_element_type=jnp.float32
        )

    even = 2 * y * 8 + 1

    @functools.partial(loop, tab_ref[even, COUNT])
    def _(t):
        pair = tab_ref[even, t]
        a, b = pair // 8, lax.rem(pair, 8)
        mine, other = jnp.where(core == 0, a, b), jnp.where(core == 0, b, a)
        add_terms(u_ref, sib_ref, acc_ref, kacc_ref, mine, other)


def run_tasks(stage, size, plan_ref, u_ref, q_ref, acc_ref, kacc_ref):
    def per_block(own, carry):
        row = stage * BPD + own

        def step(t, inner):
            place = plan_ref[TASK + row * 64 + t]
            add_terms(
                u_ref, q_ref, acc_ref, kacc_ref, own, (place // 256) * size + lax.rem(place, 256)
            )
            return inner

        lax.fori_loop(0, plan_ref[TASKS + row], step, 0)
        return carry

    lax.fori_loop(0, BPD, per_block, 0)


def fetch(size, sources, q_ref, sems):
    copies = [
        pltpu.make_async_copy(
            source, q_ref.at[n * size * BLOCK : (n + 1) * size * BLOCK, :], sems.at[n]
        )
        for n, source in enumerate(sources)
    ]
    for copy in copies:
        copy.start()
    for copy in copies:
        copy.wait()


def near_kernel(size, plan_ref, u_ref, acc_in, kacc_in, g0, g1, g2, g3, acc_ref, kacc_ref, q_ref, sems):
    acc_ref[...] = acc_in[...]
    kacc_ref[...] = kacc_in[...]
    fetch(size, (g0, g1, g2, g3), q_ref, sems)
    run_tasks(0, size, plan_ref, u_ref, q_ref, acc_ref, kacc_ref)


def last_kernel(
    size, plan_ref, u_ref, acc_in, kacc_in, g0, g1, g2, g3, out_ref, log_ref, acc_ref, kacc_ref, q_ref, sems
):
    own = pl.program_id(0)

    @pl.when(own == 0)
    def _():
        fetch(size, (g0, g1, g2, g3), q_ref, sems)

    acc_ref[...] = acc_in[...]
    kacc_ref[...] = kacc_in[...]
    row = BPD + own

    def step(t, carry):
        place = plan_ref[TASK + row * 64 + t]
        add_terms(
            u_ref, q_ref, acc_ref, kacc_ref, 0, (place // 256) * size + lax.rem(place, 256)
        )
        return carry

    lax.fori_loop(0, plan_ref[TASKS + row], step, 0)
    kernel = kacc_ref[...]
    density = jnp.sum(kernel, axis=1, keepdims=True)
    out_ref[...] = (u_ref[...].astype(jnp.float32) - acc_ref[...] / density).astype(jnp.bfloat16)
    log_ref[pl.ds(own, 1), :] = jnp.log(jnp.sum(kernel.T, axis=0, keepdims=True))


SMEM = pl.BlockSpec(memory_space=pltpu.SMEM)
VMEM = pl.BlockSpec(memory_space=pltpu.VMEM)
ANY = pl.BlockSpec(memory_space=pl.ANY)


def params():
    return pltpu.CompilerParams(vmem_limit_bytes=VMEM_BYTES)


def cost(pairs, width):
    return pl.CostEstimate(
        flops=pairs * 4 * BLOCK * BLOCK * width, bytes_accessed=8 * 2**20, transcendentals=pairs * BLOCK * BLOCK
    )


def exchange_and_score(first, second, pos, plan, tables, surplus, unit, sib):
    rows, width = unit.shape
    sends = lambda size: tuple(jax.ShapeDtypeStruct((size * BLOCK, width), jnp.bfloat16) for _ in range(2))
    sums = (
        jax.ShapeDtypeStruct((rows, width), jnp.float32),
        jax.ShapeDtypeStruct((rows, BLOCK), jnp.float32),
    )
    up, down = pl.pallas_call(
        functools.partial(first_pack_kernel, first),
        in_specs=[SMEM, SMEM, ANY, ANY],
        out_specs=(ANY, ANY),
        out_shape=sends(first),
        scratch_shapes=[pltpu.SemaphoreType.DMA((2 * first,))],
        name="first_pack",
    )(pos, plan, unit, sib)
    got_up, got_down = along_chips(up, 1), along_chips(down, -1)

    acc, kacc = pl.pallas_call(
        own_kernel,
        in_specs=[SMEM, SMEM, SMEM, VMEM, VMEM],
        out_specs=(VMEM, VMEM),
        out_shape=sums,
        scratch_shapes=[pltpu.SMEM((BPD * BPD,), jnp.float32)],
        compiler_params=params(),
        cost_estimate=cost(64, width),
        name="own_pairs",
    )(pos, tables, surplus, unit, sib)

    up, down = pl.pallas_call(
        functools.partial(second_pack_kernel, first, second),
        in_specs=[SMEM, SMEM] + [ANY] * 5,
        out_specs=(ANY, ANY),
        out_shape=sends(second),
        scratch_shapes=[pltpu.SemaphoreType.DMA((2 * second,))],
        name="second_pack",
    )(pos, plan, unit, sib, got_up, got_down, acc)
    far_up, far_down = along_chips(up, 1), along_chips(down, -1)
    sib_up, sib_down = to_sibling(got_up), to_sibling(got_down)

    acc, kacc = pl.pallas_call(
        functools.partial(near_kernel, first),
        in_specs=[SMEM, VMEM, VMEM, VMEM] + [ANY] * 4,
        out_specs=(VMEM, VMEM),
        out_shape=sums,
        scratch_shapes=[
            pltpu.VMEM((4 * first * BLOCK, width), jnp.bfloat16),
            pltpu.SemaphoreType.DMA((4,)),
        ],
        compiler_params=params(),
        cost_estimate=cost(12, width),
        name="near_pairs",
    )(plan, unit, acc, kacc, got_up, sib_up, got_down, sib_down)

    far_up, far_down, acc = lax.optimization_barrier((far_up, far_down, acc))
    far_sib_up, far_sib_down = to_sibling(far_up), to_sibling(far_down)
    of_block = lambda w: pl.BlockSpec((BLOCK, w), lambda i: (i, 0))
    centered, log_density = pl.pallas_call(
        functools.partial(last_kernel, second),
        grid=(BPD,),
        in_specs=[SMEM, of_block(width), of_block(width), of_block(BLOCK)] + [ANY] * 4,
        out_specs=(of_block(width), pl.BlockSpec((BPD, BLOCK), lambda i: (0, 0))),
        out_shape=(
            jax.ShapeDtypeStruct((rows, width), jnp.bfloat16),
            jax.ShapeDtypeStruct((BPD, BLOCK), jnp.float32),
        ),
        scratch_shapes=[
            pltpu.VMEM((BLOCK, width), jnp.float32),
            pltpu.VMEM((BLOCK, BLOCK), jnp.float32),
            pltpu.VMEM((4 * second * BLOCK, width), jnp.bfloat16),
            pltpu.SemaphoreType.DMA((4,)),
        ],
        compiler_params=params(),
        cost_estimate=cost(8, width),
        name="far_pairs",
    )(plan, unit, acc, kacc, far_up, far_sib_up, far_down, far_sib_down)
    return centered, log_density


def shards(embeddings, home_pairs, home_count, surplus_pairs):
    rows, width = embeddings.shape
    pairs, count = home_pairs[0, 0], home_count[0, 0]
    shifts = pairs.shape[0]
    me = lax.axis_index("owner").astype(jnp.int32)
    pos = jnp.stack([me // 2, me % 2])

    table = jnp.pad(
        jnp.concatenate([pairs[:, :, 0] * 8 + pairs[:, :, 1], count[:, None]], axis=1),
        ((0, 8 - shifts), (0, 128 - pairs.shape[1] - 1)),
    )
    spread = jnp.where(jnp.arange(OWNERS, dtype=jnp.int32)[:, None, None] == me, table[None], 0)
    tables = lax.psum(spread, "owner").reshape(OWNERS * 8, 128)

    step = 128
    unit = pl.pallas_call(
        normalize_kernel,
        grid=(rows // step,),
        in_specs=[pl.BlockSpec((step, width), lambda i: (i, 0))],
        out_specs=pl.BlockSpec((step, width), lambda i: (i, 0)),
        out_shape=jax.ShapeDtypeStruct(embeddings.shape, jnp.bfloat16),
        name="normalize",
    )(embeddings)
    sib = to_sibling(unit)

    plan, chosen = pl.pallas_call(
        plan_kernel,
        in_specs=[SMEM, SMEM],
        out_specs=(SMEM, SMEM),
        out_shape=(
            jax.ShapeDtypeStruct((PLAN,), jnp.int32),
            jax.ShapeDtypeStruct((1,), jnp.int32),
        ),
        name="plan",
    )(pos, tables)

    centered, log_density = lax.switch(
        chosen[0],
        [functools.partial(exchange_and_score, *size) for size in SIZES],
        pos, plan, tables, surplus_pairs[0, 0], unit, sib,
    )
    return centered, log_density.reshape(rows)


def solution(mesh):
    return jax.shard_map(
        shards,
        mesh=mesh,
        in_specs=(
            P(("group", "owner"), None),
            P("group", "owner", None, None, None),
            P("group", "owner", None),
            P("group", "owner", None, None),
        ),
        out_specs=(P(("group", "owner"), None), P(("group", "owner"))),
        check_vma=False,
    )
```

```python
import functools

import jax
import jax.numpy as jnp
from jax import lax
from jax.experimental import pallas as pl
from jax.experimental.pallas import tpu as pltpu
from jax.sharding import PartitionSpec as P

BLOCK = 128
BPD = 8
CHIPS = 4
OWNERS = 8
BLOCKS = OWNERS * BPD
ON_CHIP = 2 * BPD
sharpness = 4.0
epsilon = 1e-06
VMEM_BYTES = 56 * 2**20
SIZES = ((2, 1), (2, 2), (3, 2), (3, 3), (4, 3), (4, 4), (8, 8))
MOST = 20
ENTRY = MOST + 1

F_COUNT, D_COUNT, F_LIST, D_LIST, NEED, LOAD, FIRST = 0, 8, 16, 144, 272, 336, 344
PLAN = 384
TASKS, TASK, PLACE = 0, 16, 1040
PLACES = 1152


def loop(count, body):
    def step(i, carry):
        body(i)
        return carry

    lax.fori_loop(0, count, step, 0)


def along_chips(x, hops):
    route = [(o, ((o // 2 + hops) % CHIPS) * 2 + o % 2) for o in range(OWNERS)]
    return lax.ppermute(x, "owner", route)


def to_sibling(x):
    return lax.ppermute(x, "owner", [(o, o ^ 1) for o in range(OWNERS)])


def normalize_kernel(x_ref, u_ref):
    wide = x_ref[...].astype(jnp.float32)
    mean = jnp.mean(wide * wide, axis=-1, keepdims=True)
    u_ref[...] = (wide * lax.rsqrt(mean + epsilon)).astype(jnp.bfloat16)


def rows_of(block):
    return pl.ds(pl.multiple_of(block * BLOCK, BLOCK), BLOCK)


def kernel_values(p, q):
    dots = lax.dot_general(p, q, (((1,), (1,)), ((), ())), preferred_element_type=jnp.float32)
    return jnp.exp(sharpness * (dots * (1.0 / q.shape[1]) - 1.0))


def add_terms(u_ref, q_ref, acc_ref, kacc_ref, mine, other):
    q = q_ref[rows_of(other), :]
    kernel = kernel_values(u_ref[rows_of(mine), :], q)
    kacc_ref[rows_of(mine), :] += kernel
    acc_ref[rows_of(mine), :] += jnp.dot(
        kernel.astype(jnp.bfloat16), q, preferred_element_type=jnp.float32
    )


def plan_kernel(pos_ref, tab_ref, plan_ref, class_ref):
    me = pos_ref[0]

    @functools.partial(loop, BLOCKS)
    def _(i):
        plan_ref[NEED + i] = 0

    for i in range(8):
        plan_ref[LOAD + i] = 0
        plan_ref[F_COUNT + i] = 0
        plan_ref[D_COUNT + i] = 0

    @functools.partial(loop, OWNERS)
    def _(o):
        row = o ^ me
        for s in range(1, 5):
            q = (o + s) & 7
            to_q, to_o = lax.shift_left(1, q >> 1), lax.shift_left(1, o >> 1)

            @functools.partial(loop, tab_ref[row, s * ENTRY])
            def _(t):
                pair = tab_ref[row, s * ENTRY + 1 + t]
                first, second = NEED + o * BPD + (pair >> 3), NEED + q * BPD + (pair & 7)
                plan_ref[first] = plan_ref[first] | to_q
                plan_ref[second] = plan_ref[second] | to_o

    def append(count, table, chip, way, block):
        at = 2 * chip + way
        held = plan_ref[count + at]
        plan_ref[table + at * 16 + held] = block
        plan_ref[count + at] = held + 1

    def visit(body):
        @functools.partial(loop, BLOCKS)
        def _(block):
            mask = plan_ref[NEED + block]

            @pl.when(mask != 0)
            def _():
                chip = block >> 4
                bit = lambda hop: lax.shift_right_logical(mask, (chip + hop) & 3) & 1
                body(block, chip, bit(1), bit(3), bit(2))

    @visit
    def _(block, chip, up, down, far):
        at = LOAD + 2 * chip
        plan_ref[at] = plan_ref[at] + up
        plan_ref[at + 1] = plan_ref[at + 1] + down

        @pl.when(up > far)
        def _():
            append(D_COUNT, D_LIST, chip, 0, block)

        @pl.when(down > far)
        def _():
            append(D_COUNT, D_LIST, chip, 1, block)

    @visit
    def _(block, chip, up, down, far):
        @pl.when(far == 1)
        def _():
            a0, a1 = LOAD + 2 * chip, LOAD + 2 * ((chip + 1) & 3)
            b0, b1 = LOAD + 2 * chip + 1, LOAD + 2 * ((chip + 3) & 3) + 1
            up0, up1 = plan_ref[a0] + 1 - up, plan_ref[a1] + 1
            down0, down1 = plan_ref[b0] + 1 - down, plan_ref[b1] + 1
            up_most = jnp.maximum(jnp.maximum(up0, up1), 2 * plan_ref[F_COUNT + 2 * chip] + 2)
            down_most = jnp.maximum(jnp.maximum(down0, down1), 2 * plan_ref[F_COUNT + 2 * chip + 1] + 2)
            up_cost = up_most * 64 + up0 + up1 + 32 * (1 - up)
            down_cost = down_most * 64 + down0 + down1 + 32 * (1 - down)

            @pl.when(up_cost <= down_cost)
            def _():
                plan_ref[a0] = up0
                plan_ref[a1] = up1
                append(F_COUNT, F_LIST, chip, 0, block)

                @pl.when(down == 1)
                def _():
                    append(D_COUNT, D_LIST, chip, 1, block)

            @pl.when(up_cost > down_cost)
            def _():
                plan_ref[b0] = down0
                plan_ref[b1] = down1
                append(F_COUNT, F_LIST, chip, 1, block)

                @pl.when(up == 1)
                def _():
                    append(D_COUNT, D_LIST, chip, 0, block)

    twice = [plan_ref[F_COUNT + i] for i in range(8)]
    once = [plan_ref[D_COUNT + i] for i in range(8)]
    longest = functools.reduce(jnp.maximum, twice)
    second_needs = {}
    for size in sorted({size for size, _ in SIZES}):
        needs = []
        for i in range(8):
            before = (i + (6 if i % 2 == 0 else 2)) % 8
            needs.append(twice[before] + jnp.maximum(twice[i] + once[i] - 2 * size, 0))
        second_needs[size] = functools.reduce(jnp.maximum, needs)
    chosen, first_size = len(SIZES) - 1, 2 * SIZES[-1][0]
    for k in range(len(SIZES) - 2, -1, -1):
        first, second = SIZES[k]
        fits = (longest <= 2 * first) & (second_needs[first] <= 2 * second)
        chosen = jnp.where(fits, k, chosen)
        first_size = jnp.where(fits, 2 * first, first_size)
    class_ref[0] = chosen
    plan_ref[FIRST] = first_size


def places_kernel(pos_ref, tab_ref, plan_ref, out_ref):
    me = pos_ref[0]
    y, core = me >> 1, me & 1
    first_size = plan_ref[FIRST]
    for i in range(16):
        out_ref[TASKS + i] = 0

    def put(block, stage, way, position):
        other = (position & 1) ^ core
        out_ref[PLACE + block] = stage * 65536 + (way * 2 + other) * 256 + (position >> 1)

    for way in (0, 1):
        near = 2 * ((y + (3 if way == 0 else 1)) & 3) + way
        far = 2 * ((y + 2) & 3) + way
        twice, passing = plan_ref[F_COUNT + near], plan_ref[F_COUNT + far]

        @functools.partial(loop, twice)
        def _(i):
            put(plan_ref[F_LIST + near * 16 + i], 0, way, i)

        @functools.partial(loop, plan_ref[D_COUNT + near])
        def _(i):
            late = (twice + i >= first_size).astype(jnp.int32)
            put(plan_ref[D_LIST + near * 16 + i], late, way, twice + i + late * (passing - first_size))

        @functools.partial(loop, passing)
        def _(i):
            put(plan_ref[F_LIST + far * 16 + i], 1, way, i)

    def add_task(own, block):
        place = out_ref[PLACE + block]
        row = (place >> 16) * BPD + own
        count = out_ref[TASKS + row]
        out_ref[TASK + row * 64 + count] = place & 65535
        out_ref[TASKS + row] = count + 1

    for s in range(1, 5):
        above, below = (me + s) & 7, (me - s) & 7

        @pl.when((above >> 1) != y)
        def _():
            @functools.partial(loop, tab_ref[0, s * ENTRY])
            def _(t):
                pair = tab_ref[0, s * ENTRY + 1 + t]
                add_task(pair >> 3, above * BPD + (pair & 7))

        @pl.when((below >> 1) != y)
        def _():
            row = below ^ me

            @functools.partial(loop, tab_ref[row, s * ENTRY])
            def _(t):
                pair = tab_ref[row, s * ENTRY + 1 + t]
                add_task(pair & 7, below * BPD + (pair >> 3))


def start_from(id_, core, unit_ref, sib_ref, dst, sem):
    here = rows_of(id_ & 7)
    mine = ((id_ >> 3) & 1) == core

    @pl.when(mine)
    def _():
        pltpu.make_async_copy(unit_ref.at[here, :], dst, sem).start()

    @pl.when(jnp.logical_not(mine))
    def _():
        pltpu.make_async_copy(sib_ref.at[here, :], dst, sem).start()


def listed(plan_ref, row, i, chip):
    twice, once = plan_ref[F_COUNT + row], plan_ref[D_COUNT + row]
    from_f = plan_ref[F_LIST + row * 16 + jnp.clip(i, 0, 15)]
    from_d = plan_ref[D_LIST + row * 16 + jnp.clip(i - twice, 0, 15)]
    found = jnp.where(i < twice, from_f, from_d)
    return jnp.where(i < twice + once, found, chip * ON_CHIP)


def first_pack_kernel(size, pos_ref, plan_ref, unit_ref, sib_ref, up_ref, down_ref, sems):
    y, core = pos_ref[0] >> 1, pos_ref[0] & 1
    slots = [(way, j, out) for way, out in ((0, up_ref), (1, down_ref)) for j in range(size)]
    for n, (way, j, out) in enumerate(slots):
        block = listed(plan_ref, 2 * y + way, 2 * j + core, y)
        start_from(block, core, unit_ref, sib_ref, out.at[j * BLOCK : (j + 1) * BLOCK, :], sems.at[n])
    for n, (way, j, out) in enumerate(slots):
        pltpu.make_async_copy(
            unit_ref.at[0:BLOCK, :], out.at[j * BLOCK : (j + 1) * BLOCK, :], sems.at[n]
        ).wait()


def second_pack_kernel(
    first, size, pos_ref, plan_ref, unit_ref, sib_ref, got_up, got_down, up_ref, down_ref, sems
):
    y, core = pos_ref[0] >> 1, pos_ref[0] & 1
    slots = [
        (way, j, out, got)
        for way, out, got in ((0, up_ref, got_up), (1, down_ref, got_down))
        for j in range(size)
    ]
    for n, (way, j, out, got) in enumerate(slots):
        dst = out.at[j * BLOCK : (j + 1) * BLOCK, :]
        position = 2 * j + core
        passing = plan_ref[F_COUNT + 2 * ((y + (3 if way == 0 else 1)) & 3) + way]
        passes = (position < passing) if j < first else (position < 0)
        if j < first:

            @pl.when(passes)
            def _():
                pltpu.make_async_copy(got.at[j * BLOCK : (j + 1) * BLOCK, :], dst, sems.at[n]).start()

        @pl.when(jnp.logical_not(passes))
        def _():
            block = listed(plan_ref, 2 * y + way, position - passing + 2 * first, y)
            start_from(block, core, unit_ref, sib_ref, dst, sems.at[n])

    for n, (way, j, out, got) in enumerate(slots):
        pltpu.make_async_copy(
            unit_ref.at[0:BLOCK, :], out.at[j * BLOCK : (j + 1) * BLOCK, :], sems.at[n]
        ).wait()


def own_kernel(pos_ref, tab_ref, surplus_ref, u_ref, sib_ref, acc_ref, kacc_ref, live_ref):
    core = pos_ref[0] & 1

    @functools.partial(loop, BPD * BPD)
    def _(i):
        live_ref[i] = 0.0

    def mark(a, b):
        live_ref[a * BPD + b] = 1.0
        live_ref[b * BPD + a] = 1.0

    @functools.partial(loop, tab_ref[0, 0])
    def _(t):
        pair = tab_ref[0, 1 + t]
        mark(pair >> 3, pair & 7)

    @functools.partial(loop, surplus_ref.shape[0])
    def _(t):
        @pl.when(surplus_ref[t, 2] == 1)
        def _():
            mark(surplus_ref[t, 0], surplus_ref[t, 1])

    step = 2

    @functools.partial(loop, BPD // step)
    def _(part):
        here = pl.ds(pl.multiple_of(part * step * BLOCK, step * BLOCK), step * BLOCK)
        kernel = kernel_values(u_ref[here, :], u_ref[...])
        rows = []
        for i in range(step):
            parts = [
                kernel[i * BLOCK : (i + 1) * BLOCK, j * BLOCK : (j + 1) * BLOCK]
                * live_ref[(part * step + i) * BPD + j]
                for j in range(BPD)
            ]
            kacc_ref[rows_of(part * step + i), :] = sum(parts)
            rows.append(jnp.concatenate(parts, axis=1).astype(jnp.bfloat16))
        acc_ref[here, :] = jnp.dot(
            jnp.concatenate(rows, axis=0), u_ref[...], preferred_element_type=jnp.float32
        )

    @functools.partial(loop, tab_ref[core, ENTRY])
    def _(t):
        pair = tab_ref[core, ENTRY + 1 + t]
        a, b = pair >> 3, pair & 7
        mine, other = jnp.where(core == 0, a, b), jnp.where(core == 0, b, a)
        add_terms(u_ref, sib_ref, acc_ref, kacc_ref, mine, other)


def run_tasks(stage, size, task_ref, u_ref, q_ref, acc_ref, kacc_ref):
    def per_block(own, carry):
        row = stage * BPD + own

        def step(t, inner):
            place = task_ref[TASK + row * 64 + t]
            add_terms(
                u_ref, q_ref, acc_ref, kacc_ref, own, (place >> 8) * size + (place & 255)
            )
            return inner

        lax.fori_loop(0, task_ref[TASKS + row], step, 0)
        return carry

    lax.fori_loop(0, BPD, per_block, 0)


def fetch(size, sources, q_ref, sems):
    copies = [
        pltpu.make_async_copy(
            source, q_ref.at[n * size * BLOCK : (n + 1) * size * BLOCK, :], sems.at[n]
        )
        for n, source in enumerate(sources)
    ]
    for copy in copies:
        copy.start()
    for copy in copies:
        copy.wait()


def near_kernel(size, task_ref, u_ref, acc_in, kacc_in, g0, g1, g2, g3, acc_ref, kacc_ref, q_ref, sems):
    acc_ref[...] = acc_in[...]
    kacc_ref[...] = kacc_in[...]
    fetch(size, (g0, g1, g2, g3), q_ref, sems)
    run_tasks(0, size, task_ref, u_ref, q_ref, acc_ref, kacc_ref)


def last_kernel(
    size, task_ref, u_ref, acc_in, kacc_in, g0, g1, g2, g3, out_ref, log_ref, acc_ref, kacc_ref, q_ref, sems
):
    own = pl.program_id(0)

    @pl.when(own == 0)
    def _():
        fetch(size, (g0, g1, g2, g3), q_ref, sems)

    acc_ref[...] = acc_in[...]
    kacc_ref[...] = kacc_in[...]
    row = BPD + own

    def step(t, carry):
        place = task_ref[TASK + row * 64 + t]
        add_terms(
            u_ref, q_ref, acc_ref, kacc_ref, 0, (place >> 8) * size + (place & 255)
        )
        return carry

    lax.fori_loop(0, task_ref[TASKS + row], step, 0)
    kernel = kacc_ref[...]
    density = jnp.sum(kernel, axis=1, keepdims=True)
    out_ref[...] = (u_ref[...].astype(jnp.float32) - acc_ref[...] / density).astype(jnp.bfloat16)
    log_ref[pl.ds(own, 1), :] = jnp.log(jnp.sum(kernel.T, axis=0, keepdims=True))


SMEM = pl.BlockSpec(memory_space=pltpu.SMEM)
VMEM = pl.BlockSpec(memory_space=pltpu.VMEM)
ANY = pl.BlockSpec(memory_space=pl.ANY)


def params():
    return pltpu.CompilerParams(vmem_limit_bytes=VMEM_BYTES)


def cost(pairs, width):
    return pl.CostEstimate(
        flops=pairs * 4 * BLOCK * BLOCK * width, bytes_accessed=8 * 2**20, transcendentals=pairs * BLOCK * BLOCK
    )


def exchange_and_score(first, second, pos, plan, tables, surplus, unit, sib):
    rows, width = unit.shape
    sends = lambda size: tuple(jax.ShapeDtypeStruct((size * BLOCK, width), jnp.bfloat16) for _ in range(2))
    sums = (
        jax.ShapeDtypeStruct((rows, width), jnp.float32),
        jax.ShapeDtypeStruct((rows, BLOCK), jnp.float32),
    )
    up, down = pl.pallas_call(
        functools.partial(first_pack_kernel, first),
        in_specs=[SMEM, SMEM, ANY, ANY],
        out_specs=(VMEM, VMEM),
        out_shape=sends(first),
        scratch_shapes=[pltpu.SemaphoreType.DMA((2 * first,))],
        compiler_params=params(),
        name="first_pack",
    )(pos, plan, unit, sib)
    got_up, got_down = along_chips(up, 1), along_chips(down, -1)

    places = pl.pallas_call(
        places_kernel,
        in_specs=[SMEM, SMEM, SMEM],
        out_specs=SMEM,
        out_shape=jax.ShapeDtypeStruct((PLACES,), jnp.int32),
        cost_estimate=cost(16, width),
        name="places",
    )(pos, tables, plan)
    acc, kacc = pl.pallas_call(
        own_kernel,
        in_specs=[SMEM, SMEM, SMEM, VMEM, VMEM],
        out_specs=(VMEM, VMEM),
        out_shape=sums,
        scratch_shapes=[pltpu.SMEM((BPD * BPD,), jnp.float32)],
        compiler_params=params(),
        cost_estimate=cost(64, width),
        name="own_pairs",
    )(pos, tables, surplus, unit, sib)

    got_up, got_down, acc, places = lax.optimization_barrier((got_up, got_down, acc, places))
    up, down = pl.pallas_call(
        functools.partial(second_pack_kernel, first, second),
        in_specs=[SMEM, SMEM] + [ANY] * 4,
        out_specs=(VMEM, VMEM),
        out_shape=sends(second),
        scratch_shapes=[pltpu.SemaphoreType.DMA((2 * second,))],
        compiler_params=params(),
        name="second_pack",
    )(pos, plan, unit, sib, got_up, got_down)
    far_up, far_down = along_chips(up, 1), along_chips(down, -1)
    sib_up, sib_down = to_sibling(got_up), to_sibling(got_down)

    acc, kacc = pl.pallas_call(
        functools.partial(near_kernel, first),
        in_specs=[SMEM, VMEM, VMEM, VMEM] + [ANY] * 4,
        out_specs=(VMEM, VMEM),
        out_shape=sums,
        scratch_shapes=[
            pltpu.VMEM((4 * first * BLOCK, width), jnp.bfloat16),
            pltpu.SemaphoreType.DMA((4,)),
        ],
        compiler_params=params(),
        cost_estimate=cost(12, width),
        name="near_pairs",
    )(places, unit, acc, kacc, got_up, sib_up, got_down, sib_down)

    far_up, far_down, acc = lax.optimization_barrier((far_up, far_down, acc))
    far_sib_up, far_sib_down = to_sibling(far_up), to_sibling(far_down)
    of_block = lambda w: pl.BlockSpec((BLOCK, w), lambda i: (i, 0))
    centered, log_density = pl.pallas_call(
        functools.partial(last_kernel, second),
        grid=(BPD,),
        in_specs=[SMEM, of_block(width), of_block(width), of_block(BLOCK)] + [ANY] * 4,
        out_specs=(of_block(width), pl.BlockSpec((BPD, BLOCK), lambda i: (0, 0))),
        out_shape=(
            jax.ShapeDtypeStruct((rows, width), jnp.bfloat16),
            jax.ShapeDtypeStruct((BPD, BLOCK), jnp.float32),
        ),
        scratch_shapes=[
            pltpu.VMEM((BLOCK, width), jnp.float32),
            pltpu.VMEM((BLOCK, BLOCK), jnp.float32),
            pltpu.VMEM((4 * second * BLOCK, width), jnp.bfloat16),
            pltpu.SemaphoreType.DMA((4,)),
        ],
        compiler_params=params(),
        cost_estimate=cost(8, width),
        name="far_pairs",
    )(places, unit, acc, kacc, far_up, far_sib_up, far_down, far_sib_down)
    return centered, log_density


def shards(embeddings, home_pairs, home_count, surplus_pairs):
    rows, width = embeddings.shape
    pairs, count = home_pairs[0, 0], home_count[0, 0]
    shifts = pairs.shape[0]
    pos = lax.axis_index("owner").astype(jnp.int32).reshape(1)

    step = 128
    unit = pl.pallas_call(
        normalize_kernel,
        grid=(rows // step,),
        in_specs=[pl.BlockSpec((step, width), lambda i: (i, 0))],
        out_specs=pl.BlockSpec((step, width), lambda i: (i, 0)),
        out_shape=jax.ShapeDtypeStruct(embeddings.shape, jnp.bfloat16),
        cost_estimate=pl.CostEstimate(flops=2**22, bytes_accessed=2**22, transcendentals=1024),
        name="normalize",
    )(embeddings)

    packed = jnp.concatenate([count[:, None], pairs[:, :MOST, 0] * 8 + pairs[:, :MOST, 1]], axis=1)
    tables = jnp.pad(packed.reshape(1, -1), ((0, 0), (0, 128 - shifts * ENTRY)))
    for bit in (1, 2, 4):
        route = [(o, o ^ bit) for o in range(OWNERS)]
        came = lax.ppermute(tables, "owner", route)
        if bit == 1:
            came, unit = lax.optimization_barrier((came, unit))
            sib = to_sibling(unit)
        tables = jnp.concatenate([tables, came], axis=0)

    plan, chosen = pl.pallas_call(
        plan_kernel,
        in_specs=[SMEM, SMEM],
        out_specs=(SMEM, SMEM),
        out_shape=(
            jax.ShapeDtypeStruct((PLAN,), jnp.int32),
            jax.ShapeDtypeStruct((1,), jnp.int32),
        ),
        name="plan",
    )(pos, tables)

    centered, log_density = lax.switch(
        chosen[0],
        [functools.partial(exchange_and_score, *size) for size in SIZES],
        pos, plan, tables, surplus_pairs[0, 0], unit, sib,
    )
    return centered, log_density.reshape(rows)


def solution(mesh):
    return jax.shard_map(
        shards,
        mesh=mesh,
        in_specs=(
            P(("group", "owner"), None),
            P("group", "owner", None, None, None),
            P("group", "owner", None),
            P("group", "owner", None, None),
        ),
        out_specs=(P(("group", "owner"), None), P(("group", "owner"))),
        check_vma=False,
    )
```

```python
import functools

import jax
import jax.numpy as jnp
from jax import lax
from jax.experimental import pallas as pl
from jax.experimental.pallas import tpu as pltpu
from jax.sharding import PartitionSpec as P

BLOCK = 128
BPD = 8
CHIPS = 4
OWNERS = 8
BLOCKS = OWNERS * BPD
ON_CHIP = 2 * BPD
sharpness = 4.0
epsilon = 1e-06
SIZES = ((3, 3), (4, 4), (8, 8))
MOST = 20
ENTRY = MOST + 1

STRIDE = 32
F_COUNT, D_COUNT, LOAD, FIRST, NEED, TOUCHED, FAR, F_LIST, D_LIST = 0, 8, 16, 24, 32, 96, 161, 256, 512
PLAN = 768
TASKS, TASK, PLACE = 0, 16, 1040
PLACES = 1152


def loop(count, body):
    def step(i, carry):
        body(i)
        return carry

    lax.fori_loop(0, count, step, 0)


def along_chips(x, hops):
    route = [(o, ((o // 2 + hops) % CHIPS) * 2 + o % 2) for o in range(OWNERS)]
    return lax.ppermute(x, "owner", route)


def to_sibling(x):
    return lax.ppermute(x, "owner", [(o, o ^ 1) for o in range(OWNERS)])


def normalize_kernel(x_ref, u_ref):
    wide = x_ref[...].astype(jnp.float32)
    mean = jnp.mean(wide * wide, axis=-1, keepdims=True)
    u_ref[...] = (wide * lax.rsqrt(mean + epsilon)).astype(jnp.bfloat16)


def rows_of(block):
    return pl.ds(pl.multiple_of(block * BLOCK, BLOCK), BLOCK)


def kernel_values(p, q):
    dots = lax.dot_general(p, q, (((1,), (1,)), ((), ())), preferred_element_type=jnp.float32)
    return jnp.exp(sharpness * (dots * (1.0 / q.shape[1]) - 1.0))


def add_terms(u_ref, q_ref, acc_ref, kacc_ref, mine, other):
    q = q_ref[rows_of(other), :]
    kernel = kernel_values(u_ref[rows_of(mine), :], q)
    kacc_ref[rows_of(mine), :] += kernel
    acc_ref[rows_of(mine), :] += jnp.dot(
        kernel.astype(jnp.bfloat16), q, preferred_element_type=jnp.float32
    )


def plan_kernel(pos_ref, tab_ref, plan_ref, class_ref):
    me = pos_ref[0]
    for i in range(8):
        plan_ref[LOAD + i] = 0
        plan_ref[F_COUNT + i] = 0
        plan_ref[D_COUNT + i] = 0
    for i in range(BLOCKS):
        plan_ref[NEED + i] = 0

    def of_owner(o, touched):
        row = o ^ me
        for s in range(1, 5):
            q = (o + s) & 7
            to_q, to_o = lax.shift_left(1, q >> 1), lax.shift_left(1, o >> 1)

            def of_pair(t, touched):
                pair = tab_ref[row, s * ENTRY + 1 + t]
                for block, chip in ((o * BPD + (pair >> 3), to_q), (q * BPD + (pair & 7), to_o)):
                    before = plan_ref[NEED + block]
                    plan_ref[NEED + block] = before | chip
                    plan_ref[TOUCHED + touched] = block
                    touched = touched + (before == 0).astype(jnp.int32)
                return touched

            touched = lax.fori_loop(0, tab_ref[row, s * ENTRY], of_pair, touched)
        return touched

    touched = lax.fori_loop(0, OWNERS, of_owner, 0)

    def needs(block):
        mask, chip = plan_ref[NEED + block], block >> 4
        bit = lambda hop: lax.shift_right_logical(mask, (chip + hop) & 3) & 1
        return chip, bit(1), bit(3), bit(2)

    def append(count, table, at, block, wanted):
        held = plan_ref[count + at]
        plan_ref[table + at * STRIDE + held] = block
        plan_ref[count + at] = held + wanted

    def one_hop(i, fars):
        block = plan_ref[TOUCHED + i]
        chip, up, down, far = needs(block)
        at = 2 * chip
        plan_ref[LOAD + at] = plan_ref[LOAD + at] + up
        plan_ref[LOAD + at + 1] = plan_ref[LOAD + at + 1] + down
        append(D_COUNT, D_LIST, at, block, up & (1 - far))
        append(D_COUNT, D_LIST, at + 1, block, down & (1 - far))
        plan_ref[FAR + fars] = block
        return fars + far

    fars = lax.fori_loop(0, touched, one_hop, 0)

    @functools.partial(loop, fars)
    def _(i):
        block = plan_ref[FAR + i]
        chip, up, down, _ = needs(block)
        costs, loads = [], []
        for way, near, hop in ((0, up, 1), (1, down, 3)):
            at, after = 2 * chip + way, 2 * ((chip + hop) & 3) + way
            here, there = plan_ref[LOAD + at] + 1 - near, plan_ref[LOAD + after] + 1
            most = jnp.maximum(jnp.maximum(here, there), 2 * plan_ref[F_COUNT + at] + 2)
            costs.append(most * 64 + here + there + 32 * (1 - near))
            loads.append((at, after, here, there))
        goes_down = costs[0] > costs[1]
        at, after, here, there = (jnp.where(goes_down, b, a) for a, b in zip(*loads))
        plan_ref[LOAD + at] = here
        plan_ref[LOAD + after] = there
        append(F_COUNT, F_LIST, at, block, 1)
        append(D_COUNT, D_LIST, at ^ 1, block, jnp.where(goes_down, up, down))

    twice = [plan_ref[F_COUNT + i] for i in range(8)]
    once = [plan_ref[D_COUNT + i] for i in range(8)]
    longest = functools.reduce(jnp.maximum, twice)
    second_needs = {}
    for size in sorted({size for size, _ in SIZES}):
        needs = []
        for i in range(8):
            before = (i + (6 if i % 2 == 0 else 2)) % 8
            needs.append(twice[before] + jnp.maximum(twice[i] + once[i] - 2 * size, 0))
        second_needs[size] = functools.reduce(jnp.maximum, needs)
    chosen, first_size = len(SIZES) - 1, 2 * SIZES[-1][0]
    for k in range(len(SIZES) - 2, -1, -1):
        first, second = SIZES[k]
        fits = (longest <= 2 * first) & (second_needs[first] <= 2 * second)
        chosen = jnp.where(fits, k, chosen)
        first_size = jnp.where(fits, 2 * first, first_size)
    class_ref[0] = chosen
    plan_ref[FIRST] = first_size


def places_kernel(pos_ref, tab_ref, plan_ref, out_ref):
    me = pos_ref[0]
    y, core = me >> 1, me & 1
    first_size = plan_ref[FIRST]
    for i in range(16):
        out_ref[TASKS + i] = 0

    def put(block, stage, way, position):
        other = (position & 1) ^ core
        out_ref[PLACE + block] = stage * 65536 + (way * 2 + other) * 256 + (position >> 1)

    for way in (0, 1):
        near = 2 * ((y + (3 if way == 0 else 1)) & 3) + way
        far = 2 * ((y + 2) & 3) + way
        twice, passing = plan_ref[F_COUNT + near], plan_ref[F_COUNT + far]

        @functools.partial(loop, twice)
        def _(i):
            put(plan_ref[F_LIST + near * STRIDE + i], 0, way, i)

        @functools.partial(loop, plan_ref[D_COUNT + near])
        def _(i):
            late = (twice + i >= first_size).astype(jnp.int32)
            put(plan_ref[D_LIST + near * STRIDE + i], late, way, twice + i + late * (passing - first_size))

        @functools.partial(loop, passing)
        def _(i):
            put(plan_ref[F_LIST + far * STRIDE + i], 1, way, i)

    def add_task(own, block):
        place = out_ref[PLACE + block]
        row = (place >> 16) * BPD + own
        count = out_ref[TASKS + row]
        out_ref[TASK + row * 64 + count] = place & 65535
        out_ref[TASKS + row] = count + 1

    for s in range(1, 5):
        above, below = (me + s) & 7, (me - s) & 7

        @pl.when((above >> 1) != y)
        def _():
            @functools.partial(loop, tab_ref[0, s * ENTRY])
            def _(t):
                pair = tab_ref[0, s * ENTRY + 1 + t]
                add_task(pair >> 3, above * BPD + (pair & 7))

        @pl.when((below >> 1) != y)
        def _():
            row = below ^ me

            @functools.partial(loop, tab_ref[row, s * ENTRY])
            def _(t):
                pair = tab_ref[row, s * ENTRY + 1 + t]
                add_task(pair & 7, below * BPD + (pair >> 3))


def start_from(id_, core, unit_ref, sib_ref, dst, sem):
    here = rows_of(id_ & 7)
    mine = ((id_ >> 3) & 1) == core

    @pl.when(mine)
    def _():
        pltpu.make_async_copy(unit_ref.at[here, :], dst, sem).start()

    @pl.when(jnp.logical_not(mine))
    def _():
        pltpu.make_async_copy(sib_ref.at[here, :], dst, sem).start()


def listed(plan_ref, row, i, chip):
    twice, once = plan_ref[F_COUNT + row], plan_ref[D_COUNT + row]
    from_f = plan_ref[F_LIST + row * STRIDE + jnp.clip(i, 0, 15)]
    from_d = plan_ref[D_LIST + row * STRIDE + jnp.clip(i - twice, 0, 15)]
    found = jnp.where(i < twice, from_f, from_d)
    return jnp.where(i < twice + once, found, chip * ON_CHIP)


def first_pack_kernel(size, pos_ref, plan_ref, unit_ref, sib_ref, up_ref, down_ref, sems):
    y, core = pos_ref[0] >> 1, pos_ref[0] & 1
    slots = [(way, j, out) for way, out in ((0, up_ref), (1, down_ref)) for j in range(size)]
    for n, (way, j, out) in enumerate(slots):
        block = listed(plan_ref, 2 * y + way, 2 * j + core, y)
        start_from(block, core, unit_ref, sib_ref, out.at[j * BLOCK : (j + 1) * BLOCK, :], sems.at[n])
    for n, (way, j, out) in enumerate(slots):
        pltpu.make_async_copy(
            unit_ref.at[0:BLOCK, :], out.at[j * BLOCK : (j + 1) * BLOCK, :], sems.at[n]
        ).wait()


def second_pack_kernel(
    first, size, pos_ref, plan_ref, unit_ref, sib_ref, got_up, got_down, up_ref, down_ref, sems
):
    y, core = pos_ref[0] >> 1, pos_ref[0] & 1
    slots = [
        (way, j, out, got)
        for way, out, got in ((0, up_ref, got_up), (1, down_ref, got_down))
        for j in range(size)
    ]
    for n, (way, j, out, got) in enumerate(slots):
        dst = out.at[j * BLOCK : (j + 1) * BLOCK, :]
        position = 2 * j + core
        passing = plan_ref[F_COUNT + 2 * ((y + (3 if way == 0 else 1)) & 3) + way]
        passes = (position < passing) if j < first else (position < 0)
        if j < first:

            @pl.when(passes)
            def _():
                pltpu.make_async_copy(got.at[j * BLOCK : (j + 1) * BLOCK, :], dst, sems.at[n]).start()

        @pl.when(jnp.logical_not(passes))
        def _():
            block = listed(plan_ref, 2 * y + way, position - passing + 2 * first, y)
            start_from(block, core, unit_ref, sib_ref, dst, sems.at[n])

    for n, (way, j, out, got) in enumerate(slots):
        pltpu.make_async_copy(
            unit_ref.at[0:BLOCK, :], out.at[j * BLOCK : (j + 1) * BLOCK, :], sems.at[n]
        ).wait()


def own_kernel(pos_ref, tab_ref, surplus_ref, u_ref, sib_ref, acc_ref, kacc_ref, live_ref):
    core = pos_ref[0] & 1

    @functools.partial(loop, BPD * BPD)
    def _(i):
        live_ref[i] = 0.0

    def mark(a, b):
        live_ref[a * BPD + b] = 1.0
        live_ref[b * BPD + a] = 1.0

    @functools.partial(loop, tab_ref[0, 0])
    def _(t):
        pair = tab_ref[0, 1 + t]
        mark(pair >> 3, pair & 7)

    @functools.partial(loop, surplus_ref.shape[0])
    def _(t):
        @pl.when(surplus_ref[t, 2] == 1)
        def _():
            mark(surplus_ref[t, 0], surplus_ref[t, 1])

    step = 2

    @functools.partial(loop, BPD // step)
    def _(part):
        here = pl.ds(pl.multiple_of(part * step * BLOCK, step * BLOCK), step * BLOCK)
        kernel = kernel_values(u_ref[here, :], u_ref[...])
        rows = []
        for i in range(step):
            parts = [
                kernel[i * BLOCK : (i + 1) * BLOCK, j * BLOCK : (j + 1) * BLOCK]
                * live_ref[(part * step + i) * BPD + j]
                for j in range(BPD)
            ]
            kacc_ref[rows_of(part * step + i), :] = sum(parts)
            rows.append(jnp.concatenate(parts, axis=1).astype(jnp.bfloat16))
        acc_ref[here, :] = jnp.dot(
            jnp.concatenate(rows, axis=0), u_ref[...], preferred_element_type=jnp.float32
        )

    @functools.partial(loop, tab_ref[core, ENTRY])
    def _(t):
        pair = tab_ref[core, ENTRY + 1 + t]
        a, b = pair >> 3, pair & 7
        mine, other = jnp.where(core == 0, a, b), jnp.where(core == 0, b, a)
        add_terms(u_ref, sib_ref, acc_ref, kacc_ref, mine, other)


def run_tasks(stage, size, task_ref, u_ref, q_ref, acc_ref, kacc_ref):
    def per_block(own, carry):
        row = stage * BPD + own

        def step(t, inner):
            place = task_ref[TASK + row * 64 + t]
            add_terms(
                u_ref, q_ref, acc_ref, kacc_ref, own, (place >> 8) * size + (place & 255)
            )
            return inner

        lax.fori_loop(0, task_ref[TASKS + row], step, 0)
        return carry

    lax.fori_loop(0, BPD, per_block, 0)


def fetch(size, sources, q_ref, sems):
    copies = [
        pltpu.make_async_copy(
            source, q_ref.at[n * size * BLOCK : (n + 1) * size * BLOCK, :], sems.at[n]
        )
        for n, source in enumerate(sources)
    ]
    for copy in copies:
        copy.start()
    for copy in copies:
        copy.wait()


def near_kernel(size, task_ref, u_ref, acc_in, kacc_in, g0, g1, g2, g3, acc_ref, kacc_ref, q_ref, sems):
    acc_ref[...] = acc_in[...]
    kacc_ref[...] = kacc_in[...]
    fetch(size, (g0, g1, g2, g3), q_ref, sems)
    run_tasks(0, size, task_ref, u_ref, q_ref, acc_ref, kacc_ref)


def last_kernel(
    size, task_ref, u_ref, acc_in, kacc_in, g0, g1, g2, g3, out_ref, log_ref, acc_ref, kacc_ref, done_ref, q_ref, sems, out_sems
):
    fetch(size, (g0, g1, g2, g3), q_ref, sems)
    rows = lax.broadcasted_iota(jnp.int32, (BLOCK, BLOCK), 0)
    diagonal = rows == lax.broadcasted_iota(jnp.int32, (BLOCK, BLOCK), 1)

    def out_copy(own):
        return pltpu.make_async_copy(
            done_ref.at[rows_of(own), :], out_ref.at[rows_of(own), :], out_sems.at[own]
        )

    @functools.partial(loop, BPD)
    def _(own):
        row = BPD + own
        acc_ref[...] = acc_in[rows_of(own), :]
        kacc_ref[...] = kacc_in[rows_of(own), :]

        @functools.partial(loop, task_ref[TASKS + row])
        def _(t):
            place = task_ref[TASK + row * 64 + t]
            other = (place >> 8) * size + (place & 255)
            q = q_ref[rows_of(other), :]
            kernel = kernel_values(u_ref[rows_of(own), :], q)
            kacc_ref[...] += kernel
            acc_ref[...] += jnp.dot(kernel.astype(jnp.bfloat16), q, preferred_element_type=jnp.float32)

        density = jnp.sum(kacc_ref[...], axis=1, keepdims=True)
        done_ref[rows_of(own), :] = (
            u_ref[rows_of(own), :].astype(jnp.float32) - acc_ref[...] * (1.0 / density)
        ).astype(jnp.bfloat16)
        out_copy(own).start()
        across = jnp.sum(jnp.where(diagonal, density, 0.0), axis=0, keepdims=True)
        log_ref[pl.ds(own, 1), :] = jnp.log(across)

    for own in range(BPD):
        out_copy(own).wait()


SMEM = pl.BlockSpec(memory_space=pltpu.SMEM)
VMEM = pl.BlockSpec(memory_space=pltpu.VMEM)
ANY = pl.BlockSpec(memory_space=pl.ANY)


def params(mib):
    return pltpu.CompilerParams(vmem_limit_bytes=mib * 2**20)


def cost(pairs, width):
    return pl.CostEstimate(
        flops=pairs * 4 * BLOCK * BLOCK * width, bytes_accessed=8 * 2**20, transcendentals=pairs * BLOCK * BLOCK
    )


def exchange_and_score(first, second, pos, plan, tables, surplus, unit, sib):
    rows, width = unit.shape
    sends = lambda size: tuple(jax.ShapeDtypeStruct((size * BLOCK, width), jnp.bfloat16) for _ in range(2))
    sums = (
        jax.ShapeDtypeStruct((rows, width), jnp.float32),
        jax.ShapeDtypeStruct((rows, BLOCK), jnp.float32),
    )
    up, down = pl.pallas_call(
        functools.partial(first_pack_kernel, first),
        in_specs=[SMEM, SMEM, ANY, ANY],
        out_specs=(VMEM, VMEM),
        out_shape=sends(first),
        scratch_shapes=[pltpu.SemaphoreType.DMA((2 * first,))],
        compiler_params=params(8 + first),
        name="first_pack",
    )(pos, plan, unit, sib)
    got_up, got_down = along_chips(up, 1), along_chips(down, -1)

    places = pl.pallas_call(
        places_kernel,
        in_specs=[SMEM, SMEM, SMEM],
        out_specs=SMEM,
        out_shape=jax.ShapeDtypeStruct((PLACES,), jnp.int32),
        cost_estimate=cost(16, width),
        name="places",
    )(pos, tables, plan)
    acc, kacc = pl.pallas_call(
        own_kernel,
        in_specs=[SMEM, SMEM, SMEM, VMEM, VMEM],
        out_specs=(VMEM, VMEM),
        out_shape=sums,
        scratch_shapes=[pltpu.SMEM((BPD * BPD,), jnp.float32)],
        compiler_params=params(20),
        cost_estimate=cost(64, width),
        name="own_pairs",
    )(pos, tables, surplus, unit, sib)

    got_up, got_down, acc, places = lax.optimization_barrier((got_up, got_down, acc, places))
    up, down = pl.pallas_call(
        functools.partial(second_pack_kernel, first, second),
        in_specs=[SMEM, SMEM] + [ANY] * 4,
        out_specs=(VMEM, VMEM),
        out_shape=sends(second),
        scratch_shapes=[pltpu.SemaphoreType.DMA((2 * second,))],
        compiler_params=params(8 + second),
        name="second_pack",
    )(pos, plan, unit, sib, got_up, got_down)
    far_up, far_down = along_chips(up, 1), along_chips(down, -1)
    got_up, got_down, _, _ = lax.optimization_barrier((got_up, got_down, up, down))
    sib_up, sib_down = to_sibling(got_up), to_sibling(got_down)

    acc, kacc = pl.pallas_call(
        functools.partial(near_kernel, first),
        in_specs=[SMEM, VMEM, VMEM, VMEM] + [ANY] * 4,
        out_specs=(VMEM, VMEM),
        out_shape=sums,
        scratch_shapes=[
            pltpu.VMEM((4 * first * BLOCK, width), jnp.bfloat16),
            pltpu.SemaphoreType.DMA((4,)),
        ],
        compiler_params=params(16 + first),
        cost_estimate=cost(12, width),
        name="near_pairs",
    )(places, unit, acc, kacc, got_up, sib_up, got_down, sib_down)

    far_up, far_down, acc = lax.optimization_barrier((far_up, far_down, acc))
    far_sib_up, far_sib_down = to_sibling(far_up), to_sibling(far_down)
    centered, log_density = pl.pallas_call(
        functools.partial(last_kernel, second),
        in_specs=[SMEM, VMEM, VMEM, VMEM] + [ANY] * 4,
        out_specs=(ANY, VMEM),
        out_shape=(
            jax.ShapeDtypeStruct((rows, width), jnp.bfloat16),
            jax.ShapeDtypeStruct((BPD, BLOCK), jnp.float32),
        ),
        scratch_shapes=[
            pltpu.VMEM((BLOCK, width), jnp.float32),
            pltpu.VMEM((BLOCK, BLOCK), jnp.float32),
            pltpu.VMEM((rows, width), jnp.bfloat16),
            pltpu.VMEM((4 * second * BLOCK, width), jnp.bfloat16),
            pltpu.SemaphoreType.DMA((4,)),
            pltpu.SemaphoreType.DMA((BPD,)),
        ],
        compiler_params=params(16 + second),
        cost_estimate=cost(8, width),
        name="far_pairs",
    )(places, unit, acc, kacc, far_up, far_sib_up, far_down, far_sib_down)
    return centered, log_density


def shards(embeddings, home_pairs, home_count, surplus_pairs):
    rows, width = embeddings.shape
    pairs, count = home_pairs[0, 0], home_count[0, 0]
    shifts = pairs.shape[0]
    pos = lax.axis_index("owner").astype(jnp.int32).reshape(1)

    step = 128
    unit = pl.pallas_call(
        normalize_kernel,
        grid=(rows // step,),
        in_specs=[pl.BlockSpec((step, width), lambda i: (i, 0))],
        out_specs=pl.BlockSpec((step, width), lambda i: (i, 0)),
        out_shape=jax.ShapeDtypeStruct(embeddings.shape, jnp.bfloat16),
        cost_estimate=pl.CostEstimate(flops=2**22, bytes_accessed=2**22, transcendentals=1024),
        name="normalize",
    )(embeddings)

    packed = jnp.concatenate([count[:, None], pairs[:, :MOST, 0] * 8 + pairs[:, :MOST, 1]], axis=1)
    tables = jnp.pad(packed.reshape(1, -1), ((0, 0), (0, 128 - shifts * ENTRY)))
    for bit in (1, 2, 4):
        route = [(o, o ^ bit) for o in range(OWNERS)]
        came = lax.ppermute(tables, "owner", route)
        if bit == 1:
            came, unit = lax.optimization_barrier((came, unit))
            sib = to_sibling(unit)
        tables = jnp.concatenate([tables, came], axis=0)

    plan, chosen = pl.pallas_call(
        plan_kernel,
        in_specs=[SMEM, SMEM],
        out_specs=(SMEM, SMEM),
        out_shape=(
            jax.ShapeDtypeStruct((PLAN,), jnp.int32),
            jax.ShapeDtypeStruct((1,), jnp.int32),
        ),
        name="plan",
    )(pos, tables)

    centered, log_density = lax.switch(
        chosen[0],
        [functools.partial(exchange_and_score, *size) for size in SIZES],
        pos, plan, tables, surplus_pairs[0, 0], unit, sib,
    )
    return centered, log_density.reshape(rows)


def solution(mesh):
    return jax.shard_map(
        shards,
        mesh=mesh,
        in_specs=(
            P(("group", "owner"), None),
            P("group", "owner", None, None, None),
            P("group", "owner", None),
            P("group", "owner", None, None),
        ),
        out_specs=(P(("group", "owner"), None), P(("group", "owner"))),
        check_vma=False,
    )
```

```python
import functools

import jax
import jax.numpy as jnp
from jax import lax
from jax.experimental import pallas as pl
from jax.experimental.pallas import tpu as pltpu
from jax.sharding import PartitionSpec as P

BLOCK = 128
BPD = 8
CHIPS = 4
OWNERS = 8
BLOCKS = OWNERS * BPD
ON_CHIP = 2 * BPD
sharpness = 4.0
epsilon = 1e-06
SIZES = ((3, 3), (4, 4), (8, 8))
COUNTS = 5

STRIDE = 32
F_COUNT, D_COUNT, LOAD, FIRST, NEED, TOUCHED, FAR, F_LIST, D_LIST = 0, 8, 16, 24, 32, 96, 161, 256, 512
PLAN = 768
TASKS, TASK, PLACE = 0, 32, 1056
ROW = 32
PLACES = 1152


def loop(count, body):
    def step(i, carry):
        body(i)
        return carry

    lax.fori_loop(0, count, step, 0)


def along_chips(x, hops):
    route = [(o, ((o // 2 + hops) % CHIPS) * 2 + o % 2) for o in range(OWNERS)]
    return lax.ppermute(x, "owner", route)


def to_sibling(x):
    return lax.ppermute(x, "owner", [(o, o ^ 1) for o in range(OWNERS)])


def normalize_kernel(x_ref, u_ref):
    wide = x_ref[...].astype(jnp.float32)
    mean = jnp.mean(wide * wide, axis=-1, keepdims=True)
    u_ref[...] = (wide * lax.rsqrt(mean + epsilon)).astype(jnp.bfloat16)


def rows_of(block):
    return pl.ds(pl.multiple_of(block * BLOCK, BLOCK), BLOCK)


def kernel_values(p, q):
    dots = lax.dot_general(p, q, (((1,), (1,)), ((), ())), preferred_element_type=jnp.float32)
    return jnp.exp(sharpness * (dots * (1.0 / q.shape[1]) - 1.0))


def add_terms(u_ref, q_ref, acc_ref, kacc_ref, mine, other):
    q = q_ref[rows_of(other), :]
    kernel = kernel_values(u_ref[rows_of(mine), :], q)
    kacc_ref[rows_of(mine), :] += kernel
    acc_ref[rows_of(mine), :] += jnp.dot(
        kernel.astype(jnp.bfloat16), q, preferred_element_type=jnp.float32
    )


def plan_kernel(pos_ref, t0, t1, t2, t3, plan_ref, tab_ref, class_ref, sems):
    copies = [
        pltpu.make_async_copy(t, tab_ref.at[i * 16 : (i + 1) * 16, :], sems.at[i])
        for i, t in enumerate((t0, t1, t2, t3))
    ]
    for copy in copies:
        copy.start()
    me = pos_ref[0]
    for i in range(8):
        plan_ref[LOAD + i] = 0
        plan_ref[F_COUNT + i] = 0
        plan_ref[D_COUNT + i] = 0
    for i in range(BLOCKS):
        plan_ref[NEED + i] = 0
    for copy in copies:
        copy.wait()

    def of_owner(o, touched):
        row = (o ^ me) * 8
        for s in range(1, 5):
            q = (o + s) & 7
            to_q, to_o = lax.shift_left(1, q >> 1), lax.shift_left(1, o >> 1)

            def of_pair(t, touched):
                pair = tab_ref[row + s, t]
                for block, chip in ((o * BPD + (pair >> 3), to_q), (q * BPD + (pair & 7), to_o)):
                    before = plan_ref[NEED + block]
                    plan_ref[NEED + block] = before | chip
                    plan_ref[TOUCHED + touched] = block
                    touched = touched + (before == 0).astype(jnp.int32)
                return touched

            touched = lax.fori_loop(0, tab_ref[row + COUNTS, s], of_pair, touched)
        return touched

    touched = lax.fori_loop(0, OWNERS, of_owner, 0)

    def needs(block):
        mask, chip = plan_ref[NEED + block], block >> 4
        bit = lambda hop: lax.shift_right_logical(mask, (chip + hop) & 3) & 1
        return chip, bit(1), bit(3), bit(2)

    def append(count, table, at, block, wanted):
        held = plan_ref[count + at]
        plan_ref[table + at * STRIDE + held] = block
        plan_ref[count + at] = held + wanted

    def one_hop(i, fars):
        block = plan_ref[TOUCHED + i]
        chip, up, down, far = needs(block)
        at = 2 * chip
        plan_ref[LOAD + at] = plan_ref[LOAD + at] + up
        plan_ref[LOAD + at + 1] = plan_ref[LOAD + at + 1] + down
        append(D_COUNT, D_LIST, at, block, up & (1 - far))
        append(D_COUNT, D_LIST, at + 1, block, down & (1 - far))
        plan_ref[FAR + fars] = block
        return fars + far

    fars = lax.fori_loop(0, touched, one_hop, 0)

    @functools.partial(loop, fars)
    def _(i):
        block = plan_ref[FAR + i]
        chip, up, down, _ = needs(block)
        costs, loads = [], []
        for way, near, hop in ((0, up, 1), (1, down, 3)):
            at, after = 2 * chip + way, 2 * ((chip + hop) & 3) + way
            here, there = plan_ref[LOAD + at] + 1 - near, plan_ref[LOAD + after] + 1
            most = jnp.maximum(jnp.maximum(here, there), 2 * plan_ref[F_COUNT + at] + 2)
            costs.append(most * 64 + here + there + 32 * (1 - near))
            loads.append((at, after, here, there))
        goes_down = costs[0] > costs[1]
        at, after, here, there = (jnp.where(goes_down, b, a) for a, b in zip(*loads))
        plan_ref[LOAD + at] = here
        plan_ref[LOAD + after] = there
        append(F_COUNT, F_LIST, at, block, 1)
        append(D_COUNT, D_LIST, at ^ 1, block, jnp.where(goes_down, up, down))

    twice = [plan_ref[F_COUNT + i] for i in range(8)]
    once = [plan_ref[D_COUNT + i] for i in range(8)]
    longest = functools.reduce(jnp.maximum, twice)
    second_needs = {}
    for size in sorted({size for size, _ in SIZES}):
        needs = []
        for i in range(8):
            before = (i + (6 if i % 2 == 0 else 2)) % 8
            needs.append(twice[before] + jnp.maximum(twice[i] + once[i] - 2 * size, 0))
        second_needs[size] = functools.reduce(jnp.maximum, needs)
    chosen, first_size = len(SIZES) - 1, 2 * SIZES[-1][0]
    for k in range(len(SIZES) - 2, -1, -1):
        first, second = SIZES[k]
        fits = (longest <= 2 * first) & (second_needs[first] <= 2 * second)
        chosen = jnp.where(fits, k, chosen)
        first_size = jnp.where(fits, 2 * first, first_size)
    class_ref[0] = chosen
    plan_ref[FIRST] = first_size


def places_kernel(pos_ref, tab_ref, plan_ref, out_ref):
    me = pos_ref[0]
    y, core = me >> 1, me & 1
    first_size = plan_ref[FIRST]
    for i in range(32):
        out_ref[TASKS + i] = 0

    def put(block, stage, way, position):
        other = (position & 1) ^ core
        out_ref[PLACE + block] = (2 * stage + other) * 65536 + way * 256 + (position >> 1)

    for way in (0, 1):
        near = 2 * ((y + (3 if way == 0 else 1)) & 3) + way
        far = 2 * ((y + 2) & 3) + way
        twice, passing = plan_ref[F_COUNT + near], plan_ref[F_COUNT + far]

        @functools.partial(loop, twice)
        def _(i):
            put(plan_ref[F_LIST + near * STRIDE + i], 0, way, i)

        @functools.partial(loop, plan_ref[D_COUNT + near])
        def _(i):
            late = (twice + i >= first_size).astype(jnp.int32)
            put(plan_ref[D_LIST + near * STRIDE + i], late, way, twice + i + late * (passing - first_size))

        @functools.partial(loop, passing)
        def _(i):
            put(plan_ref[F_LIST + far * STRIDE + i], 1, way, i)

    def add_task(own, block):
        place = out_ref[PLACE + block]
        row = (place >> 16) * BPD + own
        count = out_ref[TASKS + row]
        out_ref[TASK + row * ROW + count] = place & 65535
        out_ref[TASKS + row] = count + 1

    for s in range(1, 5):
        above, below = (me + s) & 7, (me - s) & 7

        @pl.when((above >> 1) != y)
        def _():
            @functools.partial(loop, tab_ref[COUNTS, s])
            def _(t):
                pair = tab_ref[s, t]
                add_task(pair >> 3, above * BPD + (pair & 7))

        @pl.when((below >> 1) != y)
        def _():
            row = (below ^ me) * 8

            @functools.partial(loop, tab_ref[row + COUNTS, s])
            def _(t):
                pair = tab_ref[row + s, t]
                add_task(pair & 7, below * BPD + (pair >> 3))


def start_from(id_, core, unit_ref, sib_ref, dst, sem):
    here = rows_of(id_ & 7)
    mine = ((id_ >> 3) & 1) == core

    @pl.when(mine)
    def _():
        pltpu.make_async_copy(unit_ref.at[here, :], dst, sem).start()

    @pl.when(jnp.logical_not(mine))
    def _():
        pltpu.make_async_copy(sib_ref.at[here, :], dst, sem).start()


def listed(plan_ref, row, i, chip):
    twice, once = plan_ref[F_COUNT + row], plan_ref[D_COUNT + row]
    from_f = plan_ref[F_LIST + row * STRIDE + jnp.clip(i, 0, 15)]
    from_d = plan_ref[D_LIST + row * STRIDE + jnp.clip(i - twice, 0, 15)]
    found = jnp.where(i < twice, from_f, from_d)
    return jnp.where(i < twice + once, found, chip * ON_CHIP)


def first_pack_kernel(size, pos_ref, plan_ref, unit_ref, sib_ref, up_ref, down_ref, sems):
    y, core = pos_ref[0] >> 1, pos_ref[0] & 1
    slots = [(way, j, out) for way, out in ((0, up_ref), (1, down_ref)) for j in range(size)]
    for n, (way, j, out) in enumerate(slots):
        block = listed(plan_ref, 2 * y + way, 2 * j + core, y)
        start_from(block, core, unit_ref, sib_ref, out.at[j * BLOCK : (j + 1) * BLOCK, :], sems.at[n])
    for n, (way, j, out) in enumerate(slots):
        pltpu.make_async_copy(
            unit_ref.at[0:BLOCK, :], out.at[j * BLOCK : (j + 1) * BLOCK, :], sems.at[n]
        ).wait()


def second_pack_kernel(
    first, size, pos_ref, plan_ref, unit_ref, sib_ref, got_up, got_down, up_ref, down_ref, sems
):
    y, core = pos_ref[0] >> 1, pos_ref[0] & 1
    slots = [
        (way, j, out, got)
        for way, out, got in ((0, up_ref, got_up), (1, down_ref, got_down))
        for j in range(size)
    ]
    for n, (way, j, out, got) in enumerate(slots):
        dst = out.at[j * BLOCK : (j + 1) * BLOCK, :]
        position = 2 * j + core
        passing = plan_ref[F_COUNT + 2 * ((y + (3 if way == 0 else 1)) & 3) + way]
        passes = (position < passing) if j < first else (position < 0)
        if j < first:

            @pl.when(passes)
            def _():
                pltpu.make_async_copy(got.at[j * BLOCK : (j + 1) * BLOCK, :], dst, sems.at[n]).start()

        @pl.when(jnp.logical_not(passes))
        def _():
            block = listed(plan_ref, 2 * y + way, position - passing + 2 * first, y)
            start_from(block, core, unit_ref, sib_ref, dst, sems.at[n])

    for n, (way, j, out, got) in enumerate(slots):
        pltpu.make_async_copy(
            unit_ref.at[0:BLOCK, :], out.at[j * BLOCK : (j + 1) * BLOCK, :], sems.at[n]
        ).wait()


def own_kernel(pos_ref, tab_ref, surplus_ref, u_ref, sib_ref, acc_ref, kacc_ref, live_ref):
    core = pos_ref[0] & 1

    @functools.partial(loop, BPD * BPD)
    def _(i):
        live_ref[i] = 0.0

    def mark(a, b):
        live_ref[a * BPD + b] = 1.0
        live_ref[b * BPD + a] = 1.0

    @functools.partial(loop, tab_ref[COUNTS, 0])
    def _(t):
        pair = tab_ref[0, t]
        mark(pair >> 3, pair & 7)

    @functools.partial(loop, surplus_ref.shape[0])
    def _(t):
        @pl.when(surplus_ref[t, 2] == 1)
        def _():
            mark(surplus_ref[t, 0], surplus_ref[t, 1])

    step = 2

    @functools.partial(loop, BPD // step)
    def _(part):
        here = pl.ds(pl.multiple_of(part * step * BLOCK, step * BLOCK), step * BLOCK)
        kernel = kernel_values(u_ref[here, :], u_ref[...])
        rows = []
        for i in range(step):
            parts = [
                kernel[i * BLOCK : (i + 1) * BLOCK, j * BLOCK : (j + 1) * BLOCK]
                * live_ref[(part * step + i) * BPD + j]
                for j in range(BPD)
            ]
            kacc_ref[rows_of(part * step + i), :] = sum(parts)
            rows.append(jnp.concatenate(parts, axis=1).astype(jnp.bfloat16))
        acc_ref[here, :] = jnp.dot(
            jnp.concatenate(rows, axis=0), u_ref[...], preferred_element_type=jnp.float32
        )

    @functools.partial(loop, tab_ref[core * 8 + COUNTS, 1])
    def _(t):
        pair = tab_ref[core * 8 + 1, t]
        a, b = pair >> 3, pair & 7
        mine, other = jnp.where(core == 0, a, b), jnp.where(core == 0, b, a)
        add_terms(u_ref, sib_ref, acc_ref, kacc_ref, mine, other)


def each_task(task_ref, part, own, got, body):
    row = part * BPD + own

    @functools.partial(loop, task_ref[TASKS + row])
    def _(t):
        place = task_ref[TASK + row * ROW + t]
        for way, ref in enumerate(got):

            @pl.when((place >> 8) == way)
            def _():
                body(ref[rows_of(place & 255), :])


def part_kernel(part, task_ref, u_ref, acc_in, kacc_in, up_ref, down_ref, acc_ref, kacc_ref):
    acc_ref[...] = acc_in[...]
    kacc_ref[...] = kacc_in[...]

    @functools.partial(loop, BPD)
    def _(own):
        here = rows_of(own)

        def add(q):
            kernel = kernel_values(u_ref[here, :], q)
            kacc_ref[here, :] += kernel
            acc_ref[here, :] += jnp.dot(kernel.astype(jnp.bfloat16), q, preferred_element_type=jnp.float32)

        each_task(task_ref, part, own, (up_ref, down_ref), add)


def last_kernel(
    part, task_ref, u_ref, acc_in, kacc_in, up_ref, down_ref, out_ref, log_ref, acc_ref, kacc_ref, done_ref, sems
):
    rows = lax.broadcasted_iota(jnp.int32, (BLOCK, BLOCK), 0)
    diagonal = rows == lax.broadcasted_iota(jnp.int32, (BLOCK, BLOCK), 1)

    def out_copy(own):
        here = rows_of(own)
        return pltpu.make_async_copy(done_ref.at[here, :], out_ref.at[here, :], sems.at[own])

    @functools.partial(loop, BPD)
    def _(own):
        here = rows_of(own)
        acc_ref[...] = acc_in[here, :]
        kacc_ref[...] = kacc_in[here, :]

        def add(q):
            kernel = kernel_values(u_ref[here, :], q)
            kacc_ref[...] += kernel
            acc_ref[...] += jnp.dot(kernel.astype(jnp.bfloat16), q, preferred_element_type=jnp.float32)

        each_task(task_ref, part, own, (up_ref, down_ref), add)
        density = jnp.sum(kacc_ref[...], axis=1, keepdims=True)
        done_ref[here, :] = (
            u_ref[here, :].astype(jnp.float32) - acc_ref[...] * (1.0 / density)
        ).astype(jnp.bfloat16)
        out_copy(own).start()
        across = jnp.sum(jnp.where(diagonal, density, 0.0), axis=0, keepdims=True)
        log_ref[pl.ds(own, 1), :] = jnp.log(across)

    for own in range(BPD):
        out_copy(own).wait()


SMEM = pl.BlockSpec(memory_space=pltpu.SMEM)
VMEM = pl.BlockSpec(memory_space=pltpu.VMEM)
ANY = pl.BlockSpec(memory_space=pl.ANY)


def params(mib):
    return pltpu.CompilerParams(vmem_limit_bytes=mib * 2**20)


def cost(pairs, width):
    return pl.CostEstimate(
        flops=pairs * 4 * BLOCK * BLOCK * width, bytes_accessed=8 * 2**20, transcendentals=pairs * BLOCK * BLOCK
    )


def exchange_and_score(first, second, pos, plan, tables, surplus, unit, sib):
    rows, width = unit.shape
    sends = lambda size: tuple(jax.ShapeDtypeStruct((size * BLOCK, width), jnp.bfloat16) for _ in range(2))
    sums = (
        jax.ShapeDtypeStruct((rows, width), jnp.float32),
        jax.ShapeDtypeStruct((rows, BLOCK), jnp.float32),
    )
    up, down = pl.pallas_call(
        functools.partial(first_pack_kernel, first),
        in_specs=[SMEM, SMEM, VMEM, VMEM],
        out_specs=(VMEM, VMEM),
        out_shape=sends(first),
        scratch_shapes=[pltpu.SemaphoreType.DMA((2 * first,))],
        compiler_params=params(16 + first),
        name="first_pack",
    )(pos, plan, unit, sib)
    got_up, got_down = along_chips(up, 1), along_chips(down, -1)

    places = pl.pallas_call(
        places_kernel,
        in_specs=[SMEM, SMEM, SMEM],
        out_specs=SMEM,
        out_shape=jax.ShapeDtypeStruct((PLACES,), jnp.int32),
        cost_estimate=cost(16, width),
        compiler_params=params(4),
        name="places",
    )(pos, tables, plan)
    acc, kacc = pl.pallas_call(
        own_kernel,
        in_specs=[SMEM, SMEM, SMEM, VMEM, VMEM],
        out_specs=(VMEM, VMEM),
        out_shape=sums,
        scratch_shapes=[pltpu.SMEM((BPD * BPD,), jnp.float32)],
        compiler_params=params(20),
        cost_estimate=cost(64, width),
        name="own_pairs",
    )(pos, tables, surplus, unit, sib)

    got_up, got_down, acc, places = lax.optimization_barrier((got_up, got_down, acc, places))
    up, down = pl.pallas_call(
        functools.partial(second_pack_kernel, first, second),
        in_specs=[SMEM, SMEM] + [VMEM] * 4,
        out_specs=(VMEM, VMEM),
        out_shape=sends(second),
        scratch_shapes=[pltpu.SemaphoreType.DMA((2 * second,))],
        compiler_params=params(16 + second + first),
        name="second_pack",
    )(pos, plan, unit, sib, got_up, got_down)
    far_up, far_down = along_chips(up, 1), along_chips(down, -1)

    def add_part(part, size, acc, kacc, from_below, from_above):
        return pl.pallas_call(
            functools.partial(part_kernel, part),
            in_specs=[SMEM] + [VMEM] * 5,
            out_specs=(VMEM, VMEM),
            out_shape=sums,
            compiler_params=params(16 + size),
            cost_estimate=cost(12, width),
            name=f"part{part}_pairs",
        )(places, unit, acc, kacc, from_below, from_above)

    got_up, got_down, _, _ = lax.optimization_barrier((got_up, got_down, up, down))

    acc, kacc = add_part(0, first, acc, kacc, got_up, got_down)
    got_up, got_down, acc = lax.optimization_barrier((got_up, got_down, acc))
    sib_up, sib_down = to_sibling(got_up), to_sibling(got_down)
    acc, kacc = add_part(1, first, acc, kacc, sib_up, sib_down)
    far_up, far_down, acc = lax.optimization_barrier((far_up, far_down, acc))
    far_sib_up, far_sib_down = to_sibling(far_up), to_sibling(far_down)
    acc, kacc = add_part(2, second, acc, kacc, far_up, far_down)
    far_sib_up, far_sib_down, acc = lax.optimization_barrier((far_sib_up, far_sib_down, acc))
    centered, log_density = pl.pallas_call(
        functools.partial(last_kernel, 3),
        in_specs=[SMEM] + [VMEM] * 5,
        out_specs=(ANY, VMEM),
        out_shape=(
            jax.ShapeDtypeStruct((rows, width), jnp.bfloat16),
            jax.ShapeDtypeStruct((BPD, BLOCK), jnp.float32),
        ),
        scratch_shapes=[
            pltpu.VMEM((BLOCK, width), jnp.float32),
            pltpu.VMEM((BLOCK, BLOCK), jnp.float32),
            pltpu.VMEM((rows, width), jnp.bfloat16),
            pltpu.SemaphoreType.DMA((BPD,)),
        ],
        compiler_params=params(14 + second),
        cost_estimate=cost(8, width),
        name="part3_pairs",
    )(places, unit, acc, kacc, far_sib_up, far_sib_down)
    return centered, log_density


def shards(embeddings, home_pairs, home_count, surplus_pairs):
    rows, width = embeddings.shape
    pairs, count = home_pairs[0, 0], home_count[0, 0]
    shifts = pairs.shape[0]
    pos = lax.axis_index("owner").astype(jnp.int32).reshape(1)

    step = 128
    unit = pl.pallas_call(
        normalize_kernel,
        grid=(rows // step,),
        in_specs=[pl.BlockSpec((step, width), lambda i: (i, 0))],
        out_specs=pl.BlockSpec((step, width), lambda i: (i, 0)),
        out_shape=jax.ShapeDtypeStruct(embeddings.shape, jnp.bfloat16),
        cost_estimate=pl.CostEstimate(flops=2**22, bytes_accessed=2**22, transcendentals=1024),
        compiler_params=params(8),
        name="normalize",
    )(embeddings)

    codes = jnp.sum(pairs * jnp.array([8, 1], jnp.int32), axis=-1)
    table = jnp.pad(codes, ((0, 8 - shifts), (0, 128 - codes.shape[1]))) + jnp.pad(
        count[None], ((COUNTS, 7 - COUNTS), (0, 128 - shifts))
    )

    def turned(x, bits):
        return lax.ppermute(x, "owner", [(o, o ^ bits) for o in range(OWNERS)])

    came, unit = lax.optimization_barrier((turned(table, 1), unit))
    sib = to_sibling(unit)
    tables = jnp.concatenate([table, came], axis=0)
    tables = [tables] + [turned(tables, bits) for bits in (2, 4, 6)]

    plan, tables, chosen = pl.pallas_call(
        plan_kernel,
        in_specs=[SMEM] + [VMEM] * 4,
        out_specs=(SMEM, SMEM, SMEM),
        out_shape=(
            jax.ShapeDtypeStruct((PLAN,), jnp.int32),
            jax.ShapeDtypeStruct((OWNERS * 8, 128), jnp.int32),
            jax.ShapeDtypeStruct((1,), jnp.int32),
        ),
        scratch_shapes=[pltpu.SemaphoreType.DMA((4,))],
        compiler_params=params(4),
        name="plan",
    )(pos, *tables)

    centered, log_density = lax.switch(
        chosen[0],
        [functools.partial(exchange_and_score, *size) for size in SIZES],
        pos, plan, tables, surplus_pairs[0, 0], unit, sib,
    )
    return centered, log_density.reshape(rows)


def solution(mesh):
    return jax.shard_map(
        shards,
        mesh=mesh,
        in_specs=(
            P(("group", "owner"), None),
            P("group", "owner", None, None, None),
            P("group", "owner", None),
            P("group", "owner", None, None),
        ),
        out_specs=(P(("group", "owner"), None), P(("group", "owner"))),
        check_vma=False,
    )
```

```python
import functools

import jax
import jax.numpy as jnp
from jax import lax
from jax.experimental import pallas as pl
from jax.experimental.pallas import tpu as pltpu
from jax.sharding import PartitionSpec as P

BLOCK = 128
BPD = 8
CHIPS = 4
OWNERS = 8
BLOCKS = OWNERS * BPD
ON_CHIP = 2 * BPD
sharpness = 4.0
epsilon = 1e-06
SIZES = ((3, 3), (4, 4), (8, 8))
COUNTS = 5

STRIDE = 32
F_COUNT, D_COUNT, LOAD, FIRST, NEED, TOUCHED, FAR, F_LIST, D_LIST = 0, 8, 16, 24, 32, 96, 161, 256, 512
PLAN = 768
TASKS, TASK, PLACE = 0, 32, 1056
ROW = 32
PLACES = 1152


def loop(count, body):
    def step(i, carry):
        body(i)
        return carry

    lax.fori_loop(0, count, step, 0)


def along_chips(x, hops):
    route = [(o, ((o // 2 + hops) % CHIPS) * 2 + o % 2) for o in range(OWNERS)]
    return lax.ppermute(x, "owner", route)


def to_sibling(x):
    return lax.ppermute(x, "owner", [(o, o ^ 1) for o in range(OWNERS)])


def normalize_kernel(x_ref, u_ref):
    wide = x_ref[...].astype(jnp.float32)
    mean = jnp.mean(wide * wide, axis=-1, keepdims=True)
    u_ref[...] = (wide * lax.rsqrt(mean + epsilon)).astype(jnp.bfloat16)


def rows_of(block):
    return pl.ds(pl.multiple_of(block * BLOCK, BLOCK), BLOCK)


def kernel_values(p, q):
    dots = lax.dot_general(p, q, (((1,), (1,)), ((), ())), preferred_element_type=jnp.float32)
    return jnp.exp(sharpness * (dots * (1.0 / q.shape[1]) - 1.0))


def add_terms(u_ref, q_ref, acc_ref, kacc_ref, mine, other):
    q = q_ref[rows_of(other), :]
    kernel = kernel_values(u_ref[rows_of(mine), :], q)
    kacc_ref[rows_of(mine), :] += kernel
    acc_ref[rows_of(mine), :] += jnp.dot(
        kernel.astype(jnp.bfloat16), q, preferred_element_type=jnp.float32
    )


def plan_kernel(pos_ref, t0, t1, t2, t3, plan_ref, tab_ref, class_ref, sems):
    copies = [
        pltpu.make_async_copy(t, tab_ref.at[i * 16 : (i + 1) * 16, :], sems.at[i])
        for i, t in enumerate((t0, t1, t2, t3))
    ]
    for copy in copies:
        copy.start()
    me = pos_ref[0]
    for i in range(8):
        plan_ref[LOAD + i] = 0
        plan_ref[F_COUNT + i] = 0
        plan_ref[D_COUNT + i] = 0
    for i in range(BLOCKS):
        plan_ref[NEED + i] = 0
    for copy in copies:
        copy.wait()

    def of_owner(o, touched):
        row = (o ^ me) * 8
        for s in range(1, 5):
            q = (o + s) & 7
            to_q, to_o = lax.shift_left(1, q >> 1), lax.shift_left(1, o >> 1)

            def of_pair(t, touched):
                pair = tab_ref[row + s, t]
                for block, chip in ((o * BPD + (pair >> 3), to_q), (q * BPD + (pair & 7), to_o)):
                    before = plan_ref[NEED + block]
                    plan_ref[NEED + block] = before | chip
                    plan_ref[TOUCHED + touched] = block
                    touched = touched + (before == 0).astype(jnp.int32)
                return touched

            touched = lax.fori_loop(0, tab_ref[row + COUNTS, s], of_pair, touched)
        return touched

    touched = lax.fori_loop(0, OWNERS, of_owner, 0)

    def needs(block):
        mask, chip = plan_ref[NEED + block], block >> 4
        bit = lambda hop: lax.shift_right_logical(mask, (chip + hop) & 3) & 1
        return chip, bit(1), bit(3), bit(2)

    def append(count, table, at, block, wanted):
        held = plan_ref[count + at]
        plan_ref[table + at * STRIDE + held] = block
        plan_ref[count + at] = held + wanted

    def one_hop(i, fars):
        block = plan_ref[TOUCHED + i]
        chip, up, down, far = needs(block)
        at = 2 * chip
        plan_ref[LOAD + at] = plan_ref[LOAD + at] + up
        plan_ref[LOAD + at + 1] = plan_ref[LOAD + at + 1] + down
        append(D_COUNT, D_LIST, at, block, up & (1 - far))
        append(D_COUNT, D_LIST, at + 1, block, down & (1 - far))
        plan_ref[FAR + fars] = block
        return fars + far

    fars = lax.fori_loop(0, touched, one_hop, 0)

    @functools.partial(loop, fars)
    def _(i):
        block = plan_ref[FAR + i]
        chip, up, down, _ = needs(block)
        costs, loads = [], []
        for way, near, hop in ((0, up, 1), (1, down, 3)):
            at, after = 2 * chip + way, 2 * ((chip + hop) & 3) + way
            here, there = plan_ref[LOAD + at] + 1 - near, plan_ref[LOAD + after] + 1
            most = jnp.maximum(jnp.maximum(here, there), 2 * plan_ref[F_COUNT + at] + 2)
            costs.append(most * 64 + here + there + 32 * (1 - near))
            loads.append((at, after, here, there))
        goes_down = costs[0] > costs[1]
        at, after, here, there = (jnp.where(goes_down, b, a) for a, b in zip(*loads))
        plan_ref[LOAD + at] = here
        plan_ref[LOAD + after] = there
        append(F_COUNT, F_LIST, at, block, 1)
        append(D_COUNT, D_LIST, at ^ 1, block, jnp.where(goes_down, up, down))

    twice = [plan_ref[F_COUNT + i] for i in range(8)]
    once = [plan_ref[D_COUNT + i] for i in range(8)]
    longest = functools.reduce(jnp.maximum, twice)
    second_needs = {}
    for size in sorted({size for size, _ in SIZES}):
        needs = []
        for i in range(8):
            before = (i + (6 if i % 2 == 0 else 2)) % 8
            needs.append(twice[before] + jnp.maximum(twice[i] + once[i] - 2 * size, 0))
        second_needs[size] = functools.reduce(jnp.maximum, needs)
    chosen, first_size = len(SIZES) - 1, 2 * SIZES[-1][0]
    for k in range(len(SIZES) - 2, -1, -1):
        first, second = SIZES[k]
        fits = (longest <= 2 * first) & (second_needs[first] <= 2 * second)
        chosen = jnp.where(fits, k, chosen)
        first_size = jnp.where(fits, 2 * first, first_size)
    class_ref[0] = chosen
    plan_ref[FIRST] = first_size


def places_kernel(pos_ref, tab_ref, plan_ref, out_ref):
    me = pos_ref[0]
    y, core = me >> 1, me & 1
    first_size = plan_ref[FIRST]
    for i in range(32):
        out_ref[TASKS + i] = 0

    def put(block, stage, way, position):
        other = (position & 1) ^ core
        out_ref[PLACE + block] = (2 * stage + other) * 65536 + way * 256 + (position >> 1)

    for way in (0, 1):
        near = 2 * ((y + (3 if way == 0 else 1)) & 3) + way
        far = 2 * ((y + 2) & 3) + way
        twice, passing = plan_ref[F_COUNT + near], plan_ref[F_COUNT + far]

        @functools.partial(loop, twice)
        def _(i):
            put(plan_ref[F_LIST + near * STRIDE + i], 0, way, i)

        @functools.partial(loop, plan_ref[D_COUNT + near])
        def _(i):
            late = (twice + i >= first_size).astype(jnp.int32)
            put(plan_ref[D_LIST + near * STRIDE + i], late, way, twice + i + late * (passing - first_size))

        @functools.partial(loop, passing)
        def _(i):
            put(plan_ref[F_LIST + far * STRIDE + i], 1, way, i)

    def add_task(own, block):
        place = out_ref[PLACE + block]
        row = (place >> 16) * BPD + own
        count = out_ref[TASKS + row]
        out_ref[TASK + row * ROW + count] = place & 65535
        out_ref[TASKS + row] = count + 1

    for s in range(1, 5):
        above, below = (me + s) & 7, (me - s) & 7

        @pl.when((above >> 1) != y)
        def _():
            @functools.partial(loop, tab_ref[COUNTS, s])
            def _(t):
                pair = tab_ref[s, t]
                add_task(pair >> 3, above * BPD + (pair & 7))

        @pl.when((below >> 1) != y)
        def _():
            row = (below ^ me) * 8

            @functools.partial(loop, tab_ref[row + COUNTS, s])
            def _(t):
                pair = tab_ref[row + s, t]
                add_task(pair & 7, below * BPD + (pair >> 3))


def start_from(id_, core, unit_ref, sib_ref, dst, sem):
    here = rows_of(id_ & 7)
    mine = ((id_ >> 3) & 1) == core

    @pl.when(mine)
    def _():
        pltpu.make_async_copy(unit_ref.at[here, :], dst, sem).start()

    @pl.when(jnp.logical_not(mine))
    def _():
        pltpu.make_async_copy(sib_ref.at[here, :], dst, sem).start()


def listed(plan_ref, row, i, chip):
    twice, once = plan_ref[F_COUNT + row], plan_ref[D_COUNT + row]
    from_f = plan_ref[F_LIST + row * STRIDE + jnp.clip(i, 0, 15)]
    from_d = plan_ref[D_LIST + row * STRIDE + jnp.clip(i - twice, 0, 15)]
    found = jnp.where(i < twice, from_f, from_d)
    return jnp.where(i < twice + once, found, chip * ON_CHIP)


def first_pack_kernel(size, pos_ref, plan_ref, unit_ref, sib_ref, up_ref, down_ref, sems):
    y, core = pos_ref[0] >> 1, pos_ref[0] & 1
    slots = [(way, j, out) for way, out in ((0, up_ref), (1, down_ref)) for j in range(size)]
    for n, (way, j, out) in enumerate(slots):
        block = listed(plan_ref, 2 * y + way, 2 * j + core, y)
        start_from(block, core, unit_ref, sib_ref, out.at[j * BLOCK : (j + 1) * BLOCK, :], sems.at[n])
    for n, (way, j, out) in enumerate(slots):
        pltpu.make_async_copy(
            unit_ref.at[0:BLOCK, :], out.at[j * BLOCK : (j + 1) * BLOCK, :], sems.at[n]
        ).wait()


def second_pack_kernel(
    first, size, pos_ref, plan_ref, unit_ref, sib_ref, got_up, got_down, up_ref, down_ref, sems
):
    y, core = pos_ref[0] >> 1, pos_ref[0] & 1
    slots = [
        (way, j, out, got)
        for way, out, got in ((0, up_ref, got_up), (1, down_ref, got_down))
        for j in range(size)
    ]
    for n, (way, j, out, got) in enumerate(slots):
        dst = out.at[j * BLOCK : (j + 1) * BLOCK, :]
        position = 2 * j + core
        passing = plan_ref[F_COUNT + 2 * ((y + (3 if way == 0 else 1)) & 3) + way]
        passes = (position < passing) if j < first else (position < 0)
        if j < first:

            @pl.when(passes)
            def _():
                pltpu.make_async_copy(got.at[j * BLOCK : (j + 1) * BLOCK, :], dst, sems.at[n]).start()

        @pl.when(jnp.logical_not(passes))
        def _():
            block = listed(plan_ref, 2 * y + way, position - passing + 2 * first, y)
            start_from(block, core, unit_ref, sib_ref, dst, sems.at[n])

    for n, (way, j, out, got) in enumerate(slots):
        pltpu.make_async_copy(
            unit_ref.at[0:BLOCK, :], out.at[j * BLOCK : (j + 1) * BLOCK, :], sems.at[n]
        ).wait()


def own_kernel(pos_ref, tab_ref, surplus_ref, u_ref, sib_ref, acc_ref, kacc_ref, live_ref):
    core = pos_ref[0] & 1

    @functools.partial(loop, BPD * BPD)
    def _(i):
        live_ref[i] = 0.0

    def mark(a, b):
        live_ref[a * BPD + b] = 1.0
        live_ref[b * BPD + a] = 1.0

    @functools.partial(loop, tab_ref[COUNTS, 0])
    def _(t):
        pair = tab_ref[0, t]
        mark(pair >> 3, pair & 7)

    @functools.partial(loop, surplus_ref.shape[0])
    def _(t):
        @pl.when(surplus_ref[t, 2] == 1)
        def _():
            mark(surplus_ref[t, 0], surplus_ref[t, 1])

    step = 2

    @functools.partial(loop, BPD // step)
    def _(part):
        here = pl.ds(pl.multiple_of(part * step * BLOCK, step * BLOCK), step * BLOCK)
        kernel = kernel_values(u_ref[here, :], u_ref[...])
        rows = []
        for i in range(step):
            parts = [
                kernel[i * BLOCK : (i + 1) * BLOCK, j * BLOCK : (j + 1) * BLOCK]
                * live_ref[(part * step + i) * BPD + j]
                for j in range(BPD)
            ]
            kacc_ref[rows_of(part * step + i), :] = sum(parts)
            rows.append(jnp.concatenate(parts, axis=1).astype(jnp.bfloat16))
        acc_ref[here, :] = jnp.dot(
            jnp.concatenate(rows, axis=0), u_ref[...], preferred_element_type=jnp.float32
        )

    @functools.partial(loop, tab_ref[core * 8 + COUNTS, 1])
    def _(t):
        pair = tab_ref[core * 8 + 1, t]
        a, b = pair >> 3, pair & 7
        mine, other = jnp.where(core == 0, a, b), jnp.where(core == 0, b, a)
        add_terms(u_ref, sib_ref, acc_ref, kacc_ref, mine, other)


def each_task(task_ref, part, own, got, body):
    row = part * BPD + own

    @functools.partial(loop, task_ref[TASKS + row])
    def _(t):
        place = task_ref[TASK + row * ROW + t]
        for way, ref in enumerate(got):

            @pl.when((place >> 8) == way)
            def _():
                body(ref[rows_of(place & 255), :])


def part_kernel(part, task_ref, u_ref, acc_in, kacc_in, up_ref, down_ref, acc_ref, kacc_ref):
    acc_ref[...] = acc_in[...]
    kacc_ref[...] = kacc_in[...]

    @functools.partial(loop, BPD)
    def _(own):
        here = rows_of(own)

        def add(q):
            kernel = kernel_values(u_ref[here, :], q)
            kacc_ref[here, :] += kernel
            acc_ref[here, :] += jnp.dot(kernel.astype(jnp.bfloat16), q, preferred_element_type=jnp.float32)

        each_task(task_ref, part, own, (up_ref, down_ref), add)


def last_kernel(
    part, task_ref, u_ref, acc_in, kacc_in, up_ref, down_ref, out_ref, log_ref, acc_ref, kacc_ref, done_ref, sems
):
    rows = lax.broadcasted_iota(jnp.int32, (BLOCK, BLOCK), 0)
    diagonal = rows == lax.broadcasted_iota(jnp.int32, (BLOCK, BLOCK), 1)

    def out_copy(own):
        here = rows_of(own)
        return pltpu.make_async_copy(done_ref.at[here, :], out_ref.at[here, :], sems.at[own])

    @functools.partial(loop, BPD)
    def _(own):
        here = rows_of(own)
        acc_ref[...] = acc_in[here, :]
        kacc_ref[...] = kacc_in[here, :]

        def add(q):
            kernel = kernel_values(u_ref[here, :], q)
            kacc_ref[...] += kernel
            acc_ref[...] += jnp.dot(kernel.astype(jnp.bfloat16), q, preferred_element_type=jnp.float32)

        each_task(task_ref, part, own, (up_ref, down_ref), add)
        density = jnp.sum(kacc_ref[...], axis=1, keepdims=True)
        done_ref[here, :] = (
            u_ref[here, :].astype(jnp.float32) - acc_ref[...] * (1.0 / density)
        ).astype(jnp.bfloat16)
        out_copy(own).start()
        across = jnp.sum(jnp.where(diagonal, density, 0.0), axis=0, keepdims=True)
        log_ref[pl.ds(own, 1), :] = jnp.log(across)

    for own in range(BPD):
        out_copy(own).wait()


SMEM = pl.BlockSpec(memory_space=pltpu.SMEM)
VMEM = pl.BlockSpec(memory_space=pltpu.VMEM)
ANY = pl.BlockSpec(memory_space=pl.ANY)


def params():
    return pltpu.CompilerParams(vmem_limit_bytes=26 * 2**20)


COST = pl.CostEstimate(flops=1, bytes_accessed=1, transcendentals=0)


def sends(size, width):
    return tuple(jax.ShapeDtypeStruct((size * BLOCK, width), jnp.bfloat16) for _ in range(2))


def first_pack(first, pos, plan, unit, sib):
    return pl.pallas_call(
        functools.partial(first_pack_kernel, first),
        in_specs=[SMEM, SMEM, VMEM, VMEM],
        out_specs=(VMEM, VMEM),
        out_shape=sends(first, unit.shape[1]),
        scratch_shapes=[pltpu.SemaphoreType.DMA((2 * first,))],
        compiler_params=params(),
        name="first_pack",
    )(pos, plan, unit, sib)


def exchange_and_score(first, second, packed, pos, plan, tables, surplus, unit, sib):
    rows, width = unit.shape
    sums = (
        jax.ShapeDtypeStruct((rows, width), jnp.float32),
        jax.ShapeDtypeStruct((rows, BLOCK), jnp.float32),
    )
    up, down = packed if first == SIZES[0][0] else first_pack(first, pos, plan, unit, sib)
    got_up, got_down = along_chips(up, 1), along_chips(down, -1)

    places = pl.pallas_call(
        places_kernel,
        in_specs=[SMEM, SMEM, SMEM],
        out_specs=SMEM,
        out_shape=jax.ShapeDtypeStruct((PLACES,), jnp.int32),
        cost_estimate=COST,
        compiler_params=params(),
        name="places",
    )(pos, tables, plan)
    acc, kacc = pl.pallas_call(
        own_kernel,
        in_specs=[SMEM, SMEM, SMEM, VMEM, VMEM],
        out_specs=(VMEM, VMEM),
        out_shape=sums,
        scratch_shapes=[pltpu.SMEM((BPD * BPD,), jnp.float32)],
        compiler_params=params(),
        cost_estimate=COST,
        name="own_pairs",
    )(pos, tables, surplus, unit, sib)

    got_up, got_down, acc, places = lax.optimization_barrier((got_up, got_down, acc, places))
    up, down = pl.pallas_call(
        functools.partial(second_pack_kernel, first, second),
        in_specs=[SMEM, SMEM] + [VMEM] * 4,
        out_specs=(VMEM, VMEM),
        out_shape=sends(second, width),
        scratch_shapes=[pltpu.SemaphoreType.DMA((2 * second,))],
        compiler_params=params(),
        name="second_pack",
    )(pos, plan, unit, sib, got_up, got_down)
    far_up, far_down = along_chips(up, 1), along_chips(down, -1)

    def add_part(part, size, acc, kacc, from_below, from_above):
        return pl.pallas_call(
            functools.partial(part_kernel, part),
            in_specs=[SMEM] + [VMEM] * 5,
            out_specs=(VMEM, VMEM),
            out_shape=sums,
            compiler_params=params(),
            cost_estimate=COST,
            name=f"part{part}_pairs",
        )(places, unit, acc, kacc, from_below, from_above)

    def beside(got_up, got_down, acc, kacc):
        acc, kacc = add_part(0, first, acc, kacc, got_up, got_down)
        got_up, got_down, acc = lax.optimization_barrier((got_up, got_down, acc))
        sib_up, sib_down = to_sibling(got_up), to_sibling(got_down)
        return add_part(1, first, acc, kacc, sib_up, sib_down)

    got_up, got_down, up, down = lax.optimization_barrier((got_up, got_down, up, down))
    acc, kacc = lax.cond(plan[FIRST] > 0, beside, lambda u, d, a, k: (a, k), got_up, got_down, acc, kacc)
    far_up, far_down, acc = lax.optimization_barrier((far_up, far_down, acc))
    far_sib_up, far_sib_down = to_sibling(far_up), to_sibling(far_down)
    acc, kacc = add_part(2, second, acc, kacc, far_up, far_down)
    far_sib_up, far_sib_down, acc = lax.optimization_barrier((far_sib_up, far_sib_down, acc))
    centered, log_density = pl.pallas_call(
        functools.partial(last_kernel, 3),
        in_specs=[SMEM] + [VMEM] * 5,
        out_specs=(ANY, VMEM),
        out_shape=(
            jax.ShapeDtypeStruct((rows, width), jnp.bfloat16),
            jax.ShapeDtypeStruct((BPD, BLOCK), jnp.float32),
        ),
        scratch_shapes=[
            pltpu.VMEM((BLOCK, width), jnp.float32),
            pltpu.VMEM((BLOCK, BLOCK), jnp.float32),
            pltpu.VMEM((rows, width), jnp.bfloat16),
            pltpu.SemaphoreType.DMA((BPD,)),
        ],
        compiler_params=params(),
        cost_estimate=COST,
        name="part3_pairs",
    )(places, unit, acc, kacc, far_sib_up, far_sib_down)
    return centered, log_density


def shards(embeddings, home_pairs, home_count, surplus_pairs):
    rows, width = embeddings.shape
    pairs, count = home_pairs[0, 0], home_count[0, 0]
    shifts = pairs.shape[0]
    pos = lax.axis_index("owner").astype(jnp.int32).reshape(1)

    step = 128
    unit = pl.pallas_call(
        normalize_kernel,
        grid=(rows // step,),
        in_specs=[pl.BlockSpec((step, width), lambda i: (i, 0))],
        out_specs=pl.BlockSpec((step, width), lambda i: (i, 0)),
        out_shape=jax.ShapeDtypeStruct(embeddings.shape, jnp.bfloat16),
        cost_estimate=COST,
        compiler_params=params(),
        name="normalize",
    )(embeddings)

    codes = jnp.sum(pairs * jnp.array([8, 1], jnp.int32), axis=-1)
    table = jnp.pad(codes, ((0, 8 - shifts), (0, 128 - codes.shape[1]))) + jnp.pad(
        count[None], ((COUNTS, 7 - COUNTS), (0, 128 - shifts))
    )

    def turned(x, bits):
        return lax.ppermute(x, "owner", [(o, o ^ bits) for o in range(OWNERS)])

    came, unit = lax.optimization_barrier((turned(table, 1), unit))
    sib = to_sibling(unit)
    tables = jnp.concatenate([table, came], axis=0)
    tables = [tables] + [turned(tables, bits) for bits in (2, 4, 6)]

    plan, tables, chosen = pl.pallas_call(
        plan_kernel,
        in_specs=[SMEM] + [VMEM] * 4,
        out_specs=(SMEM, SMEM, SMEM),
        out_shape=(
            jax.ShapeDtypeStruct((PLAN,), jnp.int32),
            jax.ShapeDtypeStruct((OWNERS * 8, 128), jnp.int32),
            jax.ShapeDtypeStruct((1,), jnp.int32),
        ),
        scratch_shapes=[pltpu.SemaphoreType.DMA((4,))],
        compiler_params=params(),
        name="plan",
    )(pos, *tables)

    packed = first_pack(SIZES[0][0], pos, plan, unit, sib)
    centered, log_density = lax.switch(
        chosen[0],
        [functools.partial(exchange_and_score, *size) for size in SIZES],
        packed, pos, plan, tables, surplus_pairs[0, 0], unit, sib,
    )
    return centered, log_density.reshape(rows)


def solution(mesh):
    return jax.shard_map(
        shards,
        mesh=mesh,
        in_specs=(
            P(("group", "owner"), None),
            P("group", "owner", None, None, None),
            P("group", "owner", None),
            P("group", "owner", None, None),
        ),
        out_specs=(P(("group", "owner"), None), P(("group", "owner"))),
        check_vma=False,
    )
```

```python
import functools

import jax
import jax.numpy as jnp
from jax import lax
from jax.experimental import pallas as pl
from jax.experimental.pallas import tpu as pltpu
from jax.sharding import PartitionSpec as P

BLOCK = 128
BPD = 8
CHIPS = 4
OWNERS = 8
BLOCKS = OWNERS * BPD
ON_CHIP = 2 * BPD
sharpness = 4.0
epsilon = 1e-06
SIZES = (5, 6, 8, 16)
OWN_STEP = 1
COUNTS = 5

STRIDE = 32
F_COUNT, D_COUNT, LOAD, SIZE, NEED, TOUCHED, FAR, F_LIST, D_LIST = 0, 8, 16, 24, 32, 96, 161, 256, 512
PLAN = 768
TASKS, TASK, PLACE = 0, 16, 1040
ROW = 64
PLACES = 1152


def loop(count, body):
    def step(i, carry):
        body(i)
        return carry

    lax.fori_loop(0, count, step, 0)


def along_chips(x, hops):
    route = [(o, ((o // 2 + hops) % CHIPS) * 2 + o % 2) for o in range(OWNERS)]
    return lax.ppermute(x, "owner", route)


def one_up_one_down(x):
    route = [(o, ((o // 2 + (1 if o % 2 == 0 else -1)) % CHIPS) * 2 + o % 2) for o in range(OWNERS)]
    return lax.ppermute(x, "owner", route)


def to_sibling(x):
    return lax.ppermute(x, "owner", [(o, o ^ 1) for o in range(OWNERS)])


def normalize_kernel(x_ref, u_ref):
    wide = x_ref[...].astype(jnp.float32)
    mean = jnp.mean(wide * wide, axis=-1, keepdims=True)
    u_ref[...] = (wide * lax.rsqrt(mean + epsilon)).astype(jnp.bfloat16)


def rows_of(block):
    return pl.ds(pl.multiple_of(block * BLOCK, BLOCK), BLOCK)


def kernel_values(p, q):
    dots = lax.dot_general(p, q, (((1,), (1,)), ((), ())), preferred_element_type=jnp.float32)
    return jnp.exp(sharpness * (dots * (1.0 / q.shape[1]) - 1.0))


def add_terms(u_ref, q_ref, acc_ref, kacc_ref, mine, other):
    q = q_ref[rows_of(other), :]
    kernel = kernel_values(u_ref[rows_of(mine), :], q)
    kacc_ref[rows_of(mine), :] += kernel
    acc_ref[rows_of(mine), :] += jnp.dot(
        kernel.astype(jnp.bfloat16), q, preferred_element_type=jnp.float32
    )


def plan_kernel(pos_ref, t0, t1, t2, t3, plan_ref, tab_ref, class_ref, sems):
    copies = [
        pltpu.make_async_copy(t, tab_ref.at[i * 16 : (i + 1) * 16, :], sems.at[i])
        for i, t in enumerate((t0, t1, t2, t3))
    ]
    for copy in copies:
        copy.start()
    me = pos_ref[0]
    for i in range(8):
        plan_ref[LOAD + i] = 0
        plan_ref[F_COUNT + i] = 0
        plan_ref[D_COUNT + i] = 0
    for i in range(BLOCKS):
        plan_ref[NEED + i] = 0
    for copy in copies:
        copy.wait()

    def of_owner(o, touched):
        row = (o ^ me) * 8
        for s in range(1, 5):
            q = (o + s) & 7
            to_q, to_o = lax.shift_left(1, q >> 1), lax.shift_left(1, o >> 1)

            def of_pair(t, touched):
                pair = tab_ref[row + s, t]
                for block, chip in ((o * BPD + (pair >> 3), to_q), (q * BPD + (pair & 7), to_o)):
                    before = plan_ref[NEED + block]
                    plan_ref[NEED + block] = before | chip
                    plan_ref[TOUCHED + touched] = block
                    touched = touched + (before == 0).astype(jnp.int32)
                return touched

            touched = lax.fori_loop(0, tab_ref[row + COUNTS, s], of_pair, touched)
        return touched

    touched = lax.fori_loop(0, OWNERS, of_owner, 0)

    def needs(block):
        mask, chip = plan_ref[NEED + block], block >> 4
        bit = lambda hop: lax.shift_right_logical(mask, (chip + hop) & 3) & 1
        return chip, bit(1), bit(3), bit(2)

    def append(count, table, at, block, wanted):
        held = plan_ref[count + at]
        plan_ref[table + at * STRIDE + held] = block
        plan_ref[count + at] = held + wanted

    def one_hop(i, fars):
        block = plan_ref[TOUCHED + i]
        chip, up, down, far = needs(block)
        at = 2 * chip
        plan_ref[LOAD + at] = plan_ref[LOAD + at] + up
        plan_ref[LOAD + at + 1] = plan_ref[LOAD + at + 1] + down
        append(D_COUNT, D_LIST, at, block, up & (1 - far))
        append(D_COUNT, D_LIST, at + 1, block, down & (1 - far))
        plan_ref[FAR + fars] = block
        return fars + far

    fars = lax.fori_loop(0, touched, one_hop, 0)

    @functools.partial(loop, fars)
    def _(i):
        block = plan_ref[FAR + i]
        chip, up, down, _ = needs(block)
        costs, loads = [], []
        for way, near, hop in ((0, up, 1), (1, down, 3)):
            at, after = 2 * chip + way, 2 * ((chip + hop) & 3) + way
            here, there = plan_ref[LOAD + at] + 1 - near, plan_ref[LOAD + after] + 1
            most = jnp.maximum(jnp.maximum(here, there), 2 * plan_ref[F_COUNT + at] + 2)
            costs.append(most * 64 + here + there + 32 * (1 - near))
            loads.append((at, after, here, there))
        goes_down = costs[0] > costs[1]
        at, after, here, there = (jnp.where(goes_down, b, a) for a, b in zip(*loads))
        plan_ref[LOAD + at] = here
        plan_ref[LOAD + after] = there
        append(F_COUNT, F_LIST, at, block, 1)
        append(D_COUNT, D_LIST, at ^ 1, block, jnp.where(goes_down, up, down))

    twice = [plan_ref[F_COUNT + i] for i in range(8)]
    once = [plan_ref[D_COUNT + i] for i in range(8)]
    longest = functools.reduce(jnp.maximum, twice)
    chosen, chosen_size = len(SIZES) - 1, SIZES[-1]
    for k in range(len(SIZES) - 2, -1, -1):
        size = SIZES[k]
        needs = []
        for i in range(8):
            before = (i + (6 if i % 2 == 0 else 2)) % 8
            needs.append(twice[before] + jnp.maximum(twice[i] + once[i] - size, 0))
        fits = jnp.maximum(longest, functools.reduce(jnp.maximum, needs)) <= size
        chosen = jnp.where(fits, k, chosen)
        chosen_size = jnp.where(fits, size, chosen_size)
    class_ref[0] = chosen
    plan_ref[SIZE] = chosen_size


def places_kernel(pos_ref, tab_ref, plan_ref, out_ref):
    me = pos_ref[0]
    y, core = me >> 1, me & 1
    size = plan_ref[SIZE]
    for i in range(16):
        out_ref[TASKS + i] = 0

    def put(block, stage, way, position):
        other = ((position + way) & 1) ^ core
        slot = position >> 1
        last = (slot >= (size >> 1)).astype(jnp.int32)
        piece = 3 * other + jnp.where(last == 1, 2, way)
        out_ref[PLACE + block] = stage * 65536 + piece * 256 + slot * (1 - last)

    for way in (0, 1):
        near = 2 * ((y + (3 if way == 0 else 1)) & 3) + way
        far = 2 * ((y + 2) & 3) + way
        twice, passing = plan_ref[F_COUNT + near], plan_ref[F_COUNT + far]

        @functools.partial(loop, twice)
        def _(i):
            put(plan_ref[F_LIST + near * STRIDE + i], 0, way, i)

        @functools.partial(loop, plan_ref[D_COUNT + near])
        def _(i):
            late = (twice + i >= size).astype(jnp.int32)
            put(plan_ref[D_LIST + near * STRIDE + i], late, way, twice + i + late * (passing - size))

        @functools.partial(loop, passing)
        def _(i):
            put(plan_ref[F_LIST + far * STRIDE + i], 1, way, i)

    def add_task(own, block):
        place = out_ref[PLACE + block]
        row = (place >> 16) * BPD + own
        count = out_ref[TASKS + row]
        out_ref[TASK + row * ROW + count] = place & 65535
        out_ref[TASKS + row] = count + 1

    for s in range(1, 5):
        above, below = (me + s) & 7, (me - s) & 7

        @pl.when((above >> 1) != y)
        def _():
            @functools.partial(loop, tab_ref[COUNTS, s])
            def _(t):
                pair = tab_ref[s, t]
                add_task(pair >> 3, above * BPD + (pair & 7))

        @pl.when((below >> 1) != y)
        def _():
            row = (below ^ me) * 8

            @functools.partial(loop, tab_ref[row + COUNTS, s])
            def _(t):
                pair = tab_ref[row + s, t]
                add_task(pair & 7, below * BPD + (pair >> 3))


def start_from(id_, core, unit_ref, sib_ref, dst, sem):
    here = rows_of(id_ & 7)
    mine = ((id_ >> 3) & 1) == core

    @pl.when(mine)
    def _():
        pltpu.make_async_copy(unit_ref.at[here, :], dst, sem).start()

    @pl.when(jnp.logical_not(mine))
    def _():
        pltpu.make_async_copy(sib_ref.at[here, :], dst, sem).start()


def listed(plan_ref, row, i, chip):
    twice, once = plan_ref[F_COUNT + row], plan_ref[D_COUNT + row]
    from_f = plan_ref[F_LIST + row * STRIDE + jnp.clip(i, 0, 15)]
    from_d = plan_ref[D_LIST + row * STRIDE + jnp.clip(i - twice, 0, 15)]
    found = jnp.where(i < twice, from_f, from_d)
    return jnp.where(i < twice + once, found, chip * ON_CHIP)


def slots_of(size, core):
    slots = [(way, j, way, 2 * j + (core ^ way)) for way in (0, 1) for j in range(size // 2)]
    return slots + [(2, 0, core, size - 1)] * (size % 2)


def place_ref(ref, j):
    return ref.at[j * BLOCK : (j + 1) * BLOCK, :]


def first_pack_kernel(size, pos_ref, plan_ref, unit_ref, sib_ref, *refs):
    pieces, sems = refs[:-1], refs[-1]
    y, core = pos_ref[0] >> 1, pos_ref[0] & 1
    for n, (piece, j, way, position) in enumerate(slots_of(size, core)):
        block = listed(plan_ref, 2 * y + way, position, y)
        start_from(block, core, unit_ref, sib_ref, place_ref(pieces[piece], j), sems.at[n])
    for n, (piece, j, _, _) in enumerate(slots_of(size, core)):
        pltpu.make_async_copy(place_ref(unit_ref, 0), place_ref(pieces[piece], j), sems.at[n]).wait()


def second_pack_kernel(size, pos_ref, plan_ref, unit_ref, sib_ref, *refs):
    got, pieces, sems = refs[: len(refs) // 2], refs[len(refs) // 2 : -1], refs[-1]
    y, core = pos_ref[0] >> 1, pos_ref[0] & 1
    for n, (piece, j, way, position) in enumerate(slots_of(size, core)):
        passing = plan_ref[F_COUNT + 2 * ((y + 3 + 2 * way) & 3) + way]
        dst = place_ref(pieces[piece], j)

        @pl.when(position < passing)
        def _():
            pltpu.make_async_copy(place_ref(got[piece], j), dst, sems.at[n]).start()

        @pl.when(position >= passing)
        def _():
            block = listed(plan_ref, 2 * y + way, position - passing + size, y)
            start_from(block, core, unit_ref, sib_ref, dst, sems.at[n])

    for n, (piece, j, _, _) in enumerate(slots_of(size, core)):
        pltpu.make_async_copy(place_ref(unit_ref, 0), place_ref(pieces[piece], j), sems.at[n]).wait()


def own_kernel(pos_ref, tab_ref, surplus_ref, u_ref, sib_ref, acc_ref, kacc_ref, live_ref):
    core = pos_ref[0] & 1

    @functools.partial(loop, BPD * BPD)
    def _(i):
        live_ref[i] = 0.0

    def mark(a, b):
        live_ref[a * BPD + b] = 1.0
        live_ref[b * BPD + a] = 1.0

    @functools.partial(loop, tab_ref[COUNTS, 0])
    def _(t):
        pair = tab_ref[0, t]
        mark(pair >> 3, pair & 7)

    @functools.partial(loop, surplus_ref.shape[0])
    def _(t):
        @pl.when(surplus_ref[t, 2] == 1)
        def _():
            mark(surplus_ref[t, 0], surplus_ref[t, 1])

    step = OWN_STEP

    @functools.partial(loop, BPD // step)
    def _(part):
        here = pl.ds(pl.multiple_of(part * step * BLOCK, step * BLOCK), step * BLOCK)
        kernel = kernel_values(u_ref[here, :], u_ref[...])
        rows = []
        for i in range(step):
            parts = [
                kernel[i * BLOCK : (i + 1) * BLOCK, j * BLOCK : (j + 1) * BLOCK]
                * live_ref[(part * step + i) * BPD + j]
                for j in range(BPD)
            ]
            kacc_ref[rows_of(part * step + i), :] = sum(parts)
            rows.append(jnp.concatenate(parts, axis=1).astype(jnp.bfloat16))
        acc_ref[here, :] = jnp.dot(
            jnp.concatenate(rows, axis=0), u_ref[...], preferred_element_type=jnp.float32
        )

    @functools.partial(loop, tab_ref[core * 8 + COUNTS, 1])
    def _(t):
        pair = tab_ref[core * 8 + 1, t]
        a, b = pair >> 3, pair & 7
        mine, other = jnp.where(core == 0, a, b), jnp.where(core == 0, b, a)
        add_terms(u_ref, sib_ref, acc_ref, kacc_ref, mine, other)


def each_task(stage, task_ref, own, pieces, q_ref, body):
    row = stage * BPD + own

    @functools.partial(loop, task_ref[TASKS + row])
    def _(t):
        place = task_ref[TASK + row * ROW + t]
        for n, piece in pieces:

            @pl.when((place >> 8) == n)
            def _():
                q_ref[...] = piece[rows_of(place & 255), :]

        body(q_ref[...])


def numbered(refs):
    half = len(refs) // 2
    return [(n, ref) for n, ref in enumerate(refs[:half])] + [(3 + n, ref) for n, ref in enumerate(refs[half:])]


def first_part_kernel(task_ref, u_ref, acc_in, kacc_in, *refs):
    pieces, (acc_ref, kacc_ref, q_ref) = numbered(refs[:-3]), refs[-3:]
    acc_ref[...] = acc_in[...]
    kacc_ref[...] = kacc_in[...]

    @functools.partial(loop, BPD)
    def _(own):
        here = rows_of(own)

        def add(q):
            kernel = kernel_values(u_ref[here, :], q)
            kacc_ref[here, :] += kernel
            acc_ref[here, :] += jnp.dot(kernel.astype(jnp.bfloat16), q, preferred_element_type=jnp.float32)

        each_task(0, task_ref, own, pieces, q_ref, add)


def last_kernel(task_ref, u_ref, acc_in, kacc_in, *refs):
    pieces, (out_ref, log_ref, acc_ref, kacc_ref, q_ref, done_ref, sems) = numbered(refs[:-7]), refs[-7:]
    rows = lax.broadcasted_iota(jnp.int32, (BLOCK, BLOCK), 0)
    diagonal = rows == lax.broadcasted_iota(jnp.int32, (BLOCK, BLOCK), 1)

    def out_copy(own):
        here = rows_of(own)
        return pltpu.make_async_copy(done_ref.at[here, :], out_ref.at[here, :], sems.at[own])

    @functools.partial(loop, BPD)
    def _(own):
        here = rows_of(own)
        acc_ref[...] = acc_in[here, :]
        kacc_ref[...] = kacc_in[here, :]

        def add(q):
            kernel = kernel_values(u_ref[here, :], q)
            kacc_ref[...] += kernel
            acc_ref[...] += jnp.dot(kernel.astype(jnp.bfloat16), q, preferred_element_type=jnp.float32)

        each_task(1, task_ref, own, pieces, q_ref, add)
        density = jnp.sum(kacc_ref[...], axis=1, keepdims=True)
        done_ref[here, :] = (
            u_ref[here, :].astype(jnp.float32) - acc_ref[...] * (1.0 / density)
        ).astype(jnp.bfloat16)
        out_copy(own).start()
        across = jnp.sum(jnp.where(diagonal, density, 0.0), axis=0, keepdims=True)
        log_ref[pl.ds(own, 1), :] = jnp.log(across)

    for own in range(BPD):
        out_copy(own).wait()


SMEM = pl.BlockSpec(memory_space=pltpu.SMEM)
VMEM = pl.BlockSpec(memory_space=pltpu.VMEM)
ANY = pl.BlockSpec(memory_space=pl.ANY)
HBM = pl.BlockSpec(memory_space=pltpu.HBM)


def params():
    return pltpu.CompilerParams(vmem_limit_bytes=26 * 2**20)


COST = pl.CostEstimate(flops=1, bytes_accessed=1, transcendentals=0)


def pieces_of(size, width):
    counts = [size // 2] * 2 + [1] * (size % 2)
    return tuple(jax.ShapeDtypeStruct((count * BLOCK, width), jnp.bfloat16) for count in counts)


def send(pieces):
    moved = [along_chips(pieces[0], 1), along_chips(pieces[1], -1)]
    return moved + [one_up_one_down(x) for x in pieces[2:]]


def exchange_and_score(size, pos, plan, tables, surplus, unit, sib):
    rows, width = unit.shape
    sums = (
        jax.ShapeDtypeStruct((rows, width), jnp.float32),
        jax.ShapeDtypeStruct((rows, BLOCK), jnp.float32),
    )

    def pack(kernel, name, *operands):
        out = pieces_of(size, width)
        return pl.pallas_call(
            functools.partial(kernel, size),
            in_specs=[SMEM, SMEM, HBM, HBM] + [ANY] * (len(operands) - 4),
            out_specs=(VMEM,) * len(out),
            out_shape=out,
            scratch_shapes=[pltpu.SemaphoreType.DMA((size,))],
            compiler_params=params(),
            name=name,
        )(*operands)

    got = send(pack(first_pack_kernel, "first_pack", pos, plan, unit, sib))
    places = pl.pallas_call(
        places_kernel,
        in_specs=[SMEM, SMEM, SMEM],
        out_specs=SMEM,
        out_shape=jax.ShapeDtypeStruct((PLACES,), jnp.int32),
        cost_estimate=COST,
        compiler_params=params(),
        name="places",
    )(pos, tables, plan)
    acc, kacc = pl.pallas_call(
        own_kernel,
        in_specs=[SMEM, SMEM, SMEM, VMEM, VMEM],
        out_specs=(VMEM, VMEM),
        out_shape=sums,
        scratch_shapes=[pltpu.SMEM((BPD * BPD,), jnp.float32)],
        compiler_params=params(),
        cost_estimate=COST,
        name="own_pairs",
    )(pos, tables, surplus, unit, sib)
    *got, acc, places = lax.optimization_barrier((*got, acc, places))
    passed_on = pack(second_pack_kernel, "second_pack", pos, plan, unit, sib, *got)
    far = send(passed_on)

    def beside(acc, kacc, *here):
        there = []
        for x in here:
            if there:
                x, there[-1] = lax.optimization_barrier((x, there[-1]))
            there.append(to_sibling(x))
        return pl.pallas_call(
            first_part_kernel,
            in_specs=[SMEM] + [VMEM] * (3 + 2 * len(here)),
            out_specs=(VMEM, VMEM),
            out_shape=sums,
            scratch_shapes=[pltpu.VMEM((BLOCK, width), jnp.bfloat16)],
            compiler_params=params(),
            cost_estimate=COST,
            name="first_part",
        )(places, unit, acc, kacc, *here, *there)

    here = lax.optimization_barrier((*got, *passed_on))[: len(got)]
    acc, kacc = lax.cond(plan[SIZE] > 0, beside, lambda a, k, *_: (a, k), acc, kacc, *here)

    *far, acc = lax.optimization_barrier((*far, acc))
    sib_far = [to_sibling(x) for x in far]
    return pl.pallas_call(
        last_kernel,
        in_specs=[SMEM] + [VMEM] * (3 + 2 * len(far)),
        out_specs=(ANY, VMEM),
        out_shape=(
            jax.ShapeDtypeStruct((rows, width), jnp.bfloat16),
            jax.ShapeDtypeStruct((BPD, BLOCK), jnp.float32),
        ),
        scratch_shapes=[
            pltpu.VMEM((BLOCK, width), jnp.float32),
            pltpu.VMEM((BLOCK, BLOCK), jnp.float32),
            pltpu.VMEM((BLOCK, width), jnp.bfloat16),
            pltpu.VMEM((rows, width), jnp.bfloat16),
            pltpu.SemaphoreType.DMA((BPD,)),
        ],
        compiler_params=params(),
        cost_estimate=COST,
        name="last_part",
    )(places, unit, acc, kacc, *far, *sib_far)


def shards(embeddings, home_pairs, home_count, surplus_pairs):
    rows, width = embeddings.shape
    pairs, count = home_pairs[0, 0], home_count[0, 0]
    shifts = pairs.shape[0]
    pos = lax.axis_index("owner").astype(jnp.int32).reshape(1)

    step = 128
    unit = pl.pallas_call(
        normalize_kernel,
        grid=(rows // step,),
        in_specs=[pl.BlockSpec((step, width), lambda i: (i, 0))],
        out_specs=pl.BlockSpec((step, width), lambda i: (i, 0)),
        out_shape=pltpu.HBM(embeddings.shape, jnp.bfloat16),
        cost_estimate=COST,
        compiler_params=params(),
        name="normalize",
    )(embeddings)

    codes = jnp.sum(pairs * jnp.array([8, 1], jnp.int32), axis=-1)
    table = jnp.pad(codes, ((0, 8 - shifts), (0, 128 - codes.shape[1]))) + jnp.pad(
        count[None], ((COUNTS, 7 - COUNTS), (0, 128 - shifts))
    )

    def turned(x, bits):
        return lax.ppermute(x, "owner", [(o, o ^ bits) for o in range(OWNERS)])

    came, unit = lax.optimization_barrier((turned(table, 1), unit))
    sib = to_sibling(unit)
    tables = jnp.concatenate([table, came], axis=0)
    tables = [tables] + [turned(tables, bits) for bits in (2, 4, 6)]

    plan, tables, chosen = pl.pallas_call(
        plan_kernel,
        in_specs=[SMEM] + [VMEM] * 4,
        out_specs=(SMEM, SMEM, SMEM),
        out_shape=(
            jax.ShapeDtypeStruct((PLAN,), jnp.int32),
            jax.ShapeDtypeStruct((OWNERS * 8, 128), jnp.int32),
            jax.ShapeDtypeStruct((1,), jnp.int32),
        ),
        scratch_shapes=[pltpu.SemaphoreType.DMA((4,))],
        compiler_params=params(),
        name="plan",
    )(pos, *tables)

    centered, log_density = lax.switch(
        chosen[0],
        [functools.partial(exchange_and_score, size) for size in SIZES],
        pos, plan, tables, surplus_pairs[0, 0], unit, sib,
    )
    return centered, log_density.reshape(rows)


def solution(mesh):
    return jax.shard_map(
        shards,
        mesh=mesh,
        in_specs=(
            P(("group", "owner"), None),
            P("group", "owner", None, None, None),
            P("group", "owner", None),
            P("group", "owner", None, None),
        ),
        out_specs=(P(("group", "owner"), None), P(("group", "owner"))),
        check_vma=False,
    )
```

```python
import functools

import jax
import jax.numpy as jnp
from jax import lax
from jax.experimental import pallas as pl
from jax.experimental.pallas import tpu as pltpu
from jax.sharding import PartitionSpec as P

BLOCK = 128
BPD = 8
CHIPS = 4
OWNERS = 8
BLOCKS = OWNERS * BPD
ON_CHIP = 2 * BPD
sharpness = 4.0
epsilon = 1e-06
SIZES = (5, 6, 8, 16)


def heads_of(size):
    return (2, size - 4) if size <= 6 else (size // 2, 0)


OWN_STEP = 2
COUNTS = 5

STRIDE = 32
F_COUNT, D_COUNT, LOAD, SIZE, NEED, TOUCHED, FAR, F_LIST, D_LIST = 0, 8, 16, 24, 32, 96, 161, 256, 512
PLAN = 768
TASKS, TASK, PLACE = 0, 16, 1040
ROW = 64
PLACES = 1152


def loop(count, body):
    def step(i, carry):
        body(i)
        return carry

    lax.fori_loop(0, count, step, 0)


def along_chips(x, hops):
    route = [(o, ((o // 2 + hops) % CHIPS) * 2 + o % 2) for o in range(OWNERS)]
    return lax.ppermute(x, "owner", route)


def both_ways(x, flip):
    route = [(o, ((o // 2 + (1 if o % 2 == flip else -1)) % CHIPS) * 2 + o % 2) for o in range(OWNERS)]
    return lax.ppermute(x, "owner", route)


def to_sibling(x):
    return lax.ppermute(x, "owner", [(o, o ^ 1) for o in range(OWNERS)])


def normalize_kernel(x_ref, u_ref):
    wide = x_ref[...].astype(jnp.float32)
    mean = jnp.mean(wide * wide, axis=-1, keepdims=True)
    u_ref[...] = (wide * lax.rsqrt(mean + epsilon)).astype(jnp.bfloat16)


def rows_of(block):
    return pl.ds(pl.multiple_of(block * BLOCK, BLOCK), BLOCK)


def kernel_values(p, q):
    dots = lax.dot_general(p, q, (((1,), (1,)), ((), ())), preferred_element_type=jnp.float32)
    return jnp.exp(sharpness * (dots * (1.0 / q.shape[1]) - 1.0))


def add_terms(u_ref, q_ref, acc_ref, kacc_ref, mine, other):
    q = q_ref[rows_of(other), :]
    kernel = kernel_values(u_ref[rows_of(mine), :], q)
    kacc_ref[rows_of(mine), :] += kernel
    acc_ref[rows_of(mine), :] += jnp.dot(
        kernel.astype(jnp.bfloat16), q, preferred_element_type=jnp.float32
    )


def plan_kernel(pos_ref, t0, t1, t2, t3, plan_ref, tab_ref, class_ref, sems):
    copies = [
        pltpu.make_async_copy(t, tab_ref.at[i * 16 : (i + 1) * 16, :], sems.at[i])
        for i, t in enumerate((t0, t1, t2, t3))
    ]
    for copy in copies:
        copy.start()
    me = pos_ref[0]
    for i in range(8):
        plan_ref[LOAD + i] = 0
        plan_ref[F_COUNT + i] = 0
        plan_ref[D_COUNT + i] = 0
    for i in range(BLOCKS):
        plan_ref[NEED + i] = 0
    for copy in copies:
        copy.wait()

    def of_owner(o, touched):
        row = (o ^ me) * 8
        for s in range(1, 5):
            q = (o + s) & 7
            to_q, to_o = lax.shift_left(1, q >> 1), lax.shift_left(1, o >> 1)

            def of_pair(t, touched):
                pair = tab_ref[row + s, t]
                for block, chip in ((o * BPD + (pair >> 3), to_q), (q * BPD + (pair & 7), to_o)):
                    before = plan_ref[NEED + block]
                    plan_ref[NEED + block] = before | chip
                    plan_ref[TOUCHED + touched] = block
                    touched = touched + (before == 0).astype(jnp.int32)
                return touched

            touched = lax.fori_loop(0, tab_ref[row + COUNTS, s], of_pair, touched)
        return touched

    touched = lax.fori_loop(0, OWNERS, of_owner, 0)

    def needs(block):
        mask, chip = plan_ref[NEED + block], block >> 4
        bit = lambda hop: lax.shift_right_logical(mask, (chip + hop) & 3) & 1
        return chip, bit(1), bit(3), bit(2)

    def append(count, table, at, block, wanted):
        held = plan_ref[count + at]
        plan_ref[table + at * STRIDE + held] = block
        plan_ref[count + at] = held + wanted

    def one_hop(i, fars):
        block = plan_ref[TOUCHED + i]
        chip, up, down, far = needs(block)
        at = 2 * chip
        plan_ref[LOAD + at] = plan_ref[LOAD + at] + up
        plan_ref[LOAD + at + 1] = plan_ref[LOAD + at + 1] + down
        append(D_COUNT, D_LIST, at, block, up & (1 - far))
        append(D_COUNT, D_LIST, at + 1, block, down & (1 - far))
        plan_ref[FAR + fars] = block
        return fars + far

    fars = lax.fori_loop(0, touched, one_hop, 0)

    @functools.partial(loop, fars)
    def _(i):
        block = plan_ref[FAR + i]
        chip, up, down, _ = needs(block)
        costs, loads = [], []
        for way, near, hop in ((0, up, 1), (1, down, 3)):
            at, after = 2 * chip + way, 2 * ((chip + hop) & 3) + way
            here, there = plan_ref[LOAD + at] + 1 - near, plan_ref[LOAD + after] + 1
            most = jnp.maximum(jnp.maximum(here, there), 2 * plan_ref[F_COUNT + at] + 2)
            costs.append(most * 64 + here + there + 32 * (1 - near))
            loads.append((at, after, here, there))
        goes_down = costs[0] > costs[1]
        at, after, here, there = (jnp.where(goes_down, b, a) for a, b in zip(*loads))
        plan_ref[LOAD + at] = here
        plan_ref[LOAD + after] = there
        append(F_COUNT, F_LIST, at, block, 1)
        append(D_COUNT, D_LIST, at ^ 1, block, jnp.where(goes_down, up, down))

    twice = [plan_ref[F_COUNT + i] for i in range(8)]
    once = [plan_ref[D_COUNT + i] for i in range(8)]
    longest = functools.reduce(jnp.maximum, twice)
    chosen, chosen_size = len(SIZES) - 1, SIZES[-1]
    for k in range(len(SIZES) - 2, -1, -1):
        size = SIZES[k]
        needs = []
        for i in range(8):
            before = (i + (6 if i % 2 == 0 else 2)) % 8
            needs.append(twice[before] + jnp.maximum(twice[i] + once[i] - size, 0))
        fits = jnp.maximum(longest, functools.reduce(jnp.maximum, needs)) <= size
        chosen = jnp.where(fits, k, chosen)
        chosen_size = jnp.where(fits, size, chosen_size)
    class_ref[0] = chosen
    plan_ref[SIZE] = chosen_size


def places_kernel(pos_ref, tab_ref, plan_ref, out_ref):
    me = pos_ref[0]
    y, core = me >> 1, me & 1
    size = plan_ref[SIZE]
    for i in range(16):
        out_ref[TASKS + i] = 0

    heads = jnp.where(size <= 6, 2, size >> 1)

    def put(block, stage, way, position):
        other = ((position + way) & 1) ^ core
        slot = position >> 1
        single = slot >= heads
        place = jnp.where(single, (2 + position - 2 * heads) * 256, way * 256 + slot) + 4 * 256 * other
        joined = 4 * 256 + jnp.where(single, position, way * heads + slot)
        place = jnp.where((stage == 0) & (other == 1), joined, place)
        out_ref[PLACE + block] = stage * 65536 + place

    for way in (0, 1):
        near = 2 * ((y + (3 if way == 0 else 1)) & 3) + way
        far = 2 * ((y + 2) & 3) + way
        twice, passing = plan_ref[F_COUNT + near], plan_ref[F_COUNT + far]

        @functools.partial(loop, twice)
        def _(i):
            put(plan_ref[F_LIST + near * STRIDE + i], 0, way, i)

        @functools.partial(loop, plan_ref[D_COUNT + near])
        def _(i):
            late = (twice + i >= size).astype(jnp.int32)
            put(plan_ref[D_LIST + near * STRIDE + i], late, way, twice + i + late * (passing - size))

        @functools.partial(loop, passing)
        def _(i):
            put(plan_ref[F_LIST + far * STRIDE + i], 1, way, i)

    def add_task(own, block):
        place = out_ref[PLACE + block]
        row = (place >> 16) * BPD + own
        count = out_ref[TASKS + row]
        out_ref[TASK + row * ROW + count] = place & 65535
        out_ref[TASKS + row] = count + 1

    for s in range(1, 5):
        above, below = (me + s) & 7, (me - s) & 7

        @pl.when((above >> 1) != y)
        def _():
            @functools.partial(loop, tab_ref[COUNTS, s])
            def _(t):
                pair = tab_ref[s, t]
                add_task(pair >> 3, above * BPD + (pair & 7))

        @pl.when((below >> 1) != y)
        def _():
            row = (below ^ me) * 8

            @functools.partial(loop, tab_ref[row + COUNTS, s])
            def _(t):
                pair = tab_ref[row + s, t]
                add_task(pair & 7, below * BPD + (pair >> 3))


def start_from(id_, core, unit_ref, sib_ref, dst, sem):
    here = rows_of(id_ & 7)
    mine = ((id_ >> 3) & 1) == core

    @pl.when(mine)
    def _():
        pltpu.make_async_copy(unit_ref.at[here, :], dst, sem).start()

    @pl.when(jnp.logical_not(mine))
    def _():
        pltpu.make_async_copy(sib_ref.at[here, :], dst, sem).start()


def listed(plan_ref, row, i, chip):
    twice, once = plan_ref[F_COUNT + row], plan_ref[D_COUNT + row]
    from_f = plan_ref[F_LIST + row * STRIDE + jnp.clip(i, 0, 15)]
    from_d = plan_ref[D_LIST + row * STRIDE + jnp.clip(i - twice, 0, 15)]
    found = jnp.where(i < twice, from_f, from_d)
    return jnp.where(i < twice + once, found, chip * ON_CHIP)


def slots_of(size, core):
    heads, singles = heads_of(size)
    slots = [(way, j, way, 2 * j + (core ^ way)) for way in (0, 1) for j in range(heads)]
    return slots + [(2 + k, 0, core ^ k, 2 * heads + k) for k in range(singles)]


def place_ref(ref, j):
    return ref.at[j * BLOCK : (j + 1) * BLOCK, :]


def first_pack_kernel(size, pos_ref, plan_ref, unit_ref, sib_ref, *refs):
    pieces, sems = refs[:-1], refs[-1]
    y, core = pos_ref[0] >> 1, pos_ref[0] & 1
    for n, (piece, j, way, position) in enumerate(slots_of(size, core)):
        block = listed(plan_ref, 2 * y + way, position, y)
        start_from(block, core, unit_ref, sib_ref, place_ref(pieces[piece], j), sems.at[n])
    for n, (piece, j, _, _) in enumerate(slots_of(size, core)):
        pltpu.make_async_copy(place_ref(unit_ref, 0), place_ref(pieces[piece], j), sems.at[n]).wait()


def second_pack_kernel(size, pos_ref, plan_ref, unit_ref, sib_ref, *refs):
    count = 2 + heads_of(size)[1]
    got, pieces, joined, sems = refs[:count], refs[count:-2], refs[-2], refs[-1]
    joins, row = [], 0
    for n, piece in enumerate(got):
        rows = piece.shape[0]
        joins.append(pltpu.make_async_copy(piece, joined.at[row : row + rows, :], sems.at[size + n]))
        row += rows
    y, core = pos_ref[0] >> 1, pos_ref[0] & 1
    for n, (piece, j, way, position) in enumerate(slots_of(size, core)):
        passing = plan_ref[F_COUNT + 2 * ((y + 3 + 2 * way) & 3) + way]
        dst = place_ref(pieces[piece], j)

        @pl.when(position < passing)
        def _():
            pltpu.make_async_copy(place_ref(got[piece], j), dst, sems.at[n]).start()

        @pl.when(position >= passing)
        def _():
            block = listed(plan_ref, 2 * y + way, position - passing + size, y)
            start_from(block, core, unit_ref, sib_ref, dst, sems.at[n])

    for join in joins:
        join.start()
    for n, (piece, j, _, _) in enumerate(slots_of(size, core)):
        pltpu.make_async_copy(place_ref(unit_ref, 0), place_ref(pieces[piece], j), sems.at[n]).wait()
    for join in joins:
        join.wait()


def own_kernel(pos_ref, tab_ref, surplus_ref, u_ref, sib_ref, acc_ref, kacc_ref, live_ref):
    core = pos_ref[0] & 1

    @functools.partial(loop, BPD * BPD)
    def _(i):
        live_ref[i] = 0.0

    def mark(a, b):
        live_ref[a * BPD + b] = 1.0
        live_ref[b * BPD + a] = 1.0

    @functools.partial(loop, tab_ref[COUNTS, 0])
    def _(t):
        pair = tab_ref[0, t]
        mark(pair >> 3, pair & 7)

    @functools.partial(loop, surplus_ref.shape[0])
    def _(t):
        @pl.when(surplus_ref[t, 2] == 1)
        def _():
            mark(surplus_ref[t, 0], surplus_ref[t, 1])

    step = OWN_STEP

    @functools.partial(loop, BPD // step)
    def _(part):
        here = pl.ds(pl.multiple_of(part * step * BLOCK, step * BLOCK), step * BLOCK)
        kernel = kernel_values(u_ref[here, :], u_ref[...])
        rows = []
        for i in range(step):
            parts = [
                kernel[i * BLOCK : (i + 1) * BLOCK, j * BLOCK : (j + 1) * BLOCK]
                * live_ref[(part * step + i) * BPD + j]
                for j in range(BPD)
            ]
            kacc_ref[rows_of(part * step + i), :] = sum(parts)
            rows.append(jnp.concatenate(parts, axis=1).astype(jnp.bfloat16))
        acc_ref[here, :] = jnp.dot(
            jnp.concatenate(rows, axis=0), u_ref[...], preferred_element_type=jnp.float32
        )

    @functools.partial(loop, tab_ref[core * 8 + COUNTS, 1])
    def _(t):
        pair = tab_ref[core * 8 + 1, t]
        a, b = pair >> 3, pair & 7
        mine, other = jnp.where(core == 0, a, b), jnp.where(core == 0, b, a)
        add_terms(u_ref, sib_ref, acc_ref, kacc_ref, mine, other)


def each_task(stage, task_ref, own, pieces, q_ref, body):
    row = stage * BPD + own

    @functools.partial(loop, task_ref[TASKS + row])
    def _(t):
        place = task_ref[TASK + row * ROW + t]
        for n, piece in pieces:

            @pl.when((place >> 8) == n)
            def _():
                q_ref[...] = piece[rows_of(place & 255), :]

        body(q_ref[...])


def numbered(here, there):
    return [*enumerate(here), *enumerate(there, 4)]


def first_part_kernel(task_ref, u_ref, acc_in, kacc_in, *refs):
    pieces, (acc_ref, kacc_ref, q_ref) = numbered(refs[:-4], refs[-4:-3]), refs[-3:]
    acc_ref[...] = acc_in[...]
    kacc_ref[...] = kacc_in[...]

    @functools.partial(loop, BPD)
    def _(own):
        here = rows_of(own)

        def add(q):
            kernel = kernel_values(u_ref[here, :], q)
            kacc_ref[here, :] += kernel
            acc_ref[here, :] += jnp.dot(kernel.astype(jnp.bfloat16), q, preferred_element_type=jnp.float32)

        each_task(0, task_ref, own, pieces, q_ref, add)


def last_kernel(task_ref, u_ref, acc_in, kacc_in, *refs):
    got, (out_ref, log_ref, acc_ref, kacc_ref, q_ref, done_ref, sems) = refs[:-7], refs[-7:]
    pieces = numbered(got[: len(got) // 2], got[len(got) // 2 :])
    rows = lax.broadcasted_iota(jnp.int32, (BLOCK, BLOCK), 0)
    diagonal = rows == lax.broadcasted_iota(jnp.int32, (BLOCK, BLOCK), 1)

    def out_copy(own):
        here = rows_of(own)
        return pltpu.make_async_copy(done_ref.at[here, :], out_ref.at[here, :], sems.at[own])

    @functools.partial(loop, BPD)
    def _(own):
        here = rows_of(own)
        acc_ref[...] = acc_in[here, :]
        kacc_ref[...] = kacc_in[here, :]

        def add(q):
            kernel = kernel_values(u_ref[here, :], q)
            kacc_ref[...] += kernel
            acc_ref[...] += jnp.dot(kernel.astype(jnp.bfloat16), q, preferred_element_type=jnp.float32)

        each_task(1, task_ref, own, pieces, q_ref, add)
        density = jnp.sum(kacc_ref[...], axis=1, keepdims=True)
        done_ref[here, :] = (
            u_ref[here, :].astype(jnp.float32) - acc_ref[...] * (1.0 / density)
        ).astype(jnp.bfloat16)
        out_copy(own).start()
        across = jnp.sum(jnp.where(diagonal, density, 0.0), axis=0, keepdims=True)
        log_ref[pl.ds(own, 1), :] = jnp.log(across)

    for own in range(BPD):
        out_copy(own).wait()


SMEM = pl.BlockSpec(memory_space=pltpu.SMEM)
VMEM = pl.BlockSpec(memory_space=pltpu.VMEM)
ANY = pl.BlockSpec(memory_space=pl.ANY)
HBM = pl.BlockSpec(memory_space=pltpu.HBM)


def params():
    return pltpu.CompilerParams(vmem_limit_bytes=26 * 2**20)


COST = pl.CostEstimate(flops=1, bytes_accessed=1, transcendentals=0)


def pieces_of(size, width):
    heads, singles = heads_of(size)
    counts = [heads] * 2 + [1] * singles
    return tuple(jax.ShapeDtypeStruct((count * BLOCK, width), jnp.bfloat16) for count in counts)


def send(pieces):
    moved = [along_chips(pieces[0], 1), along_chips(pieces[1], -1)]
    return moved + [both_ways(x, flip) for flip, x in enumerate(pieces[2:])]


def pack(kernel, name, size, more, *operands):
    out = pieces_of(size, operands[2].shape[1]) + more
    return pl.pallas_call(
        functools.partial(kernel, size),
        in_specs=[SMEM, SMEM, HBM, HBM] + [ANY] * (len(operands) - 4),
        out_specs=(VMEM,) * len(out),
        out_shape=out,
        scratch_shapes=[pltpu.SemaphoreType.DMA((size + 4,))],
        compiler_params=params(),
        name=name,
    )(*operands)


def exchange_and_score(size, packed, pos, plan, tables, surplus, unit, sib):
    rows, width = unit.shape
    sums = (
        jax.ShapeDtypeStruct((rows, width), jnp.float32),
        jax.ShapeDtypeStruct((rows, BLOCK), jnp.float32),
    )

    if size > 6:
        packed = pack(first_pack_kernel, "first_pack", size, (), pos, plan, unit, sib)
    got = send(packed[: 2 + heads_of(size)[1]])
    places = pl.pallas_call(
        places_kernel,
        in_specs=[SMEM, SMEM, SMEM],
        out_specs=SMEM,
        out_shape=jax.ShapeDtypeStruct((PLACES,), jnp.int32),
        cost_estimate=COST,
        compiler_params=params(),
        name="places",
    )(pos, tables, plan)
    acc, kacc = pl.pallas_call(
        own_kernel,
        in_specs=[SMEM, SMEM, SMEM, VMEM, VMEM],
        out_specs=(VMEM, VMEM),
        out_shape=sums,
        scratch_shapes=[pltpu.SMEM((BPD * BPD,), jnp.float32)],
        compiler_params=params(),
        cost_estimate=COST,
        name="own_pairs",
    )(pos, tables, surplus, unit, sib)
    *got, acc, places = lax.optimization_barrier((*got, acc, places))
    joined = (jax.ShapeDtypeStruct((size * BLOCK, width), jnp.bfloat16),)
    *passed_on, joined = pack(second_pack_kernel, "second_pack", size, joined, pos, plan, unit, sib, *got)
    far = send(passed_on)
    acc, kacc = pl.pallas_call(
        first_part_kernel,
        in_specs=[SMEM] + [VMEM] * (4 + len(got)),
        out_specs=(VMEM, VMEM),
        out_shape=sums,
        scratch_shapes=[pltpu.VMEM((BLOCK, width), jnp.bfloat16)],
        compiler_params=params(),
        cost_estimate=COST,
        name="first_part",
    )(places, unit, acc, kacc, *got, to_sibling(joined))
    *far, acc = lax.optimization_barrier((*far, acc))
    sib_far = [to_sibling(x) for x in far]
    return pl.pallas_call(
        last_kernel,
        in_specs=[SMEM] + [VMEM] * (3 + 2 * len(far)),
        out_specs=(ANY, VMEM),
        out_shape=(
            jax.ShapeDtypeStruct((rows, width), jnp.bfloat16),
            jax.ShapeDtypeStruct((BPD, BLOCK), jnp.float32),
        ),
        scratch_shapes=[
            pltpu.VMEM((BLOCK, width), jnp.float32),
            pltpu.VMEM((BLOCK, BLOCK), jnp.float32),
            pltpu.VMEM((BLOCK, width), jnp.bfloat16),
            pltpu.VMEM((rows, width), jnp.bfloat16),
            pltpu.SemaphoreType.DMA((BPD,)),
        ],
        compiler_params=params(),
        cost_estimate=COST,
        name="last_part",
    )(places, unit, acc, kacc, *far, *sib_far)


def shards(embeddings, home_pairs, home_count, surplus_pairs):
    rows, width = embeddings.shape
    pairs, count = home_pairs[0, 0], home_count[0, 0]
    shifts = pairs.shape[0]
    pos = lax.axis_index("owner").astype(jnp.int32).reshape(1)

    step = 128
    unit = pl.pallas_call(
        normalize_kernel,
        grid=(rows // step,),
        in_specs=[pl.BlockSpec((step, width), lambda i: (i, 0))],
        out_specs=pl.BlockSpec((step, width), lambda i: (i, 0)),
        out_shape=pltpu.HBM(embeddings.shape, jnp.bfloat16),
        cost_estimate=COST,
        compiler_params=params(),
        name="normalize",
    )(embeddings)

    codes = jnp.sum(pairs * jnp.array([8, 1], jnp.int32), axis=-1)
    table = jnp.pad(codes, ((0, 8 - shifts), (0, 128 - codes.shape[1]))) + jnp.pad(
        count[None], ((COUNTS, 7 - COUNTS), (0, 128 - shifts))
    )

    def turned(x, bits):
        return lax.ppermute(x, "owner", [(o, o ^ bits) for o in range(OWNERS)])

    came, unit = lax.optimization_barrier((turned(table, 1), unit))
    sib = to_sibling(unit)
    tables = jnp.concatenate([table, came], axis=0)
    tables = [tables] + [turned(tables, bits) for bits in (2, 4, 6)]

    plan, tables, chosen = pl.pallas_call(
        plan_kernel,
        in_specs=[SMEM] + [VMEM] * 4,
        out_specs=(SMEM, SMEM, SMEM),
        out_shape=(
            jax.ShapeDtypeStruct((PLAN,), jnp.int32),
            jax.ShapeDtypeStruct((OWNERS * 8, 128), jnp.int32),
            jax.ShapeDtypeStruct((1,), jnp.int32),
        ),
        scratch_shapes=[pltpu.SemaphoreType.DMA((4,))],
        compiler_params=params(),
        name="plan",
    )(pos, *tables)

    packed = pack(first_pack_kernel, "first_pack", 6, (), pos, plan, unit, sib)
    centered, log_density = lax.switch(
        chosen[0],
        [functools.partial(exchange_and_score, size) for size in SIZES],
        packed, pos, plan, tables, surplus_pairs[0, 0], unit, sib,
    )
    return centered, log_density.reshape(rows)


def solution(mesh):
    return jax.shard_map(
        shards,
        mesh=mesh,
        in_specs=(
            P(("group", "owner"), None),
            P("group", "owner", None, None, None),
            P("group", "owner", None),
            P("group", "owner", None, None),
        ),
        out_specs=(P(("group", "owner"), None), P(("group", "owner"))),
        check_vma=False,
    )
```

```python
import functools

import jax
import jax.numpy as jnp
from jax import lax
from jax.experimental import pallas as pl
from jax.experimental.pallas import tpu as pltpu
from jax.sharding import PartitionSpec as P

BLOCK = 128
BPD = 8
CHIPS = 4
OWNERS = 8
BLOCKS = OWNERS * BPD
ON_CHIP = 2 * BPD
sharpness = 4.0
epsilon = 1e-06
SIZES = (5, 6, 8, 16)


def heads_of(size):
    return (2, size - 4) if size <= 6 else (size // 2, 0)


OWN_STEP = 2
COUNTS = 5

STRIDE = 32
F_COUNT, D_COUNT, LOAD, SIZE, NEED, TOUCHED, FAR, F_LIST, D_LIST = 0, 8, 16, 24, 32, 96, 161, 256, 512
PLAN = 768
TASKS, TASK, PLACE = 0, 24, 1560
ROW = 64
PLACES = 1664


def loop(count, body):
    def step(i, carry):
        body(i)
        return carry

    lax.fori_loop(0, count, step, 0)


def along_chips(x, hops):
    route = [(o, ((o // 2 + hops) % CHIPS) * 2 + o % 2) for o in range(OWNERS)]
    return lax.ppermute(x, "owner", route)


def both_ways(x, flip):
    route = [(o, ((o // 2 + (1 if o % 2 == flip else -1)) % CHIPS) * 2 + o % 2) for o in range(OWNERS)]
    return lax.ppermute(x, "owner", route)


def to_sibling(x):
    return lax.ppermute(x, "owner", [(o, o ^ 1) for o in range(OWNERS)])


def normalize_kernel(x_ref, u_ref):
    wide = x_ref[...].astype(jnp.float32)
    mean = jnp.mean(wide * wide, axis=-1, keepdims=True)
    u_ref[...] = (wide * lax.rsqrt(mean + epsilon)).astype(jnp.bfloat16)


def rows_of(block):
    return pl.ds(pl.multiple_of(block * BLOCK, BLOCK), BLOCK)


def kernel_values(p, q):
    dots = lax.dot_general(p, q, (((1,), (1,)), ((), ())), preferred_element_type=jnp.float32)
    return jnp.exp(sharpness * (dots * (1.0 / q.shape[1]) - 1.0))


def add_terms(u_ref, q_ref, acc_ref, kacc_ref, mine, other):
    q = q_ref[rows_of(other), :]
    kernel = kernel_values(u_ref[rows_of(mine), :], q)
    kacc_ref[rows_of(mine), :] += kernel
    acc_ref[rows_of(mine), :] += jnp.dot(
        kernel.astype(jnp.bfloat16), q, preferred_element_type=jnp.float32
    )


def gather_tables(tables, tab_ref, sems):
    return [
        pltpu.make_async_copy(t, tab_ref.at[i * 16 : (i + 1) * 16, :], sems.at[i])
        for i, t in enumerate(tables)
    ]


def plan_kernel(pos_ref, t0, t1, t2, t3, plan_ref, class_ref, tab_ref, sems):
    copies = gather_tables((t0, t1, t2, t3), tab_ref, sems)
    for copy in copies:
        copy.start()
    me = pos_ref[0]
    for i in range(8):
        plan_ref[LOAD + i] = 0
        plan_ref[F_COUNT + i] = 0
        plan_ref[D_COUNT + i] = 0
    for i in range(BLOCKS):
        plan_ref[NEED + i] = 0
    for copy in copies:
        copy.wait()

    def of_owner(o, touched):
        row = (o ^ me) * 8
        for s in range(1, 5):
            q = (o + s) & 7
            to_q, to_o = lax.shift_left(1, q >> 1), lax.shift_left(1, o >> 1)

            def of_pair(t, touched):
                pair = tab_ref[row + s, t]
                for block, chip in ((o * BPD + (pair >> 3), to_q), (q * BPD + (pair & 7), to_o)):
                    before = plan_ref[NEED + block]
                    plan_ref[NEED + block] = before | chip
                    plan_ref[TOUCHED + touched] = block
                    touched = touched + (before == 0).astype(jnp.int32)
                return touched

            touched = lax.fori_loop(0, tab_ref[row + COUNTS, s], of_pair, touched)
        return touched

    touched = lax.fori_loop(0, OWNERS, of_owner, 0)

    def needs(block):
        mask, chip = plan_ref[NEED + block], block >> 4
        bit = lambda hop: lax.shift_right_logical(mask, (chip + hop) & 3) & 1
        return chip, bit(1), bit(3), bit(2)

    def append(count, table, at, block, wanted):
        held = plan_ref[count + at]
        plan_ref[table + at * STRIDE + held] = block
        plan_ref[count + at] = held + wanted

    def one_hop(i, fars):
        block = plan_ref[TOUCHED + i]
        chip, up, down, far = needs(block)
        at = 2 * chip
        plan_ref[LOAD + at] = plan_ref[LOAD + at] + up
        plan_ref[LOAD + at + 1] = plan_ref[LOAD + at + 1] + down
        append(D_COUNT, D_LIST, at, block, up & (1 - far))
        append(D_COUNT, D_LIST, at + 1, block, down & (1 - far))
        plan_ref[FAR + fars] = block
        return fars + far

    fars = lax.fori_loop(0, touched, one_hop, 0)

    @functools.partial(loop, fars)
    def _(i):
        block = plan_ref[FAR + i]
        chip, up, down, _ = needs(block)
        costs, loads = [], []
        for way, near, hop in ((0, up, 1), (1, down, 3)):
            at, after = 2 * chip + way, 2 * ((chip + hop) & 3) + way
            here, there = plan_ref[LOAD + at] + 1 - near, plan_ref[LOAD + after] + 1
            most = jnp.maximum(jnp.maximum(here, there), 2 * plan_ref[F_COUNT + at] + 2)
            costs.append(most * 64 + here + there + 32 * (1 - near))
            loads.append((at, after, here, there))
        goes_down = costs[0] > costs[1]
        at, after, here, there = (jnp.where(goes_down, b, a) for a, b in zip(*loads))
        plan_ref[LOAD + at] = here
        plan_ref[LOAD + after] = there
        append(F_COUNT, F_LIST, at, block, 1)
        append(D_COUNT, D_LIST, at ^ 1, block, jnp.where(goes_down, up, down))

    twice = [plan_ref[F_COUNT + i] for i in range(8)]
    once = [plan_ref[D_COUNT + i] for i in range(8)]
    longest = functools.reduce(jnp.maximum, twice)
    chosen, chosen_size = len(SIZES) - 1, SIZES[-1]
    for k in range(len(SIZES) - 2, -1, -1):
        size = SIZES[k]
        needs = []
        for i in range(8):
            before = (i + (6 if i % 2 == 0 else 2)) % 8
            needs.append(twice[before] + jnp.maximum(twice[i] + once[i] - size, 0))
        fits = jnp.maximum(longest, functools.reduce(jnp.maximum, needs)) <= size
        chosen = jnp.where(fits, k, chosen)
        chosen_size = jnp.where(fits, size, chosen_size)
    class_ref[0] = chosen
    plan_ref[SIZE] = chosen_size


def places_kernel(pos_ref, plan_ref, t0, t1, t2, t3, out_ref, tab_ref, sems):
    copies = gather_tables((t0, t1, t2, t3), tab_ref, sems)
    for copy in copies:
        copy.start()
    for copy in copies:
        copy.wait()
    me = pos_ref[0]
    y, core = me >> 1, me & 1
    size = plan_ref[SIZE]
    for i in range(24):
        out_ref[TASKS + i] = 0

    heads = jnp.where(size <= 6, 2, size >> 1)

    def put(block, stage, way, position):
        other = ((position + way) & 1) ^ core
        slot = position >> 1
        single = slot >= heads
        place = jnp.where(single, (2 + position - 2 * heads) * 256, way * 256 + slot) + 4 * 256 * other
        joined = 4 * 256 + jnp.where(single, position, way * heads + slot)
        place = jnp.where((stage == 0) & (other == 1), joined, place)
        out_ref[PLACE + block] = stage * (1 + other) * 65536 + place

    for way in (0, 1):
        near = 2 * ((y + (3 if way == 0 else 1)) & 3) + way
        far = 2 * ((y + 2) & 3) + way
        twice, passing = plan_ref[F_COUNT + near], plan_ref[F_COUNT + far]

        @functools.partial(loop, twice)
        def _(i):
            put(plan_ref[F_LIST + near * STRIDE + i], 0, way, i)

        @functools.partial(loop, plan_ref[D_COUNT + near])
        def _(i):
            late = (twice + i >= size).astype(jnp.int32)
            put(plan_ref[D_LIST + near * STRIDE + i], late, way, twice + i + late * (passing - size))

        @functools.partial(loop, passing)
        def _(i):
            put(plan_ref[F_LIST + far * STRIDE + i], 1, way, i)

    def add_task(own, block):
        place = out_ref[PLACE + block]
        row = (place >> 16) * BPD + own
        count = out_ref[TASKS + row]
        out_ref[TASK + row * ROW + count] = place & 65535
        out_ref[TASKS + row] = count + 1

    for s in range(1, 5):
        above, below = (me + s) & 7, (me - s) & 7

        @pl.when((above >> 1) != y)
        def _():
            @functools.partial(loop, tab_ref[COUNTS, s])
            def _(t):
                pair = tab_ref[s, t]
                add_task(pair >> 3, above * BPD + (pair & 7))

        @pl.when((below >> 1) != y)
        def _():
            row = (below ^ me) * 8

            @functools.partial(loop, tab_ref[row + COUNTS, s])
            def _(t):
                pair = tab_ref[row + s, t]
                add_task(pair & 7, below * BPD + (pair >> 3))


def start_from(id_, core, unit_ref, sib_ref, dst, sem):
    here = rows_of(id_ & 7)
    mine = ((id_ >> 3) & 1) == core

    @pl.when(mine)
    def _():
        pltpu.make_async_copy(unit_ref.at[here, :], dst, sem).start()

    @pl.when(jnp.logical_not(mine))
    def _():
        pltpu.make_async_copy(sib_ref.at[here, :], dst, sem).start()


def listed(plan_ref, row, i, chip):
    twice, once = plan_ref[F_COUNT + row], plan_ref[D_COUNT + row]
    from_f = plan_ref[F_LIST + row * STRIDE + jnp.clip(i, 0, 15)]
    from_d = plan_ref[D_LIST + row * STRIDE + jnp.clip(i - twice, 0, 15)]
    found = jnp.where(i < twice, from_f, from_d)
    return jnp.where(i < twice + once, found, chip * ON_CHIP)


def slots_of(size, core):
    heads, singles = heads_of(size)
    slots = [(way, j, way, 2 * j + (core ^ way)) for way in (0, 1) for j in range(heads)]
    return slots + [(2 + k, 0, core ^ k, 2 * heads + k) for k in range(singles)]


def place_ref(ref, j):
    return ref.at[j * BLOCK : (j + 1) * BLOCK, :]


def first_pack_kernel(size, pos_ref, plan_ref, unit_ref, sib_ref, *refs):
    pieces, sems = refs[:-1], refs[-1]
    y, core = pos_ref[0] >> 1, pos_ref[0] & 1
    for n, (piece, j, way, position) in enumerate(slots_of(size, core)):
        block = listed(plan_ref, 2 * y + way, position, y)
        start_from(block, core, unit_ref, sib_ref, place_ref(pieces[piece], j), sems.at[n])
    for n, (piece, j, _, _) in enumerate(slots_of(size, core)):
        pltpu.make_async_copy(place_ref(unit_ref, 0), place_ref(pieces[piece], j), sems.at[n]).wait()


def second_pack_kernel(size, lo, hi, join, pos_ref, plan_ref, unit_ref, sib_ref, *refs):
    sems = refs[-1]
    joined, refs = (refs[-2], refs[:-2]) if join else (None, refs[:-1])
    got, pieces = refs[: len(refs) - (hi - lo)], refs[len(refs) - (hi - lo) :]
    joins, row = [], 0
    if join:
        for n, piece in enumerate(got):
            rows = piece.shape[0]
            joins.append(pltpu.make_async_copy(piece, joined.at[row : row + rows, :], sems.at[size + n]))
            row += rows
        got = got[lo:]
    y, core = pos_ref[0] >> 1, pos_ref[0] & 1
    slots = [slot for slot in slots_of(size, core) if lo <= slot[0] < hi]
    for n, (piece, j, way, position) in enumerate(slots):
        passing = plan_ref[F_COUNT + 2 * ((y + 3 + 2 * way) & 3) + way]
        dst = place_ref(pieces[piece - lo], j)

        @pl.when(position < passing)
        def _():
            pltpu.make_async_copy(place_ref(got[piece - lo], j), dst, sems.at[n]).start()

        @pl.when(position >= passing)
        def _():
            block = listed(plan_ref, 2 * y + way, position - passing + size, y)
            start_from(block, core, unit_ref, sib_ref, dst, sems.at[n])

    for copy in joins:
        copy.start()
    for n, (piece, j, _, _) in enumerate(slots):
        pltpu.make_async_copy(place_ref(unit_ref, 0), place_ref(pieces[piece - lo], j), sems.at[n]).wait()
    for copy in joins:
        copy.wait()


def own_kernel(pos_ref, tab_ref, surplus_ref, u_ref, sib_ref, acc_ref, kacc_ref, live_ref):
    core = pos_ref[0] & 1

    @functools.partial(loop, BPD * BPD)
    def _(i):
        live_ref[i] = 0.0

    def mark(a, b):
        live_ref[a * BPD + b] = 1.0
        live_ref[b * BPD + a] = 1.0

    @functools.partial(loop, tab_ref[COUNTS, 0])
    def _(t):
        pair = tab_ref[0, t]
        mark(pair >> 3, pair & 7)

    @functools.partial(loop, surplus_ref.shape[0])
    def _(t):
        @pl.when(surplus_ref[t, 2] == 1)
        def _():
            mark(surplus_ref[t, 0], surplus_ref[t, 1])

    step = OWN_STEP

    @functools.partial(loop, BPD // step)
    def _(part):
        here = pl.ds(pl.multiple_of(part * step * BLOCK, step * BLOCK), step * BLOCK)
        kernel = kernel_values(u_ref[here, :], u_ref[...])
        rows = []
        for i in range(step):
            parts = [
                kernel[i * BLOCK : (i + 1) * BLOCK, j * BLOCK : (j + 1) * BLOCK]
                * live_ref[(part * step + i) * BPD + j]
                for j in range(BPD)
            ]
            kacc_ref[rows_of(part * step + i), :] = sum(parts)
            rows.append(jnp.concatenate(parts, axis=1).astype(jnp.bfloat16))
        acc_ref[here, :] = jnp.dot(
            jnp.concatenate(rows, axis=0), u_ref[...], preferred_element_type=jnp.float32
        )

    @functools.partial(loop, tab_ref[core * 8 + COUNTS, 1])
    def _(t):
        pair = tab_ref[core * 8 + 1, t]
        a, b = pair >> 3, pair & 7
        mine, other = jnp.where(core == 0, a, b), jnp.where(core == 0, b, a)
        add_terms(u_ref, sib_ref, acc_ref, kacc_ref, mine, other)


def each_task(part, task_ref, own, pieces, q_ref, body):
    row = part * BPD + own

    @functools.partial(loop, task_ref[TASKS + row])
    def _(t):
        place = task_ref[TASK + row * ROW + t]
        for n, piece in pieces:

            @pl.when((place >> 8) == n)
            def _():
                q_ref[...] = piece[rows_of(place & 255), :]

        body(q_ref[...])


def numbered(here, there):
    return [*enumerate(here), *enumerate(there, 4)]


def part_kernel(part, here, task_ref, u_ref, acc_in, kacc_in, *refs):
    pieces, (acc_ref, kacc_ref, q_ref) = numbered(refs[:here], refs[here:-3]), refs[-3:]
    acc_ref[...] = acc_in[...]
    kacc_ref[...] = kacc_in[...]

    @functools.partial(loop, BPD)
    def _(own):
        here = rows_of(own)

        def add(q):
            kernel = kernel_values(u_ref[here, :], q)
            kacc_ref[here, :] += kernel
            acc_ref[here, :] += jnp.dot(kernel.astype(jnp.bfloat16), q, preferred_element_type=jnp.float32)

        each_task(part, task_ref, own, pieces, q_ref, add)


def last_kernel(task_ref, u_ref, acc_in, kacc_in, *refs):
    got, (out_ref, log_ref, acc_ref, kacc_ref, q_ref, done_ref, sems) = refs[:-7], refs[-7:]
    pieces = numbered((), got)
    rows = lax.broadcasted_iota(jnp.int32, (BLOCK, BLOCK), 0)
    diagonal = rows == lax.broadcasted_iota(jnp.int32, (BLOCK, BLOCK), 1)

    def out_copy(own):
        here = rows_of(own)
        return pltpu.make_async_copy(done_ref.at[here, :], out_ref.at[here, :], sems.at[own])

    @functools.partial(loop, BPD)
    def _(own):
        here = rows_of(own)
        acc_ref[...] = acc_in[here, :]
        kacc_ref[...] = kacc_in[here, :]

        def add(q):
            kernel = kernel_values(u_ref[here, :], q)
            kacc_ref[...] += kernel
            acc_ref[...] += jnp.dot(kernel.astype(jnp.bfloat16), q, preferred_element_type=jnp.float32)

        each_task(2, task_ref, own, pieces, q_ref, add)
        density = jnp.sum(kacc_ref[...], axis=1, keepdims=True)
        done_ref[here, :] = (
            u_ref[here, :].astype(jnp.float32) - acc_ref[...] * (1.0 / density)
        ).astype(jnp.bfloat16)
        out_copy(own).start()
        across = jnp.sum(jnp.where(diagonal, density, 0.0), axis=0, keepdims=True)
        log_ref[pl.ds(own, 1), :] = jnp.log(across)

    for own in range(BPD):
        out_copy(own).wait()


SMEM = pl.BlockSpec(memory_space=pltpu.SMEM)
VMEM = pl.BlockSpec(memory_space=pltpu.VMEM)
ANY = pl.BlockSpec(memory_space=pl.ANY)


def params():
    return pltpu.CompilerParams(vmem_limit_bytes=26 * 2**20)


COST = pl.CostEstimate(flops=1, bytes_accessed=1, transcendentals=0)


def pieces_of(size, width):
    heads, singles = heads_of(size)
    counts = [heads] * 2 + [1] * singles
    return tuple(jax.ShapeDtypeStruct((count * BLOCK, width), jnp.bfloat16) for count in counts)


def send(pieces):
    moved = [along_chips(pieces[0], 1), along_chips(pieces[1], -1)]
    return moved + [both_ways(x, flip) for flip, x in enumerate(pieces[2:])]


def pack(kernel, name, size, out, *operands):
    return pl.pallas_call(
        kernel,
        in_specs=[SMEM, SMEM] + [ANY] * (len(operands) - 2),
        out_specs=(VMEM,) * len(out),
        out_shape=out,
        scratch_shapes=[pltpu.SemaphoreType.DMA((size + 4,))],
        compiler_params=params(),
        name=name,
    )(*operands)


def first_pack(size, pos, plan, unit, sib):
    out = pieces_of(size, unit.shape[1])
    return pack(functools.partial(first_pack_kernel, size), "first_pack", size, out, pos, plan, unit, sib)


def exchange_and_score(size, packed, pos, plan, tables, surplus, unit, sib):
    rows, width = unit.shape
    sums = (
        jax.ShapeDtypeStruct((rows, width), jnp.float32),
        jax.ShapeDtypeStruct((rows, BLOCK), jnp.float32),
    )

    if size > 6:
        packed = first_pack(size, pos, plan, unit, sib)
    got = send(packed[: 2 + heads_of(size)[1]])
    places = pl.pallas_call(
        places_kernel,
        in_specs=[SMEM, SMEM] + [VMEM] * 4,
        out_specs=SMEM,
        out_shape=jax.ShapeDtypeStruct((PLACES,), jnp.int32),
        scratch_shapes=[pltpu.SMEM((OWNERS * 8, 128), jnp.int32), pltpu.SemaphoreType.DMA((4,))],
        cost_estimate=COST,
        compiler_params=params(),
        name="places",
    )(pos, plan, *tables)
    acc, kacc = pl.pallas_call(
        own_kernel,
        in_specs=[SMEM, SMEM, SMEM, VMEM, VMEM],
        out_specs=(VMEM, VMEM),
        out_shape=sums,
        scratch_shapes=[pltpu.SMEM((BPD * BPD,), jnp.float32)],
        compiler_params=params(),
        cost_estimate=COST,
        name="own_pairs",
    )(pos, tables[0], surplus, unit, sib)
    heads, singles = heads_of(size)
    out = pieces_of(size, width)
    joined = (jax.ShapeDtypeStruct((size * BLOCK, width), jnp.bfloat16),)

    def pass_on(lo, hi, join, got):
        kernel = functools.partial(second_pack_kernel, size, lo, hi, join)
        more = joined if join else ()
        return pack(kernel, "second_pack", size, out[lo:hi] + more, pos, plan, unit, sib, *got)

    got[0], got[1], acc, places = lax.optimization_barrier((got[0], got[1], acc, places))
    sent = pass_on(0, 2, not singles, got[:2])
    far = [along_chips(sent[0], 1), along_chips(sent[1], -1)]
    if singles:
        *late, got[0], got[1], _ = lax.optimization_barrier((*got[2:], *got[:2], sent[0]))
        got[2:] = late
        sent = pass_on(2, 2 + singles, True, got)
        far += [both_ways(x, flip) for flip, x in enumerate(sent[:-1])]
    joined = sent[-1]

    def add_part(part, acc, kacc, here, there):
        return pl.pallas_call(
            functools.partial(part_kernel, part, len(here)),
            in_specs=[SMEM] + [VMEM] * (3 + len(here) + len(there)),
            out_specs=(VMEM, VMEM),
            out_shape=sums,
            scratch_shapes=[pltpu.VMEM((BLOCK, width), jnp.bfloat16)],
            compiler_params=params(),
            cost_estimate=COST,
            name=f"part{part}",
        )(places, unit, acc, kacc, *here, *there)

    acc, kacc = add_part(0, acc, kacc, got, [to_sibling(joined)])
    *far, acc = lax.optimization_barrier((*far, acc))
    sib_far = [to_sibling(x) for x in far]
    acc, kacc = add_part(1, acc, kacc, far, [])
    *sib_far, acc = lax.optimization_barrier((*sib_far, acc))
    return pl.pallas_call(
        last_kernel,
        in_specs=[SMEM] + [VMEM] * (3 + len(far)),
        out_specs=(ANY, VMEM),
        out_shape=(
            jax.ShapeDtypeStruct((rows, width), jnp.bfloat16),
            jax.ShapeDtypeStruct((BPD, BLOCK), jnp.float32),
        ),
        scratch_shapes=[
            pltpu.VMEM((BLOCK, width), jnp.float32),
            pltpu.VMEM((BLOCK, BLOCK), jnp.float32),
            pltpu.VMEM((BLOCK, width), jnp.bfloat16),
            pltpu.VMEM((rows, width), jnp.bfloat16),
            pltpu.SemaphoreType.DMA((BPD,)),
        ],
        compiler_params=params(),
        cost_estimate=COST,
        name="last_part",
    )(places, unit, acc, kacc, *sib_far)


def shards(embeddings, home_pairs, home_count, surplus_pairs):
    rows, width = embeddings.shape
    pairs, count = home_pairs[0, 0], home_count[0, 0]
    shifts = pairs.shape[0]
    pos = lax.axis_index("owner").astype(jnp.int32).reshape(1)

    step = 128
    unit = pl.pallas_call(
        normalize_kernel,
        grid=(rows // step,),
        in_specs=[pl.BlockSpec((step, width), lambda i: (i, 0))],
        out_specs=pl.BlockSpec((step, width), lambda i: (i, 0)),
        out_shape=jax.ShapeDtypeStruct(embeddings.shape, jnp.bfloat16),
        cost_estimate=COST,
        compiler_params=params(),
        name="normalize",
    )(embeddings)

    codes = jnp.sum(pairs * jnp.array([8, 1], jnp.int32), axis=-1)
    table = jnp.pad(codes, ((0, 8 - shifts), (0, 128 - codes.shape[1]))) + jnp.pad(
        count[None], ((COUNTS, 7 - COUNTS), (0, 128 - shifts))
    )

    def turned(x, bits):
        return lax.ppermute(x, "owner", [(o, o ^ bits) for o in range(OWNERS)])

    came, unit = lax.optimization_barrier((turned(table, 1), unit))
    sib = to_sibling(unit)
    tables = jnp.concatenate([table, came], axis=0)
    tables = [tables] + [turned(tables, bits) for bits in (2, 4, 6)]

    plan, chosen = pl.pallas_call(
        plan_kernel,
        in_specs=[SMEM] + [VMEM] * 4,
        out_specs=(SMEM, SMEM),
        out_shape=(
            jax.ShapeDtypeStruct((PLAN,), jnp.int32),
            jax.ShapeDtypeStruct((1,), jnp.int32),
        ),
        scratch_shapes=[pltpu.SMEM((OWNERS * 8, 128), jnp.int32), pltpu.SemaphoreType.DMA((4,))],
        compiler_params=params(),
        name="plan",
    )(pos, *tables)

    packed = first_pack(6, pos, plan, unit, sib)
    centered, log_density = lax.switch(
        chosen[0],
        [functools.partial(exchange_and_score, size) for size in SIZES],
        packed, pos, plan, tables, surplus_pairs[0, 0], unit, sib,
    )
    return centered, log_density.reshape(rows)


def solution(mesh):
    return jax.shard_map(
        shards,
        mesh=mesh,
        in_specs=(
            P(("group", "owner"), None),
            P("group", "owner", None, None, None),
            P("group", "owner", None),
            P("group", "owner", None, None),
        ),
        out_specs=(P(("group", "owner"), None), P(("group", "owner"))),
        check_vma=False,
    )
```

```python
import functools

import jax
import jax.numpy as jnp
from jax import lax
from jax.experimental import pallas as pl
from jax.experimental.pallas import tpu as pltpu
from jax.sharding import PartitionSpec as P

BLOCK = 128
BPD = 8
CHIPS = 4
OWNERS = 8
BLOCKS = OWNERS * BPD
ON_CHIP = 2 * BPD
sharpness = 4.0
epsilon = 1e-06
SIZES = (5, 6, 8, 16)


def heads_of(size):
    return size // 2, size % 2


OWN_STEP = 2
COUNTS = 5

STRIDE = 32
F_COUNT, D_COUNT, LOAD, SIZE, NEED, TOUCHED, FAR, F_LIST, D_LIST = 0, 8, 16, 24, 32, 96, 161, 256, 512
PLAN = 768
TASKS, TASK, PLACE = 0, 24, 1560
ROW = 64
PLACES = 1664


def loop(count, body):
    def step(i, carry):
        body(i)
        return carry

    lax.fori_loop(0, count, step, 0)


def along_chips(x, hops):
    route = [(o, ((o // 2 + hops) % CHIPS) * 2 + o % 2) for o in range(OWNERS)]
    return lax.ppermute(x, "owner", route)


def both_ways(x, flip):
    route = [(o, ((o // 2 + (1 if o % 2 == flip else -1)) % CHIPS) * 2 + o % 2) for o in range(OWNERS)]
    return lax.ppermute(x, "owner", route)


def to_sibling(x):
    return lax.ppermute(x, "owner", [(o, o ^ 1) for o in range(OWNERS)])


def normalize_kernel(x_ref, u_ref):
    wide = x_ref[...].astype(jnp.float32)
    mean = jnp.mean(wide * wide, axis=-1, keepdims=True)
    u_ref[...] = (wide * lax.rsqrt(mean + epsilon)).astype(jnp.bfloat16)


def rows_of(block):
    return pl.ds(pl.multiple_of(block * BLOCK, BLOCK), BLOCK)


def kernel_values(p, q):
    dots = lax.dot_general(p, q, (((1,), (1,)), ((), ())), preferred_element_type=jnp.float32)
    return jnp.exp(sharpness * (dots * (1.0 / q.shape[1]) - 1.0))


def add_terms(u_ref, q_ref, acc_ref, kacc_ref, mine, other):
    q = q_ref[rows_of(other), :]
    kernel = kernel_values(u_ref[rows_of(mine), :], q)
    kacc_ref[rows_of(mine), :] += kernel
    acc_ref[rows_of(mine), :] += jnp.dot(
        kernel.astype(jnp.bfloat16), q, preferred_element_type=jnp.float32
    )


def gather_tables(tables, tab_ref, sems):
    return [
        pltpu.make_async_copy(t, tab_ref.at[i * 16 : (i + 1) * 16, :], sems.at[i])
        for i, t in enumerate(tables)
    ]


def plan_kernel(pos_ref, t0, t1, t2, t3, plan_ref, class_ref, tab_ref, sems):
    copies = gather_tables((t0, t1, t2, t3), tab_ref, sems)
    for copy in copies:
        copy.start()
    me = pos_ref[0]
    for i in range(8):
        plan_ref[LOAD + i] = 0
        plan_ref[F_COUNT + i] = 0
        plan_ref[D_COUNT + i] = 0
    for i in range(BLOCKS):
        plan_ref[NEED + i] = 0
    for copy in copies:
        copy.wait()

    def of_owner(o, touched):
        row = (o ^ me) * 8
        for s in range(1, 5):
            q = (o + s) & 7
            to_q, to_o = lax.shift_left(1, q >> 1), lax.shift_left(1, o >> 1)

            def of_pair(t, touched):
                pair = tab_ref[row + s, t]
                for block, chip in ((o * BPD + (pair >> 3), to_q), (q * BPD + (pair & 7), to_o)):
                    before = plan_ref[NEED + block]
                    plan_ref[NEED + block] = before | chip
                    plan_ref[TOUCHED + touched] = block
                    touched = touched + (before == 0).astype(jnp.int32)
                return touched

            touched = lax.fori_loop(0, tab_ref[row + COUNTS, s], of_pair, touched)
        return touched

    touched = lax.fori_loop(0, OWNERS, of_owner, 0)

    def needs(block):
        mask, chip = plan_ref[NEED + block], block >> 4
        bit = lambda hop: lax.shift_right_logical(mask, (chip + hop) & 3) & 1
        return chip, bit(1), bit(3), bit(2)

    def append(count, table, at, block, wanted):
        held = plan_ref[count + at]
        plan_ref[table + at * STRIDE + held] = block
        plan_ref[count + at] = held + wanted

    def one_hop(i, fars):
        block = plan_ref[TOUCHED + i]
        chip, up, down, far = needs(block)
        at = 2 * chip
        plan_ref[LOAD + at] = plan_ref[LOAD + at] + up
        plan_ref[LOAD + at + 1] = plan_ref[LOAD + at + 1] + down
        append(D_COUNT, D_LIST, at, block, up & (1 - far))
        append(D_COUNT, D_LIST, at + 1, block, down & (1 - far))
        plan_ref[FAR + fars] = block
        return fars + far

    fars = lax.fori_loop(0, touched, one_hop, 0)

    @functools.partial(loop, fars)
    def _(i):
        block = plan_ref[FAR + i]
        chip, up, down, _ = needs(block)
        costs, loads = [], []
        for way, near, hop in ((0, up, 1), (1, down, 3)):
            at, after = 2 * chip + way, 2 * ((chip + hop) & 3) + way
            here, there = plan_ref[LOAD + at] + 1 - near, plan_ref[LOAD + after] + 1
            most = jnp.maximum(jnp.maximum(here, there), 2 * plan_ref[F_COUNT + at] + 2)
            costs.append(most * 64 + here + there + 32 * (1 - near))
            loads.append((at, after, here, there))
        goes_down = costs[0] > costs[1]
        at, after, here, there = (jnp.where(goes_down, b, a) for a, b in zip(*loads))
        plan_ref[LOAD + at] = here
        plan_ref[LOAD + after] = there
        append(F_COUNT, F_LIST, at, block, 1)
        append(D_COUNT, D_LIST, at ^ 1, block, jnp.where(goes_down, up, down))

    twice = [plan_ref[F_COUNT + i] for i in range(8)]
    once = [plan_ref[D_COUNT + i] for i in range(8)]
    longest = functools.reduce(jnp.maximum, twice)
    chosen, chosen_size = len(SIZES) - 1, SIZES[-1]
    for k in range(len(SIZES) - 2, -1, -1):
        size = SIZES[k]
        needs = []
        for i in range(8):
            before = (i + (6 if i % 2 == 0 else 2)) % 8
            needs.append(twice[before] + jnp.maximum(twice[i] + once[i] - size, 0))
        fits = jnp.maximum(longest, functools.reduce(jnp.maximum, needs)) <= size
        chosen = jnp.where(fits, k, chosen)
        chosen_size = jnp.where(fits, size, chosen_size)
    class_ref[0] = chosen
    plan_ref[SIZE] = chosen_size


def places_kernel(pos_ref, plan_ref, t0, t1, t2, t3, out_ref, tab_ref, sems):
    copies = gather_tables((t0, t1, t2, t3), tab_ref, sems)
    for copy in copies:
        copy.start()
    for copy in copies:
        copy.wait()
    me = pos_ref[0]
    y, core = me >> 1, me & 1
    size = plan_ref[SIZE]
    for i in range(24):
        out_ref[TASKS + i] = 0

    heads = size >> 1

    def put(block, stage, way, position):
        other = ((position + way) & 1) ^ core
        slot = position >> 1
        single = slot >= heads
        place = jnp.where(single, (2 + position - 2 * heads) * 256, way * 256 + slot) + 4 * 256 * other
        joined = 4 * 256 + jnp.where(single, position, way * heads + slot)
        place = jnp.where((stage == 0) & (other == 1), joined, place)
        out_ref[PLACE + block] = stage * (1 + other) * 65536 + place

    for way in (0, 1):
        near = 2 * ((y + (3 if way == 0 else 1)) & 3) + way
        far = 2 * ((y + 2) & 3) + way
        twice, passing = plan_ref[F_COUNT + near], plan_ref[F_COUNT + far]

        @functools.partial(loop, twice)
        def _(i):
            put(plan_ref[F_LIST + near * STRIDE + i], 0, way, i)

        @functools.partial(loop, plan_ref[D_COUNT + near])
        def _(i):
            late = (twice + i >= size).astype(jnp.int32)
            put(plan_ref[D_LIST + near * STRIDE + i], late, way, twice + i + late * (passing - size))

        @functools.partial(loop, passing)
        def _(i):
            put(plan_ref[F_LIST + far * STRIDE + i], 1, way, i)

    def add_task(own, block):
        place = out_ref[PLACE + block]
        row = (place >> 16) * BPD + own
        count = out_ref[TASKS + row]
        out_ref[TASK + row * ROW + count] = place & 65535
        out_ref[TASKS + row] = count + 1

    for s in range(1, 5):
        above, below = (me + s) & 7, (me - s) & 7

        @pl.when((above >> 1) != y)
        def _():
            @functools.partial(loop, tab_ref[COUNTS, s])
            def _(t):
                pair = tab_ref[s, t]
                add_task(pair >> 3, above * BPD + (pair & 7))

        @pl.when((below >> 1) != y)
        def _():
            row = (below ^ me) * 8

            @functools.partial(loop, tab_ref[row + COUNTS, s])
            def _(t):
                pair = tab_ref[row + s, t]
                add_task(pair & 7, below * BPD + (pair >> 3))


def start_from(id_, core, unit_ref, sib_ref, dst, sem):
    here = rows_of(id_ & 7)
    mine = ((id_ >> 3) & 1) == core

    @pl.when(mine)
    def _():
        pltpu.make_async_copy(unit_ref.at[here, :], dst, sem).start()

    @pl.when(jnp.logical_not(mine))
    def _():
        pltpu.make_async_copy(sib_ref.at[here, :], dst, sem).start()


def listed(plan_ref, row, i, chip):
    twice, once = plan_ref[F_COUNT + row], plan_ref[D_COUNT + row]
    from_f = plan_ref[F_LIST + row * STRIDE + jnp.clip(i, 0, 15)]
    from_d = plan_ref[D_LIST + row * STRIDE + jnp.clip(i - twice, 0, 15)]
    found = jnp.where(i < twice, from_f, from_d)
    return jnp.where(i < twice + once, found, chip * ON_CHIP)


def slots_of(size, core):
    heads, singles = heads_of(size)
    slots = [(way, j, way, 2 * j + (core ^ way)) for way in (0, 1) for j in range(heads)]
    return slots + [(2 + k, 0, core ^ k, 2 * heads + k) for k in range(singles)]


def place_ref(ref, j):
    return ref.at[j * BLOCK : (j + 1) * BLOCK, :]


def first_pack_kernel(size, pos_ref, plan_ref, unit_ref, sib_ref, *refs):
    pieces, sems = refs[:-1], refs[-1]
    y, core = pos_ref[0] >> 1, pos_ref[0] & 1
    for n, (piece, j, way, position) in enumerate(slots_of(size, core)):
        block = listed(plan_ref, 2 * y + way, position, y)
        start_from(block, core, unit_ref, sib_ref, place_ref(pieces[piece], j), sems.at[n])
    for n, (piece, j, _, _) in enumerate(slots_of(size, core)):
        pltpu.make_async_copy(place_ref(unit_ref, 0), place_ref(pieces[piece], j), sems.at[n]).wait()


def second_pack_kernel(size, lo, hi, join, pos_ref, plan_ref, unit_ref, sib_ref, *refs):
    sems = refs[-1]
    joined, refs = (refs[-2], refs[:-2]) if join else (None, refs[:-1])
    got, pieces = refs[: len(refs) - (hi - lo)], refs[len(refs) - (hi - lo) :]
    joins, row = [], 0
    if join:
        for n, piece in enumerate(got):
            rows = piece.shape[0]
            joins.append(pltpu.make_async_copy(piece, joined.at[row : row + rows, :], sems.at[size + n]))
            row += rows
        got = got[lo:]
    y, core = pos_ref[0] >> 1, pos_ref[0] & 1
    slots = [slot for slot in slots_of(size, core) if lo <= slot[0] < hi]
    for n, (piece, j, way, position) in enumerate(slots):
        passing = plan_ref[F_COUNT + 2 * ((y + 3 + 2 * way) & 3) + way]
        dst = place_ref(pieces[piece - lo], j)

        @pl.when(position < passing)
        def _():
            pltpu.make_async_copy(place_ref(got[piece - lo], j), dst, sems.at[n]).start()

        @pl.when(position >= passing)
        def _():
            block = listed(plan_ref, 2 * y + way, position - passing + size, y)
            start_from(block, core, unit_ref, sib_ref, dst, sems.at[n])

    for copy in joins:
        copy.start()
    for n, (piece, j, _, _) in enumerate(slots):
        pltpu.make_async_copy(place_ref(unit_ref, 0), place_ref(pieces[piece - lo], j), sems.at[n]).wait()
    for copy in joins:
        copy.wait()


def own_kernel(pos_ref, tab_ref, surplus_ref, u_ref, sib_ref, acc_ref, kacc_ref, live_ref):
    core = pos_ref[0] & 1

    @functools.partial(loop, BPD * BPD)
    def _(i):
        live_ref[i] = 0.0

    def mark(a, b):
        live_ref[a * BPD + b] = 1.0
        live_ref[b * BPD + a] = 1.0

    @functools.partial(loop, tab_ref[COUNTS, 0])
    def _(t):
        pair = tab_ref[0, t]
        mark(pair >> 3, pair & 7)

    @functools.partial(loop, surplus_ref.shape[0])
    def _(t):
        @pl.when(surplus_ref[t, 2] == 1)
        def _():
            mark(surplus_ref[t, 0], surplus_ref[t, 1])

    step = OWN_STEP

    @functools.partial(loop, BPD // step)
    def _(part):
        here = pl.ds(pl.multiple_of(part * step * BLOCK, step * BLOCK), step * BLOCK)
        kernel = kernel_values(u_ref[here, :], u_ref[...])
        rows = []
        for i in range(step):
            parts = [
                kernel[i * BLOCK : (i + 1) * BLOCK, j * BLOCK : (j + 1) * BLOCK]
                * live_ref[(part * step + i) * BPD + j]
                for j in range(BPD)
            ]
            kacc_ref[rows_of(part * step + i), :] = sum(parts)
            rows.append(jnp.concatenate(parts, axis=1).astype(jnp.bfloat16))
        acc_ref[here, :] = jnp.dot(
            jnp.concatenate(rows, axis=0), u_ref[...], preferred_element_type=jnp.float32
        )

    @functools.partial(loop, tab_ref[core * 8 + COUNTS, 1])
    def _(t):
        pair = tab_ref[core * 8 + 1, t]
        a, b = pair >> 3, pair & 7
        mine, other = jnp.where(core == 0, a, b), jnp.where(core == 0, b, a)
        add_terms(u_ref, sib_ref, acc_ref, kacc_ref, mine, other)


def each_task(part, task_ref, own, pieces, q_ref, body):
    row = part * BPD + own

    @functools.partial(loop, task_ref[TASKS + row])
    def _(t):
        place = task_ref[TASK + row * ROW + t]
        for n, piece in pieces:

            @pl.when((place >> 8) == n)
            def _():
                q_ref[...] = piece[rows_of(place & 255), :]

        body(q_ref[...])


def numbered(here, there):
    return [*enumerate(here), *enumerate(there, 4)]


def part_kernel(part, here, sums, task_ref, u_ref, *refs):
    starts, refs = refs[: 2 * sums], refs[2 * sums :]
    pieces, (acc_ref, kacc_ref, q_ref) = numbered(refs[:here], refs[here:-3]), refs[-3:]
    for out, ins in ((acc_ref, starts[0::2]), (kacc_ref, starts[1::2])):
        out[...] = sum((x[...] for x in ins[1:]), ins[0][...]) if ins else jnp.zeros_like(out)

    @functools.partial(loop, BPD)
    def _(own):
        here = rows_of(own)

        def add(q):
            kernel = kernel_values(u_ref[here, :], q)
            kacc_ref[here, :] += kernel
            acc_ref[here, :] += jnp.dot(kernel.astype(jnp.bfloat16), q, preferred_element_type=jnp.float32)

        each_task(part, task_ref, own, pieces, q_ref, add)


def last_kernel(task_ref, u_ref, acc_in, kacc_in, *refs):
    got, (out_ref, log_ref, acc_ref, kacc_ref, q_ref, done_ref, sems) = refs[:-7], refs[-7:]
    pieces = numbered((), got)
    rows = lax.broadcasted_iota(jnp.int32, (BLOCK, BLOCK), 0)
    diagonal = rows == lax.broadcasted_iota(jnp.int32, (BLOCK, BLOCK), 1)

    def out_copy(own):
        here = rows_of(own)
        return pltpu.make_async_copy(done_ref.at[here, :], out_ref.at[here, :], sems.at[own])

    @functools.partial(loop, BPD)
    def _(own):
        here = rows_of(own)
        acc_ref[...] = acc_in[here, :]
        kacc_ref[...] = kacc_in[here, :]

        def add(q):
            kernel = kernel_values(u_ref[here, :], q)
            kacc_ref[...] += kernel
            acc_ref[...] += jnp.dot(kernel.astype(jnp.bfloat16), q, preferred_element_type=jnp.float32)

        each_task(2, task_ref, own, pieces, q_ref, add)
        density = jnp.sum(kacc_ref[...], axis=1, keepdims=True)
        done_ref[here, :] = (
            u_ref[here, :].astype(jnp.float32) - acc_ref[...] * (1.0 / density)
        ).astype(jnp.bfloat16)
        out_copy(own).start()
        across = jnp.sum(jnp.where(diagonal, density, 0.0), axis=0, keepdims=True)
        log_ref[pl.ds(own, 1), :] = jnp.log(across)

    for own in range(BPD):
        out_copy(own).wait()


SMEM = pl.BlockSpec(memory_space=pltpu.SMEM)
VMEM = pl.BlockSpec(memory_space=pltpu.VMEM)
ANY = pl.BlockSpec(memory_space=pl.ANY)


def params():
    return pltpu.CompilerParams(vmem_limit_bytes=26 * 2**20)


COST = pl.CostEstimate(flops=1, bytes_accessed=1, transcendentals=0)


def pieces_of(size, width):
    heads, singles = heads_of(size)
    counts = [heads] * 2 + [1] * singles
    return tuple(jax.ShapeDtypeStruct((count * BLOCK, width), jnp.bfloat16) for count in counts)


def send(pieces):
    moved = [along_chips(pieces[0], 1), along_chips(pieces[1], -1)]
    return moved + [both_ways(x, flip) for flip, x in enumerate(pieces[2:])]


def pack(kernel, name, size, out, *operands):
    return pl.pallas_call(
        kernel,
        in_specs=[SMEM, SMEM] + [ANY] * (len(operands) - 2),
        out_specs=(VMEM,) * len(out),
        out_shape=out,
        scratch_shapes=[pltpu.SemaphoreType.DMA((size + 4,))],
        compiler_params=params(),
        name=name,
    )(*operands)


def first_pack(size, pos, plan, unit, sib):
    out = pieces_of(size, unit.shape[1])
    return pack(functools.partial(first_pack_kernel, size), "first_pack", size, out, pos, plan, unit, sib)


def exchange_and_score(size, packed, pos, plan, tables, surplus, unit, sib):
    rows, width = unit.shape
    sums = (
        jax.ShapeDtypeStruct((rows, width), jnp.float32),
        jax.ShapeDtypeStruct((rows, BLOCK), jnp.float32),
    )

    if size != SIZES[0]:
        packed = first_pack(size, pos, plan, unit, sib)
    got = send(packed)
    places = pl.pallas_call(
        places_kernel,
        in_specs=[SMEM, SMEM] + [VMEM] * 4,
        out_specs=SMEM,
        out_shape=jax.ShapeDtypeStruct((PLACES,), jnp.int32),
        scratch_shapes=[pltpu.SMEM((OWNERS * 8, 128), jnp.int32), pltpu.SemaphoreType.DMA((4,))],
        cost_estimate=COST,
        compiler_params=params(),
        name="places",
    )(pos, plan, *tables)
    acc, kacc = pl.pallas_call(
        own_kernel,
        in_specs=[SMEM, SMEM, SMEM, VMEM, VMEM],
        out_specs=(VMEM, VMEM),
        out_shape=sums,
        scratch_shapes=[pltpu.SMEM((BPD * BPD,), jnp.float32)],
        compiler_params=params(),
        cost_estimate=COST,
        name="own_pairs",
    )(pos, tables[0], surplus, unit, sib)
    heads, singles = heads_of(size)
    out = pieces_of(size, width)
    joined = (jax.ShapeDtypeStruct((size * BLOCK, width), jnp.bfloat16),)

    def pass_on(lo, hi, join, got):
        kernel = functools.partial(second_pack_kernel, size, lo, hi, join)
        more = joined if join else ()
        return pack(kernel, "second_pack", size, out[lo:hi] + more, pos, plan, unit, sib, *got)

    got[0], got[1], acc, places = lax.optimization_barrier((got[0], got[1], acc, places))
    sent = pass_on(0, 2, not singles, got[:2])
    far = [along_chips(sent[0], 1), along_chips(sent[1], -1)]
    if singles:
        *late, got[0], got[1], _ = lax.optimization_barrier((*got[2:], *got[:2], sent[0]))
        got[2:] = late
        sent = pass_on(2, 2 + singles, True, got)
        far += [both_ways(x, flip) for flip, x in enumerate(sent[:-1])]
    joined = sent[-1]

    def add_part(part, totals, here, there):
        return pl.pallas_call(
            functools.partial(part_kernel, part, len(here), len(totals)),
            in_specs=[SMEM] + [VMEM] * (1 + 2 * len(totals) + len(here) + len(there)),
            out_specs=(VMEM, VMEM),
            out_shape=sums,
            scratch_shapes=[pltpu.VMEM((BLOCK, width), jnp.bfloat16)],
            compiler_params=params(),
            cost_estimate=COST,
            name=f"part{part}",
        )(places, unit, *(x for total in totals for x in total), *here, *there)

    def beside(joined, *got):
        return add_part(0, [], got, [to_sibling(joined)])

    def nothing(*_):
        return tuple(jnp.zeros(x.shape, x.dtype) for x in sums)

    first_part = lax.cond(plan[SIZE] > 0, beside, nothing, joined, *got)
    *far, first_acc = lax.optimization_barrier((*far, first_part[0]))
    sib_far = [to_sibling(x) for x in far]
    acc, kacc = add_part(1, [(acc, kacc), (first_acc, first_part[1])], far, [])
    *sib_far, acc = lax.optimization_barrier((*sib_far, acc))
    return pl.pallas_call(
        last_kernel,
        in_specs=[SMEM] + [VMEM] * (3 + len(far)),
        out_specs=(ANY, VMEM),
        out_shape=(
            jax.ShapeDtypeStruct((rows, width), jnp.bfloat16),
            jax.ShapeDtypeStruct((BPD, BLOCK), jnp.float32),
        ),
        scratch_shapes=[
            pltpu.VMEM((BLOCK, width), jnp.float32),
            pltpu.VMEM((BLOCK, BLOCK), jnp.float32),
            pltpu.VMEM((BLOCK, width), jnp.bfloat16),
            pltpu.VMEM((rows, width), jnp.bfloat16),
            pltpu.SemaphoreType.DMA((BPD,)),
        ],
        compiler_params=params(),
        cost_estimate=COST,
        name="last_part",
    )(places, unit, acc, kacc, *sib_far)


def shards(embeddings, home_pairs, home_count, surplus_pairs):
    rows, width = embeddings.shape
    pairs, count = home_pairs[0, 0], home_count[0, 0]
    shifts = pairs.shape[0]
    pos = lax.axis_index("owner").astype(jnp.int32).reshape(1)

    step = 128
    unit = pl.pallas_call(
        normalize_kernel,
        grid=(rows // step,),
        in_specs=[pl.BlockSpec((step, width), lambda i: (i, 0))],
        out_specs=pl.BlockSpec((step, width), lambda i: (i, 0)),
        out_shape=jax.ShapeDtypeStruct(embeddings.shape, jnp.bfloat16),
        cost_estimate=COST,
        compiler_params=params(),
        name="normalize",
    )(embeddings)

    codes = jnp.sum(pairs * jnp.array([8, 1], jnp.int32), axis=-1)
    table = jnp.pad(codes, ((0, 8 - shifts), (0, 128 - codes.shape[1]))) + jnp.pad(
        count[None], ((COUNTS, 7 - COUNTS), (0, 128 - shifts))
    )

    def turned(x, bits):
        return lax.ppermute(x, "owner", [(o, o ^ bits) for o in range(OWNERS)])

    came, unit = lax.optimization_barrier((turned(table, 1), unit))
    sib = to_sibling(unit)
    tables = jnp.concatenate([table, came], axis=0)
    tables = [tables] + [turned(tables, bits) for bits in (2, 4, 6)]

    plan, chosen = pl.pallas_call(
        plan_kernel,
        in_specs=[SMEM] + [VMEM] * 4,
        out_specs=(SMEM, SMEM),
        out_shape=(
            jax.ShapeDtypeStruct((PLAN,), jnp.int32),
            jax.ShapeDtypeStruct((1,), jnp.int32),
        ),
        scratch_shapes=[pltpu.SMEM((OWNERS * 8, 128), jnp.int32), pltpu.SemaphoreType.DMA((4,))],
        compiler_params=params(),
        name="plan",
    )(pos, *tables)

    packed = first_pack(SIZES[0], pos, plan, unit, sib)
    centered, log_density = lax.switch(
        chosen[0],
        [functools.partial(exchange_and_score, size) for size in SIZES],
        packed, pos, plan, tables, surplus_pairs[0, 0], unit, sib,
    )
    return centered, log_density.reshape(rows)


def solution(mesh):
    return jax.shard_map(
        shards,
        mesh=mesh,
        in_specs=(
            P(("group", "owner"), None),
            P("group", "owner", None, None, None),
            P("group", "owner", None),
            P("group", "owner", None, None),
        ),
        out_specs=(P(("group", "owner"), None), P(("group", "owner"))),
        check_vma=False,
    )
```

```python
import functools

import jax
import jax.numpy as jnp
from jax import lax
from jax.experimental import pallas as pl
from jax.experimental.pallas import tpu as pltpu
from jax.sharding import PartitionSpec as P

BLOCK = 128
BPD = 8
CHIPS = 4
OWNERS = 8
BLOCKS = OWNERS * BPD
ON_CHIP = 2 * BPD
sharpness = 4.0
epsilon = 1e-06
SIZES = (5, 6, 8, 16)
PACKED = 6


def heads_of(size):
    return (2, size - 4) if size <= 6 else (size // 2, 0)


OWN_STEP = 2
COUNTS = 5

STRIDE = 32
F_COUNT, D_COUNT, LOAD, SIZE, NEED, TOUCHED, FAR, F_LIST, D_LIST = 0, 8, 16, 24, 32, 96, 161, 256, 512
PLAN = 768
TASKS, TASK, PLACE = 0, 24, 1560
ROW = 64
PLACES = 1664


def loop(count, body):
    def step(i, carry):
        body(i)
        return carry

    lax.fori_loop(0, count, step, 0)


def along_chips(x, hops):
    route = [(o, ((o // 2 + hops) % CHIPS) * 2 + o % 2) for o in range(OWNERS)]
    return lax.ppermute(x, "owner", route)


def both_ways(x, flip):
    route = [(o, ((o // 2 + (1 if o % 2 == flip else -1)) % CHIPS) * 2 + o % 2) for o in range(OWNERS)]
    return lax.ppermute(x, "owner", route)


def to_sibling(x):
    return lax.ppermute(x, "owner", [(o, o ^ 1) for o in range(OWNERS)])


def normalize_kernel(x_ref, u_ref):
    wide = x_ref[...].astype(jnp.float32)
    mean = jnp.mean(wide * wide, axis=-1, keepdims=True)
    u_ref[...] = (wide * lax.rsqrt(mean + epsilon)).astype(jnp.bfloat16)


def table_kernel(pairs_ref, count_ref, out_ref):
    out_ref[...] = jnp.zeros_like(out_ref)
    shifts, _, slots = pairs_ref.shape
    for s in range(shifts):
        out_ref[s : s + 1, 0:slots] = pairs_ref[s, 0:1, :] * 8 + pairs_ref[s, 1:2, :]
    out_ref[COUNTS : COUNTS + 1, 0:shifts] = count_ref[...]


def rows_of(block):
    return pl.ds(pl.multiple_of(block * BLOCK, BLOCK), BLOCK)


def kernel_values(p, q):
    dots = lax.dot_general(p, q, (((1,), (1,)), ((), ())), preferred_element_type=jnp.float32)
    return jnp.exp(sharpness * (dots * (1.0 / q.shape[1]) - 1.0))


def add_terms(u_ref, q_ref, acc_ref, kacc_ref, mine, other):
    q = q_ref[rows_of(other), :]
    kernel = kernel_values(u_ref[rows_of(mine), :], q)
    kacc_ref[rows_of(mine), :] += kernel
    acc_ref[rows_of(mine), :] += jnp.dot(
        kernel.astype(jnp.bfloat16), q, preferred_element_type=jnp.float32
    )


def gather_tables(tables, tab_ref, sems):
    return [
        pltpu.make_async_copy(t, tab_ref.at[i * 16 : (i + 1) * 16, :], sems.at[i])
        for i, t in enumerate(tables)
    ]


def plan_and_pack_kernel(size, pos_ref, t0, t1, t2, t3, unit_ref, sib_ref, plan_ref, class_ref, *refs):
    pieces, (tab_ref, sems, pack_sems) = refs[:-3], refs[-3:]
    plan_kernel(pos_ref, t0, t1, t2, t3, plan_ref, class_ref, tab_ref, sems)
    first_pack_kernel(size, pos_ref, plan_ref, unit_ref, sib_ref, *pieces, pack_sems)


def plan_kernel(pos_ref, t0, t1, t2, t3, plan_ref, class_ref, tab_ref, sems):
    copies = gather_tables((t0, t1, t2, t3), tab_ref, sems)
    for copy in copies:
        copy.start()
    me = pos_ref[0]
    for i in range(8):
        plan_ref[LOAD + i] = 0
        plan_ref[F_COUNT + i] = 0
        plan_ref[D_COUNT + i] = 0
    for i in range(BLOCKS):
        plan_ref[NEED + i] = 0
    for copy in copies:
        copy.wait()

    def of_owner(o, touched):
        row = (o ^ me) * 8
        for s in range(1, 5):
            q = (o + s) & 7
            to_q, to_o = lax.shift_left(1, q >> 1), lax.shift_left(1, o >> 1)

            def of_pair(t, touched):
                pair = tab_ref[row + s, t]
                for block, chip in ((o * BPD + (pair >> 3), to_q), (q * BPD + (pair & 7), to_o)):
                    before = plan_ref[NEED + block]
                    plan_ref[NEED + block] = before | chip
                    plan_ref[TOUCHED + touched] = block
                    touched = touched + (before == 0).astype(jnp.int32)
                return touched

            touched = lax.fori_loop(0, tab_ref[row + COUNTS, s], of_pair, touched)
        return touched

    touched = lax.fori_loop(0, OWNERS, of_owner, 0)

    def needs(block):
        mask, chip = plan_ref[NEED + block], block >> 4
        bit = lambda hop: lax.shift_right_logical(mask, (chip + hop) & 3) & 1
        return chip, bit(1), bit(3), bit(2)

    def append(count, table, at, block, wanted):
        held = plan_ref[count + at]
        plan_ref[table + at * STRIDE + held] = block
        plan_ref[count + at] = held + wanted

    def one_hop(i, fars):
        block = plan_ref[TOUCHED + i]
        chip, up, down, far = needs(block)
        at = 2 * chip
        plan_ref[LOAD + at] = plan_ref[LOAD + at] + up
        plan_ref[LOAD + at + 1] = plan_ref[LOAD + at + 1] + down
        append(D_COUNT, D_LIST, at, block, up & (1 - far))
        append(D_COUNT, D_LIST, at + 1, block, down & (1 - far))
        plan_ref[FAR + fars] = block
        return fars + far

    fars = lax.fori_loop(0, touched, one_hop, 0)

    @functools.partial(loop, fars)
    def _(i):
        block = plan_ref[FAR + i]
        chip, up, down, _ = needs(block)
        costs, loads = [], []
        for way, near, hop in ((0, up, 1), (1, down, 3)):
            at, after = 2 * chip + way, 2 * ((chip + hop) & 3) + way
            here, there = plan_ref[LOAD + at] + 1 - near, plan_ref[LOAD + after] + 1
            most = jnp.maximum(jnp.maximum(here, there), 2 * plan_ref[F_COUNT + at] + 2)
            costs.append(most * 64 + here + there + 32 * (1 - near))
            loads.append((at, after, here, there))
        goes_down = costs[0] > costs[1]
        at, after, here, there = (jnp.where(goes_down, b, a) for a, b in zip(*loads))
        plan_ref[LOAD + at] = here
        plan_ref[LOAD + after] = there
        append(F_COUNT, F_LIST, at, block, 1)
        append(D_COUNT, D_LIST, at ^ 1, block, jnp.where(goes_down, up, down))

    twice = [plan_ref[F_COUNT + i] for i in range(8)]
    once = [plan_ref[D_COUNT + i] for i in range(8)]
    longest = functools.reduce(jnp.maximum, twice)
    chosen, chosen_size = len(SIZES) - 1, SIZES[-1]
    for k in range(len(SIZES) - 2, -1, -1):
        size = SIZES[k]
        needs = []
        for i in range(8):
            before = (i + (6 if i % 2 == 0 else 2)) % 8
            needs.append(twice[before] + jnp.maximum(twice[i] + once[i] - size, 0))
        fits = jnp.maximum(longest, functools.reduce(jnp.maximum, needs)) <= size
        chosen = jnp.where(fits, k, chosen)
        chosen_size = jnp.where(fits, size, chosen_size)
    class_ref[0] = chosen
    plan_ref[SIZE] = chosen_size


def places_kernel(pos_ref, plan_ref, t0, t1, t2, t3, out_ref, tab_ref, sems):
    copies = gather_tables((t0, t1, t2, t3), tab_ref, sems)
    for copy in copies:
        copy.start()
    for copy in copies:
        copy.wait()
    me = pos_ref[0]
    y, core = me >> 1, me & 1
    size = plan_ref[SIZE]
    for i in range(24):
        out_ref[TASKS + i] = 0

    heads = jnp.where(size <= 6, 2, size >> 1)

    def put(block, stage, way, position):
        other = ((position + way) & 1) ^ core
        slot = position >> 1
        single = slot >= heads
        place = jnp.where(single, (2 + position - 2 * heads) * 256, way * 256 + slot) + 4 * 256 * other
        joined = 4 * 256 + jnp.where(single, position, way * heads + slot)
        place = jnp.where((stage == 0) & (other == 1), joined, place)
        out_ref[PLACE + block] = stage * (1 + other) * 65536 + place

    for way in (0, 1):
        near = 2 * ((y + (3 if way == 0 else 1)) & 3) + way
        far = 2 * ((y + 2) & 3) + way
        twice, passing = plan_ref[F_COUNT + near], plan_ref[F_COUNT + far]

        @functools.partial(loop, twice)
        def _(i):
            put(plan_ref[F_LIST + near * STRIDE + i], 0, way, i)

        @functools.partial(loop, plan_ref[D_COUNT + near])
        def _(i):
            late = (twice + i >= size).astype(jnp.int32)
            put(plan_ref[D_LIST + near * STRIDE + i], late, way, twice + i + late * (passing - size))

        @functools.partial(loop, passing)
        def _(i):
            put(plan_ref[F_LIST + far * STRIDE + i], 1, way, i)

    def add_task(own, block):
        place = out_ref[PLACE + block]
        row = (place >> 16) * BPD + own
        count = out_ref[TASKS + row]
        out_ref[TASK + row * ROW + count] = place & 65535
        out_ref[TASKS + row] = count + 1

    for s in range(1, 5):
        above, below = (me + s) & 7, (me - s) & 7

        @pl.when((above >> 1) != y)
        def _():
            @functools.partial(loop, tab_ref[COUNTS, s])
            def _(t):
                pair = tab_ref[s, t]
                add_task(pair >> 3, above * BPD + (pair & 7))

        @pl.when((below >> 1) != y)
        def _():
            row = (below ^ me) * 8

            @functools.partial(loop, tab_ref[row + COUNTS, s])
            def _(t):
                pair = tab_ref[row + s, t]
                add_task(pair & 7, below * BPD + (pair >> 3))


def start_from(id_, core, unit_ref, sib_ref, dst, sem):
    here = rows_of(id_ & 7)
    mine = ((id_ >> 3) & 1) == core

    @pl.when(mine)
    def _():
        pltpu.make_async_copy(unit_ref.at[here, :], dst, sem).start()

    @pl.when(jnp.logical_not(mine))
    def _():
        pltpu.make_async_copy(sib_ref.at[here, :], dst, sem).start()


def listed(plan_ref, row, i, chip):
    twice, once = plan_ref[F_COUNT + row], plan_ref[D_COUNT + row]
    from_f = plan_ref[F_LIST + row * STRIDE + jnp.clip(i, 0, 15)]
    from_d = plan_ref[D_LIST + row * STRIDE + jnp.clip(i - twice, 0, 15)]
    found = jnp.where(i < twice, from_f, from_d)
    return jnp.where(i < twice + once, found, chip * ON_CHIP)


def slots_of(size, core):
    heads, singles = heads_of(size)
    slots = [(way, j, way, 2 * j + (core ^ way)) for way in (0, 1) for j in range(heads)]
    return slots + [(2 + k, 0, core ^ k, 2 * heads + k) for k in range(singles)]


def place_ref(ref, j):
    return ref.at[j * BLOCK : (j + 1) * BLOCK, :]


def first_pack_kernel(size, pos_ref, plan_ref, unit_ref, sib_ref, *refs):
    pieces, sems = refs[:-1], refs[-1]
    y, core = pos_ref[0] >> 1, pos_ref[0] & 1
    for n, (piece, j, way, position) in enumerate(slots_of(size, core)):
        block = listed(plan_ref, 2 * y + way, position, y)
        start_from(block, core, unit_ref, sib_ref, place_ref(pieces[piece], j), sems.at[n])
    for n, (piece, j, _, _) in enumerate(slots_of(size, core)):
        pltpu.make_async_copy(place_ref(unit_ref, 0), place_ref(pieces[piece], j), sems.at[n]).wait()


def second_pack_kernel(size, lo, hi, join, pos_ref, plan_ref, unit_ref, sib_ref, *refs):
    sems = refs[-1]
    joined, refs = (refs[-2], refs[:-2]) if join else (None, refs[:-1])
    got, pieces = refs[: len(refs) - (hi - lo)], refs[len(refs) - (hi - lo) :]
    joins, row = [], 0
    if join:
        for n, piece in enumerate(got):
            rows = piece.shape[0]
            joins.append(pltpu.make_async_copy(piece, joined.at[row : row + rows, :], sems.at[size + n]))
            row += rows
        got = got[lo:]
    y, core = pos_ref[0] >> 1, pos_ref[0] & 1
    slots = [slot for slot in slots_of(size, core) if lo <= slot[0] < hi]
    for n, (piece, j, way, position) in enumerate(slots):
        passing = plan_ref[F_COUNT + 2 * ((y + 3 + 2 * way) & 3) + way]
        dst = place_ref(pieces[piece - lo], j)

        @pl.when(position < passing)
        def _():
            pltpu.make_async_copy(place_ref(got[piece - lo], j), dst, sems.at[n]).start()

        @pl.when(position >= passing)
        def _():
            block = listed(plan_ref, 2 * y + way, position - passing + size, y)
            start_from(block, core, unit_ref, sib_ref, dst, sems.at[n])

    for copy in joins:
        copy.start()
    for n, (piece, j, _, _) in enumerate(slots):
        pltpu.make_async_copy(place_ref(unit_ref, 0), place_ref(pieces[piece - lo], j), sems.at[n]).wait()
    for copy in joins:
        copy.wait()


def own_kernel(pos_ref, tab_ref, surplus_ref, u_ref, sib_ref, acc_ref, kacc_ref, live_ref):
    core = pos_ref[0] & 1

    @functools.partial(loop, BPD * BPD)
    def _(i):
        live_ref[i] = 0.0

    def mark(a, b):
        live_ref[a * BPD + b] = 1.0
        live_ref[b * BPD + a] = 1.0

    @functools.partial(loop, tab_ref[COUNTS, 0])
    def _(t):
        pair = tab_ref[0, t]
        mark(pair >> 3, pair & 7)

    @functools.partial(loop, surplus_ref.shape[0])
    def _(t):
        @pl.when(surplus_ref[t, 2] == 1)
        def _():
            mark(surplus_ref[t, 0], surplus_ref[t, 1])

    step = OWN_STEP

    @functools.partial(loop, BPD // step)
    def _(part):
        here = pl.ds(pl.multiple_of(part * step * BLOCK, step * BLOCK), step * BLOCK)
        kernel = kernel_values(u_ref[here, :], u_ref[...])
        rows = []
        for i in range(step):
            parts = [
                kernel[i * BLOCK : (i + 1) * BLOCK, j * BLOCK : (j + 1) * BLOCK]
                * live_ref[(part * step + i) * BPD + j]
                for j in range(BPD)
            ]
            kacc_ref[rows_of(part * step + i), :] = sum(parts)
            rows.append(jnp.concatenate(parts, axis=1).astype(jnp.bfloat16))
        acc_ref[here, :] = jnp.dot(
            jnp.concatenate(rows, axis=0), u_ref[...], preferred_element_type=jnp.float32
        )

    @functools.partial(loop, tab_ref[core * 8 + COUNTS, 1])
    def _(t):
        pair = tab_ref[core * 8 + 1, t]
        a, b = pair >> 3, pair & 7
        mine, other = jnp.where(core == 0, a, b), jnp.where(core == 0, b, a)
        add_terms(u_ref, sib_ref, acc_ref, kacc_ref, mine, other)


def each_task(part, task_ref, own, pieces, q_ref, body):
    row = part * BPD + own

    @functools.partial(loop, task_ref[TASKS + row])
    def _(t):
        place = task_ref[TASK + row * ROW + t]
        for n, piece in pieces:

            @pl.when((place >> 8) == n)
            def _():
                q_ref[...] = piece[rows_of(place & 255), :]

        body(q_ref[...])


def numbered(here, there):
    return [*enumerate(here), *enumerate(there, 4)]


def part_kernel(part, here, task_ref, u_ref, acc_in, kacc_in, *refs):
    pieces, (acc_ref, kacc_ref, q_ref) = numbered(refs[:here], refs[here:-3]), refs[-3:]
    acc_ref[...] = acc_in[...]
    kacc_ref[...] = kacc_in[...]

    @functools.partial(loop, BPD)
    def _(own):
        here = rows_of(own)

        def add(q):
            kernel = kernel_values(u_ref[here, :], q)
            kacc_ref[here, :] += kernel
            acc_ref[here, :] += jnp.dot(kernel.astype(jnp.bfloat16), q, preferred_element_type=jnp.float32)

        each_task(part, task_ref, own, pieces, q_ref, add)


def last_kernel(task_ref, u_ref, acc_in, kacc_in, *refs):
    got, (out_ref, log_ref, acc_ref, kacc_ref, q_ref, done_ref, sems) = refs[:-7], refs[-7:]
    pieces = numbered((), got)
    rows = lax.broadcasted_iota(jnp.int32, (BLOCK, BLOCK), 0)
    diagonal = rows == lax.broadcasted_iota(jnp.int32, (BLOCK, BLOCK), 1)

    def out_copy(own):
        here = rows_of(own)
        return pltpu.make_async_copy(done_ref.at[here, :], out_ref.at[here, :], sems.at[own])

    @functools.partial(loop, BPD)
    def _(own):
        here = rows_of(own)
        acc_ref[...] = acc_in[here, :]
        kacc_ref[...] = kacc_in[here, :]

        def add(q):
            kernel = kernel_values(u_ref[here, :], q)
            kacc_ref[...] += kernel
            acc_ref[...] += jnp.dot(kernel.astype(jnp.bfloat16), q, preferred_element_type=jnp.float32)

        each_task(2, task_ref, own, pieces, q_ref, add)
        density = jnp.sum(kacc_ref[...], axis=1, keepdims=True)
        done_ref[here, :] = (
            u_ref[here, :].astype(jnp.float32) - acc_ref[...] * (1.0 / density)
        ).astype(jnp.bfloat16)
        out_copy(own).start()
        across = jnp.sum(jnp.where(diagonal, density, 0.0), axis=0, keepdims=True)
        log_ref[pl.ds(own, 1), :] = jnp.log(across)

    for own in range(BPD):
        out_copy(own).wait()


SMEM = pl.BlockSpec(memory_space=pltpu.SMEM)
VMEM = pl.BlockSpec(memory_space=pltpu.VMEM)
ANY = pl.BlockSpec(memory_space=pl.ANY)


def params():
    return pltpu.CompilerParams(vmem_limit_bytes=26 * 2**20)


COST = pl.CostEstimate(flops=1, bytes_accessed=1, transcendentals=0)


def pieces_of(size, width):
    heads, singles = heads_of(size)
    counts = [heads] * 2 + [1] * singles
    return tuple(jax.ShapeDtypeStruct((count * BLOCK, width), jnp.bfloat16) for count in counts)


def send(pieces):
    moved = [along_chips(pieces[0], 1), along_chips(pieces[1], -1)]
    return moved + [both_ways(x, flip) for flip, x in enumerate(pieces[2:])]


def pack(kernel, name, size, out, *operands):
    return pl.pallas_call(
        kernel,
        in_specs=[SMEM, SMEM] + [ANY] * (len(operands) - 2),
        out_specs=(VMEM,) * len(out),
        out_shape=out,
        scratch_shapes=[pltpu.SemaphoreType.DMA((size + 4,))],
        compiler_params=params(),
        name=name,
    )(*operands)


def first_pack(size, pos, plan, unit, sib):
    out = pieces_of(size, unit.shape[1])
    return pack(functools.partial(first_pack_kernel, size), "first_pack", size, out, pos, plan, unit, sib)


def exchange_and_score(size, packed, pos, plan, tables, surplus, unit, sib):
    rows, width = unit.shape
    sums = (
        jax.ShapeDtypeStruct((rows, width), jnp.float32),
        jax.ShapeDtypeStruct((rows, BLOCK), jnp.float32),
    )

    if size > PACKED:
        packed = first_pack(size, pos, plan, unit, sib)
    got = send(packed[: 2 + heads_of(size)[1]])
    places = pl.pallas_call(
        places_kernel,
        in_specs=[SMEM, SMEM] + [VMEM] * 4,
        out_specs=SMEM,
        out_shape=jax.ShapeDtypeStruct((PLACES,), jnp.int32),
        scratch_shapes=[pltpu.SMEM((OWNERS * 8, 128), jnp.int32), pltpu.SemaphoreType.DMA((4,))],
        cost_estimate=COST,
        compiler_params=params(),
        name="places",
    )(pos, plan, *tables)
    acc, kacc = pl.pallas_call(
        own_kernel,
        in_specs=[SMEM, SMEM, SMEM, VMEM, VMEM],
        out_specs=(VMEM, VMEM),
        out_shape=sums,
        scratch_shapes=[pltpu.SMEM((BPD * BPD,), jnp.float32)],
        compiler_params=params(),
        cost_estimate=COST,
        name="own_pairs",
    )(pos, tables[0], surplus, unit, sib)
    heads, singles = heads_of(size)
    out = pieces_of(size, width)
    joined = (jax.ShapeDtypeStruct((size * BLOCK, width), jnp.bfloat16),)

    def pass_on(lo, hi, join, got):
        kernel = functools.partial(second_pack_kernel, size, lo, hi, join)
        more = joined if join else ()
        return pack(kernel, "second_pack", size, out[lo:hi] + more, pos, plan, unit, sib, *got)

    got[0], got[1], acc = lax.optimization_barrier((got[0], got[1], acc))
    sent = pass_on(0, 2, not singles, got[:2])
    far = [along_chips(sent[0], 1), along_chips(sent[1], -1)]
    if singles:
        *late, got[0], got[1], _ = lax.optimization_barrier((*got[2:], *got[:2], sent[0]))
        got[2:] = late
        sent = pass_on(2, 2 + singles, True, got)
        far += [both_ways(x, flip) for flip, x in enumerate(sent[:-1])]
    joined = sent[-1]

    def add_part(part, acc, kacc, here, there):
        return pl.pallas_call(
            functools.partial(part_kernel, part, len(here)),
            in_specs=[SMEM] + [VMEM] * (3 + len(here) + len(there)),
            out_specs=(VMEM, VMEM),
            out_shape=sums,
            scratch_shapes=[pltpu.VMEM((BLOCK, width), jnp.bfloat16)],
            compiler_params=params(),
            cost_estimate=COST,
            name=f"part{part}",
        )(places, unit, acc, kacc, *here, *there)

    acc, kacc = add_part(0, acc, kacc, got, [to_sibling(joined)])
    *far, acc = lax.optimization_barrier((*far, acc))
    sib_far = [to_sibling(x) for x in far]
    acc, kacc = add_part(1, acc, kacc, far, [])
    *sib_far, acc = lax.optimization_barrier((*sib_far, acc))
    return pl.pallas_call(
        last_kernel,
        in_specs=[SMEM] + [VMEM] * (3 + len(far)),
        out_specs=(ANY, VMEM),
        out_shape=(
            jax.ShapeDtypeStruct((rows, width), jnp.bfloat16),
            jax.ShapeDtypeStruct((BPD, BLOCK), jnp.float32),
        ),
        scratch_shapes=[
            pltpu.VMEM((BLOCK, width), jnp.float32),
            pltpu.VMEM((BLOCK, BLOCK), jnp.float32),
            pltpu.VMEM((BLOCK, width), jnp.bfloat16),
            pltpu.VMEM((rows, width), jnp.bfloat16),
            pltpu.SemaphoreType.DMA((BPD,)),
        ],
        compiler_params=params(),
        cost_estimate=COST,
        name="last_part",
    )(places, unit, acc, kacc, *sib_far)


def shards(embeddings, home_pairs, home_count, surplus_pairs):
    rows, width = embeddings.shape
    pairs, count = home_pairs[0, 0], home_count[0, 0]
    shifts = pairs.shape[0]
    pos = lax.axis_index("owner").astype(jnp.int32).reshape(1)

    step = 128
    unit = pl.pallas_call(
        normalize_kernel,
        grid=(rows // step,),
        in_specs=[pl.BlockSpec((step, width), lambda i: (i, 0))],
        out_specs=pl.BlockSpec((step, width), lambda i: (i, 0)),
        out_shape=jax.ShapeDtypeStruct(embeddings.shape, jnp.bfloat16),
        cost_estimate=COST,
        compiler_params=params(),
        name="normalize",
    )(embeddings)

    table = pl.pallas_call(
        table_kernel,
        in_specs=[VMEM, VMEM],
        out_specs=VMEM,
        out_shape=jax.ShapeDtypeStruct((8, 128), jnp.int32),
        compiler_params=params(),
        cost_estimate=COST,
        name="table",
    )(jnp.swapaxes(pairs, 1, 2), count[None])

    def turned(x, bits):
        return lax.ppermute(x, "owner", [(o, o ^ bits) for o in range(OWNERS)])

    came, unit = lax.optimization_barrier((turned(table, 1), unit))
    sib = to_sibling(unit)
    tables = jnp.concatenate([table, came], axis=0)
    tables = [tables] + [turned(tables, bits) for bits in (2, 4, 6)]

    out = pieces_of(PACKED, width)
    plan, chosen, *packed = pl.pallas_call(
        functools.partial(plan_and_pack_kernel, PACKED),
        in_specs=[SMEM] + [VMEM] * 4 + [ANY] * 2,
        out_specs=(SMEM, SMEM) + (VMEM,) * len(out),
        out_shape=(
            jax.ShapeDtypeStruct((PLAN,), jnp.int32),
            jax.ShapeDtypeStruct((1,), jnp.int32),
            *out,
        ),
        scratch_shapes=[
            pltpu.SMEM((OWNERS * 8, 128), jnp.int32),
            pltpu.SemaphoreType.DMA((4,)),
            pltpu.SemaphoreType.DMA((PACKED,)),
        ],
        compiler_params=params(),
        name="plan",
    )(pos, *tables, unit, sib)

    centered, log_density = lax.switch(
        chosen[0],
        [functools.partial(exchange_and_score, size) for size in SIZES],
        packed, pos, plan, tables, surplus_pairs[0, 0], unit, sib,
    )
    return centered, log_density.reshape(rows)


def solution(mesh):
    return jax.shard_map(
        shards,
        mesh=mesh,
        in_specs=(
            P(("group", "owner"), None),
            P("group", "owner", None, None, None),
            P("group", "owner", None),
            P("group", "owner", None, None),
        ),
        out_specs=(P(("group", "owner"), None), P(("group", "owner"))),
        check_vma=False,
    )
```

```python
import functools

import jax
import jax.numpy as jnp
from jax import lax
from jax.experimental import pallas as pl
from jax.experimental.pallas import tpu as pltpu
from jax.sharding import PartitionSpec as P

BLOCK = 128
BPD = 8
CHIPS = 4
OWNERS = 8
BLOCKS = OWNERS * BPD
ON_CHIP = 2 * BPD
sharpness = 4.0
epsilon = 1e-06
SIZES = (5, 6, 8, 16)
PACKED = 6


def heads_of(size):
    return (2, size - 4) if size <= 6 else (size // 2, 0)


OWN_STEP = 2
COUNTS = 5

STRIDE = 32
F_COUNT, D_COUNT, LOAD, SIZE, NEED, TOUCHED, FAR, F_LIST, D_LIST = 0, 8, 16, 24, 32, 96, 161, 256, 512
PLAN = 768
TASKS, TASK, PLACE = 0, 24, 1560
ROW = 64
PLACES = 1664


def loop(count, body):
    def step(i, carry):
        body(i)
        return carry

    lax.fori_loop(0, count, step, 0)


def along_chips(x, hops):
    route = [(o, ((o // 2 + hops) % CHIPS) * 2 + o % 2) for o in range(OWNERS)]
    return lax.ppermute(x, "owner", route)


def both_ways(x, flip):
    route = [(o, ((o // 2 + (1 if o % 2 == flip else -1)) % CHIPS) * 2 + o % 2) for o in range(OWNERS)]
    return lax.ppermute(x, "owner", route)


def to_sibling(x):
    return lax.ppermute(x, "owner", [(o, o ^ 1) for o in range(OWNERS)])


def normalize_kernel(x_ref, u_ref):
    wide = x_ref[...].astype(jnp.float32)
    mean = jnp.mean(wide * wide, axis=-1, keepdims=True)
    u_ref[...] = (wide * lax.rsqrt(mean + epsilon)).astype(jnp.bfloat16)


def table_kernel(pairs_hbm, count_hbm, out_ref, pairs_ref, count_ref, sems):
    copies = [
        pltpu.make_async_copy(pairs_hbm, pairs_ref, sems.at[0]),
        pltpu.make_async_copy(count_hbm, count_ref, sems.at[1]),
    ]
    for copy in copies:
        copy.start()
    out_ref[...] = jnp.zeros_like(out_ref)
    for copy in copies:
        copy.wait()
    shifts, _, slots = pairs_ref.shape
    for s in range(shifts):
        out_ref[s : s + 1, 0:slots] = pairs_ref[s, 0:1, :] * 8 + pairs_ref[s, 1:2, :]
    out_ref[COUNTS : COUNTS + 1, 0:shifts] = count_ref[...]


def rows_of(block):
    return pl.ds(pl.multiple_of(block * BLOCK, BLOCK), BLOCK)


def kernel_values(p, q):
    dots = lax.dot_general(p, q, (((1,), (1,)), ((), ())), preferred_element_type=jnp.float32)
    return jnp.exp(sharpness * (dots * (1.0 / q.shape[1]) - 1.0))


def add_terms(u_ref, q_ref, acc_ref, kacc_ref, mine, other):
    q = q_ref[rows_of(other), :]
    kernel = kernel_values(u_ref[rows_of(mine), :], q)
    kacc_ref[rows_of(mine), :] += kernel
    acc_ref[rows_of(mine), :] += jnp.dot(
        kernel.astype(jnp.bfloat16), q, preferred_element_type=jnp.float32
    )


def gather_tables(tables, tab_ref, sems):
    return [
        pltpu.make_async_copy(t, tab_ref.at[i * 16 : (i + 1) * 16, :], sems.at[i])
        for i, t in enumerate(tables)
    ]


def plan_and_pack_kernel(size, pos_ref, t0, t1, t2, t3, unit_ref, sib_ref, plan_ref, class_ref, *refs):
    pieces, (tab_ref, sems, pack_sems) = refs[:-3], refs[-3:]
    plan_kernel(pos_ref, t0, t1, t2, t3, plan_ref, class_ref, tab_ref, sems)
    first_pack_kernel(size, pos_ref, plan_ref, unit_ref, sib_ref, *pieces, pack_sems)


def plan_kernel(pos_ref, t0, t1, t2, t3, plan_ref, class_ref, tab_ref, sems):
    copies = gather_tables((t0, t1, t2, t3), tab_ref, sems)
    for copy in copies:
        copy.start()
    me = pos_ref[0]
    for i in range(8):
        plan_ref[LOAD + i] = 0
        plan_ref[F_COUNT + i] = 0
        plan_ref[D_COUNT + i] = 0
    for i in range(BLOCKS):
        plan_ref[NEED + i] = 0
    for copy in copies:
        copy.wait()

    def of_owner(o, touched):
        row = (o ^ me) * 8
        for s in range(1, 5):
            q = (o + s) & 7
            to_q, to_o = lax.shift_left(1, q >> 1), lax.shift_left(1, o >> 1)

            def of_pair(t, touched):
                pair = tab_ref[row + s, t]
                for block, chip in ((o * BPD + (pair >> 3), to_q), (q * BPD + (pair & 7), to_o)):
                    before = plan_ref[NEED + block]
                    plan_ref[NEED + block] = before | chip
                    plan_ref[TOUCHED + touched] = block
                    touched = touched + (before == 0).astype(jnp.int32)
                return touched

            touched = lax.fori_loop(0, tab_ref[row + COUNTS, s], of_pair, touched)
        return touched

    touched = lax.fori_loop(0, OWNERS, of_owner, 0)

    def needs(block):
        mask, chip = plan_ref[NEED + block], block >> 4
        bit = lambda hop: lax.shift_right_logical(mask, (chip + hop) & 3) & 1
        return chip, bit(1), bit(3), bit(2)

    def append(count, table, at, block, wanted):
        held = plan_ref[count + at]
        plan_ref[table + at * STRIDE + held] = block
        plan_ref[count + at] = held + wanted

    def one_hop(i, fars):
        block = plan_ref[TOUCHED + i]
        chip, up, down, far = needs(block)
        at = 2 * chip
        plan_ref[LOAD + at] = plan_ref[LOAD + at] + up
        plan_ref[LOAD + at + 1] = plan_ref[LOAD + at + 1] + down
        append(D_COUNT, D_LIST, at, block, up & (1 - far))
        append(D_COUNT, D_LIST, at + 1, block, down & (1 - far))
        plan_ref[FAR + fars] = block
        return fars + far

    fars = lax.fori_loop(0, touched, one_hop, 0)

    @functools.partial(loop, fars)
    def _(i):
        block = plan_ref[FAR + i]
        chip, up, down, _ = needs(block)
        costs, loads = [], []
        for way, near, hop in ((0, up, 1), (1, down, 3)):
            at, after = 2 * chip + way, 2 * ((chip + hop) & 3) + way
            here, there = plan_ref[LOAD + at] + 1 - near, plan_ref[LOAD + after] + 1
            most = jnp.maximum(jnp.maximum(here, there), 2 * plan_ref[F_COUNT + at] + 2)
            costs.append(most * 64 + here + there + 32 * (1 - near))
            loads.append((at, after, here, there))
        goes_down = costs[0] > costs[1]
        at, after, here, there = (jnp.where(goes_down, b, a) for a, b in zip(*loads))
        plan_ref[LOAD + at] = here
        plan_ref[LOAD + after] = there
        append(F_COUNT, F_LIST, at, block, 1)
        append(D_COUNT, D_LIST, at ^ 1, block, jnp.where(goes_down, up, down))

    twice = [plan_ref[F_COUNT + i] for i in range(8)]
    once = [plan_ref[D_COUNT + i] for i in range(8)]
    longest = functools.reduce(jnp.maximum, twice)
    chosen, chosen_size = len(SIZES) - 1, SIZES[-1]
    for k in range(len(SIZES) - 2, -1, -1):
        size = SIZES[k]
        needs = []
        for i in range(8):
            before = (i + (6 if i % 2 == 0 else 2)) % 8
            needs.append(twice[before] + jnp.maximum(twice[i] + once[i] - size, 0))
        fits = jnp.maximum(longest, functools.reduce(jnp.maximum, needs)) <= size
        chosen = jnp.where(fits, k, chosen)
        chosen_size = jnp.where(fits, size, chosen_size)
    class_ref[0] = chosen
    plan_ref[SIZE] = chosen_size


def places_kernel(pos_ref, plan_ref, t0, t1, t2, t3, out_ref, tab_ref, sems):
    copies = gather_tables((t0, t1, t2, t3), tab_ref, sems)
    for copy in copies:
        copy.start()
    for copy in copies:
        copy.wait()
    me = pos_ref[0]
    y, core = me >> 1, me & 1
    size = plan_ref[SIZE]
    for i in range(24):
        out_ref[TASKS + i] = 0

    heads = jnp.where(size <= 6, 2, size >> 1)

    def put(block, stage, way, position):
        other = ((position + way) & 1) ^ core
        slot = position >> 1
        single = slot >= heads
        place = jnp.where(single, (2 + position - 2 * heads) * 256, way * 256 + slot) + 4 * 256 * other
        joined = 4 * 256 + jnp.where(single, position, way * heads + slot)
        place = jnp.where((stage == 0) & (other == 1), joined, place)
        out_ref[PLACE + block] = stage * (1 + other) * 65536 + place

    for way in (0, 1):
        near = 2 * ((y + (3 if way == 0 else 1)) & 3) + way
        far = 2 * ((y + 2) & 3) + way
        twice, passing = plan_ref[F_COUNT + near], plan_ref[F_COUNT + far]

        @functools.partial(loop, twice)
        def _(i):
            put(plan_ref[F_LIST + near * STRIDE + i], 0, way, i)

        @functools.partial(loop, plan_ref[D_COUNT + near])
        def _(i):
            late = (twice + i >= size).astype(jnp.int32)
            put(plan_ref[D_LIST + near * STRIDE + i], late, way, twice + i + late * (passing - size))

        @functools.partial(loop, passing)
        def _(i):
            put(plan_ref[F_LIST + far * STRIDE + i], 1, way, i)

    def add_task(own, block):
        place = out_ref[PLACE + block]
        row = (place >> 16) * BPD + own
        count = out_ref[TASKS + row]
        out_ref[TASK + row * ROW + count] = place & 65535
        out_ref[TASKS + row] = count + 1

    for s in range(1, 5):
        above, below = (me + s) & 7, (me - s) & 7

        @pl.when((above >> 1) != y)
        def _():
            @functools.partial(loop, tab_ref[COUNTS, s])
            def _(t):
                pair = tab_ref[s, t]
                add_task(pair >> 3, above * BPD + (pair & 7))

        @pl.when((below >> 1) != y)
        def _():
            row = (below ^ me) * 8

            @functools.partial(loop, tab_ref[row + COUNTS, s])
            def _(t):
                pair = tab_ref[row + s, t]
                add_task(pair & 7, below * BPD + (pair >> 3))


def start_from(id_, core, unit_ref, sib_ref, dst, sem):
    here = rows_of(id_ & 7)
    mine = ((id_ >> 3) & 1) == core

    @pl.when(mine)
    def _():
        pltpu.make_async_copy(unit_ref.at[here, :], dst, sem).start()

    @pl.when(jnp.logical_not(mine))
    def _():
        pltpu.make_async_copy(sib_ref.at[here, :], dst, sem).start()


def listed(plan_ref, row, i, chip):
    twice, once = plan_ref[F_COUNT + row], plan_ref[D_COUNT + row]
    from_f = plan_ref[F_LIST + row * STRIDE + jnp.clip(i, 0, 15)]
    from_d = plan_ref[D_LIST + row * STRIDE + jnp.clip(i - twice, 0, 15)]
    found = jnp.where(i < twice, from_f, from_d)
    return jnp.where(i < twice + once, found, chip * ON_CHIP)


def slots_of(size, core):
    heads, singles = heads_of(size)
    slots = [(way, j, way, 2 * j + (core ^ way)) for way in (0, 1) for j in range(heads)]
    return slots + [(2 + k, 0, core ^ k, 2 * heads + k) for k in range(singles)]


def place_ref(ref, j):
    return ref.at[j * BLOCK : (j + 1) * BLOCK, :]


def first_pack_kernel(size, pos_ref, plan_ref, unit_ref, sib_ref, *refs):
    pieces, sems = refs[:-1], refs[-1]
    y, core = pos_ref[0] >> 1, pos_ref[0] & 1
    for n, (piece, j, way, position) in enumerate(slots_of(size, core)):
        block = listed(plan_ref, 2 * y + way, position, y)
        start_from(block, core, unit_ref, sib_ref, place_ref(pieces[piece], j), sems.at[n])
    for n, (piece, j, _, _) in enumerate(slots_of(size, core)):
        pltpu.make_async_copy(place_ref(unit_ref, 0), place_ref(pieces[piece], j), sems.at[n]).wait()


def second_pack_kernel(size, lo, hi, join, pos_ref, plan_ref, unit_ref, sib_ref, *refs):
    sems = refs[-1]
    joined, refs = (refs[-2], refs[:-2]) if join else (None, refs[:-1])
    got, pieces = refs[: len(refs) - (hi - lo)], refs[len(refs) - (hi - lo) :]
    joins, row = [], 0
    if join:
        for n, piece in enumerate(got):
            rows = piece.shape[0]
            joins.append(pltpu.make_async_copy(piece, joined.at[row : row + rows, :], sems.at[size + n]))
            row += rows
        got = got[lo:]
    y, core = pos_ref[0] >> 1, pos_ref[0] & 1
    slots = [slot for slot in slots_of(size, core) if lo <= slot[0] < hi]
    for n, (piece, j, way, position) in enumerate(slots):
        passing = plan_ref[F_COUNT + 2 * ((y + 3 + 2 * way) & 3) + way]
        dst = place_ref(pieces[piece - lo], j)

        @pl.when(position < passing)
        def _():
            pltpu.make_async_copy(place_ref(got[piece - lo], j), dst, sems.at[n]).start()

        @pl.when(position >= passing)
        def _():
            block = listed(plan_ref, 2 * y + way, position - passing + size, y)
            start_from(block, core, unit_ref, sib_ref, dst, sems.at[n])

    for copy in joins:
        copy.start()
    for n, (piece, j, _, _) in enumerate(slots):
        pltpu.make_async_copy(place_ref(unit_ref, 0), place_ref(pieces[piece - lo], j), sems.at[n]).wait()
    for copy in joins:
        copy.wait()


def own_kernel(pos_ref, tab_ref, surplus_ref, u_ref, sib_ref, acc_ref, kacc_ref, live_ref):
    core = pos_ref[0] & 1

    @functools.partial(loop, BPD * BPD)
    def _(i):
        live_ref[i] = 0.0

    def mark(a, b):
        live_ref[a * BPD + b] = 1.0
        live_ref[b * BPD + a] = 1.0

    @functools.partial(loop, tab_ref[COUNTS, 0])
    def _(t):
        pair = tab_ref[0, t]
        mark(pair >> 3, pair & 7)

    @functools.partial(loop, surplus_ref.shape[0])
    def _(t):
        @pl.when(surplus_ref[t, 2] == 1)
        def _():
            mark(surplus_ref[t, 0], surplus_ref[t, 1])

    step = OWN_STEP

    @functools.partial(loop, BPD // step)
    def _(part):
        here = pl.ds(pl.multiple_of(part * step * BLOCK, step * BLOCK), step * BLOCK)
        kernel = kernel_values(u_ref[here, :], u_ref[...])
        rows = []
        for i in range(step):
            parts = [
                kernel[i * BLOCK : (i + 1) * BLOCK, j * BLOCK : (j + 1) * BLOCK]
                * live_ref[(part * step + i) * BPD + j]
                for j in range(BPD)
            ]
            kacc_ref[rows_of(part * step + i), :] = sum(parts)
            rows.append(jnp.concatenate(parts, axis=1).astype(jnp.bfloat16))
        acc_ref[here, :] = jnp.dot(
            jnp.concatenate(rows, axis=0), u_ref[...], preferred_element_type=jnp.float32
        )

    @functools.partial(loop, tab_ref[core * 8 + COUNTS, 1])
    def _(t):
        pair = tab_ref[core * 8 + 1, t]
        a, b = pair >> 3, pair & 7
        mine, other = jnp.where(core == 0, a, b), jnp.where(core == 0, b, a)
        add_terms(u_ref, sib_ref, acc_ref, kacc_ref, mine, other)


def each_task(part, task_ref, own, pieces, q_ref, body):
    row = part * BPD + own
    count = task_ref[TASKS + row]

    @functools.partial(loop, (count + 1) >> 1)
    def _(i):
        second = jnp.minimum(2 * i + 1, count - 1)
        for half, t in enumerate((2 * i, second)):
            place = task_ref[TASK + row * ROW + t]
            for n, piece in pieces:

                @pl.when((place >> 8) == n)
                def _():
                    q_ref[half * BLOCK : (half + 1) * BLOCK, :] = piece[rows_of(place & 255), :]

        body(q_ref[...], jnp.where(2 * i + 1 < count, 1.0, 0.0))


def two_kernels(p, q, weight):
    kernel = kernel_values(p, q)
    first, second = kernel[:, :BLOCK], kernel[:, BLOCK:] * weight
    low = jnp.concatenate([first, second], axis=1).astype(jnp.bfloat16)
    return first + second, jnp.dot(low, q, preferred_element_type=jnp.float32)


def numbered(here, there):
    return [*enumerate(here), *enumerate(there, 4)]


def part_kernel(part, here, task_ref, u_ref, acc_in, kacc_in, *refs):
    pieces, (acc_ref, kacc_ref, q_ref) = numbered(refs[:here], refs[here:-3]), refs[-3:]
    acc_ref[...] = acc_in[...]
    kacc_ref[...] = kacc_in[...]

    @functools.partial(loop, BPD)
    def _(own):
        here = rows_of(own)

        def add(q, weight):
            kernel, terms = two_kernels(u_ref[here, :], q, weight)
            kacc_ref[here, :] += kernel
            acc_ref[here, :] += terms

        each_task(part, task_ref, own, pieces, q_ref, add)


def last_kernel(task_ref, u_ref, acc_in, kacc_in, *refs):
    got, (out_ref, log_ref, acc_ref, kacc_ref, q_ref, done_ref, sems) = refs[:-7], refs[-7:]
    pieces = numbered((), got)
    rows = lax.broadcasted_iota(jnp.int32, (BLOCK, BLOCK), 0)
    diagonal = rows == lax.broadcasted_iota(jnp.int32, (BLOCK, BLOCK), 1)

    def out_copy(own):
        here = rows_of(own)
        return pltpu.make_async_copy(done_ref.at[here, :], out_ref.at[here, :], sems.at[own])

    @functools.partial(loop, BPD)
    def _(own):
        here = rows_of(own)
        acc_ref[...] = acc_in[here, :]
        kacc_ref[...] = kacc_in[here, :]

        def add(q, weight):
            kernel, terms = two_kernels(u_ref[here, :], q, weight)
            kacc_ref[...] += kernel
            acc_ref[...] += terms

        each_task(2, task_ref, own, pieces, q_ref, add)
        density = jnp.sum(kacc_ref[...], axis=1, keepdims=True)
        done_ref[here, :] = (
            u_ref[here, :].astype(jnp.float32) - acc_ref[...] * (1.0 / density)
        ).astype(jnp.bfloat16)
        out_copy(own).start()
        across = jnp.sum(jnp.where(diagonal, density, 0.0), axis=0, keepdims=True)
        log_ref[pl.ds(own, 1), :] = jnp.log(across)

    for own in range(BPD):
        out_copy(own).wait()


SMEM = pl.BlockSpec(memory_space=pltpu.SMEM)
VMEM = pl.BlockSpec(memory_space=pltpu.VMEM)
ANY = pl.BlockSpec(memory_space=pl.ANY)
HBM = pl.BlockSpec(memory_space=pltpu.HBM)


def params():
    return pltpu.CompilerParams(vmem_limit_bytes=26 * 2**20)


COST = pl.CostEstimate(flops=1, bytes_accessed=1, transcendentals=0)


def pieces_of(size, width):
    heads, singles = heads_of(size)
    counts = [heads] * 2 + [1] * singles
    return tuple(jax.ShapeDtypeStruct((count * BLOCK, width), jnp.bfloat16) for count in counts)


def send(pieces):
    moved = [along_chips(pieces[0], 1), along_chips(pieces[1], -1)]
    return moved + [both_ways(x, flip) for flip, x in enumerate(pieces[2:])]


def pack(kernel, name, size, out, *operands):
    return pl.pallas_call(
        kernel,
        in_specs=[SMEM, SMEM] + [ANY] * (len(operands) - 2),
        out_specs=(VMEM,) * len(out),
        out_shape=out,
        scratch_shapes=[pltpu.SemaphoreType.DMA((size + 4,))],
        compiler_params=params(),
        name=name,
    )(*operands)


def first_pack(size, pos, plan, unit, sib):
    out = pieces_of(size, unit.shape[1])
    return pack(functools.partial(first_pack_kernel, size), "first_pack", size, out, pos, plan, unit, sib)


def exchange_and_score(size, packed, pos, plan, tables, surplus, unit, sib):
    rows, width = unit.shape
    sums = (
        jax.ShapeDtypeStruct((rows, width), jnp.float32),
        jax.ShapeDtypeStruct((rows, BLOCK), jnp.float32),
    )

    if size > PACKED:
        packed = first_pack(size, pos, plan, unit, sib)
    got = send(packed[: 2 + heads_of(size)[1]])
    places = pl.pallas_call(
        places_kernel,
        in_specs=[SMEM, SMEM] + [VMEM] * 4,
        out_specs=SMEM,
        out_shape=jax.ShapeDtypeStruct((PLACES,), jnp.int32),
        scratch_shapes=[pltpu.SMEM((OWNERS * 8, 128), jnp.int32), pltpu.SemaphoreType.DMA((4,))],
        cost_estimate=COST,
        compiler_params=params(),
        name="places",
    )(pos, plan, *tables)
    acc, kacc = pl.pallas_call(
        own_kernel,
        in_specs=[SMEM, SMEM, SMEM, VMEM, VMEM],
        out_specs=(VMEM, VMEM),
        out_shape=sums,
        scratch_shapes=[pltpu.SMEM((BPD * BPD,), jnp.float32)],
        compiler_params=params(),
        cost_estimate=COST,
        name="own_pairs",
    )(pos, tables[0], surplus, unit, sib)
    heads, singles = heads_of(size)
    out = pieces_of(size, width)
    joined = (jax.ShapeDtypeStruct((size * BLOCK, width), jnp.bfloat16),)

    def pass_on(lo, hi, join, got):
        kernel = functools.partial(second_pack_kernel, size, lo, hi, join)
        more = joined if join else ()
        return pack(kernel, "second_pack", size, out[lo:hi] + more, pos, plan, unit, sib, *got)

    got[0], got[1], acc = lax.optimization_barrier((got[0], got[1], acc))
    sent = pass_on(0, 2, not singles, got[:2])
    far = [along_chips(sent[0], 1), along_chips(sent[1], -1)]
    if singles:
        *late, got[0], got[1], _ = lax.optimization_barrier((*got[2:], *got[:2], sent[0]))
        got[2:] = late
        sent = pass_on(2, 2 + singles, True, got)
        far += [both_ways(x, flip) for flip, x in enumerate(sent[:-1])]
    joined = sent[-1]

    def add_part(part, acc, kacc, here, there):
        return pl.pallas_call(
            functools.partial(part_kernel, part, len(here)),
            in_specs=[SMEM] + [VMEM] * (3 + len(here) + len(there)),
            out_specs=(VMEM, VMEM),
            out_shape=sums,
            scratch_shapes=[pltpu.VMEM((2 * BLOCK, width), jnp.bfloat16)],
            compiler_params=params(),
            cost_estimate=COST,
            name=f"part{part}",
        )(places, unit, acc, kacc, *here, *there)

    acc, kacc = add_part(0, acc, kacc, got, [to_sibling(joined)])
    *far, acc = lax.optimization_barrier((*far, acc))
    sib_far = [to_sibling(x) for x in far]
    acc, kacc = add_part(1, acc, kacc, far, [])
    *sib_far, acc = lax.optimization_barrier((*sib_far, acc))
    return pl.pallas_call(
        last_kernel,
        in_specs=[SMEM] + [VMEM] * (3 + len(far)),
        out_specs=(ANY, VMEM),
        out_shape=(
            jax.ShapeDtypeStruct((rows, width), jnp.bfloat16),
            jax.ShapeDtypeStruct((BPD, BLOCK), jnp.float32),
        ),
        scratch_shapes=[
            pltpu.VMEM((BLOCK, width), jnp.float32),
            pltpu.VMEM((BLOCK, BLOCK), jnp.float32),
            pltpu.VMEM((2 * BLOCK, width), jnp.bfloat16),
            pltpu.VMEM((rows, width), jnp.bfloat16),
            pltpu.SemaphoreType.DMA((BPD,)),
        ],
        compiler_params=params(),
        cost_estimate=COST,
        name="last_part",
    )(places, unit, acc, kacc, *sib_far)


def shards(embeddings, home_pairs, home_count, surplus_pairs):
    rows, width = embeddings.shape
    pairs, count = home_pairs[0, 0], home_count[0, 0]
    shifts = pairs.shape[0]
    pos = lax.axis_index("owner").astype(jnp.int32).reshape(1)

    step = 128
    unit = pl.pallas_call(
        normalize_kernel,
        grid=(rows // step,),
        in_specs=[pl.BlockSpec((step, width), lambda i: (i, 0))],
        out_specs=pl.BlockSpec((step, width), lambda i: (i, 0)),
        out_shape=jax.ShapeDtypeStruct(embeddings.shape, jnp.bfloat16),
        cost_estimate=COST,
        compiler_params=params(),
        name="normalize",
    )(embeddings)

    table = pl.pallas_call(
        table_kernel,
        in_specs=[HBM, HBM],
        scratch_shapes=[
            pltpu.VMEM((shifts, 2, pairs.shape[1]), jnp.int32),
            pltpu.VMEM((1, shifts), jnp.int32),
            pltpu.SemaphoreType.DMA((2,)),
        ],
        out_specs=VMEM,
        out_shape=jax.ShapeDtypeStruct((8, 128), jnp.int32),
        compiler_params=params(),
        cost_estimate=COST,
        name="table",
    )(jnp.swapaxes(pairs, 1, 2), count[None])

    def turned(x, bits):
        return lax.ppermute(x, "owner", [(o, o ^ bits) for o in range(OWNERS)])

    came, unit = lax.optimization_barrier((turned(table, 1), unit))
    sib = to_sibling(unit)
    tables = jnp.concatenate([table, came], axis=0)
    tables = [tables] + [turned(tables, bits) for bits in (2, 4, 6)]

    out = pieces_of(PACKED, width)
    plan, chosen, *packed = pl.pallas_call(
        functools.partial(plan_and_pack_kernel, PACKED),
        in_specs=[SMEM] + [VMEM] * 4 + [ANY] * 2,
        out_specs=(SMEM, SMEM) + (VMEM,) * len(out),
        out_shape=(
            jax.ShapeDtypeStruct((PLAN,), jnp.int32),
            jax.ShapeDtypeStruct((1,), jnp.int32),
            *out,
        ),
        scratch_shapes=[
            pltpu.SMEM((OWNERS * 8, 128), jnp.int32),
            pltpu.SemaphoreType.DMA((4,)),
            pltpu.SemaphoreType.DMA((PACKED,)),
        ],
        compiler_params=params(),
        name="plan",
    )(pos, *tables, unit, sib)

    centered, log_density = lax.switch(
        chosen[0],
        [functools.partial(exchange_and_score, size) for size in SIZES],
        packed, pos, plan, tables, surplus_pairs[0, 0], unit, sib,
    )
    return centered, log_density.reshape(rows)


def solution(mesh):
    return jax.shard_map(
        shards,
        mesh=mesh,
        in_specs=(
            P(("group", "owner"), None),
            P("group", "owner", None, None, None),
            P("group", "owner", None),
            P("group", "owner", None, None),
        ),
        out_specs=(P(("group", "owner"), None), P(("group", "owner"))),
        check_vma=False,
    )
```

```python
import functools

import jax
import jax.numpy as jnp
from jax import lax
from jax.experimental import pallas as pl
from jax.experimental.pallas import tpu as pltpu
from jax.sharding import PartitionSpec as P

BLOCK = 128
BPD = 8
CHIPS = 4
OWNERS = 8
BLOCKS = OWNERS * BPD
ON_CHIP = 2 * BPD
sharpness = 4.0
epsilon = 1e-06
SIZES = (5, 6, 8, 16)
PACKED = (5, 1)


def first_pieces(size):
    return PACKED if size == sum(PACKED) else (size,)


OWN_STEP = 2
COUNTS = 5

STRIDE = 32
F_COUNT, D_COUNT, LOAD, SIZE, NEED, TOUCHED, FAR, F_LIST, D_LIST = 0, 8, 16, 24, 32, 96, 161, 256, 512
PLAN = 768
TASKS, TASK, PLACE = 0, 24, 1560
ROW = 64
PLACES = 1664


def loop(count, body):
    def step(i, carry):
        body(i)
        return carry

    lax.fori_loop(0, count, step, 0)


def both_ways(x):
    route = [(o, ((o // 2 + (1 if o % 2 == 0 else -1)) % CHIPS) * 2 + o % 2) for o in range(OWNERS)]
    return lax.ppermute(x, "owner", route)


def to_sibling(x):
    return lax.ppermute(x, "owner", [(o, o ^ 1) for o in range(OWNERS)])


def normalize_kernel(x_ref, u_ref):
    wide = x_ref[...].astype(jnp.float32)
    mean = jnp.mean(wide * wide, axis=-1, keepdims=True)
    u_ref[...] = (wide * lax.rsqrt(mean + epsilon)).astype(jnp.bfloat16)


def table_kernel(pairs_hbm, count_hbm, out_ref, pairs_ref, count_ref, sems):
    copies = [
        pltpu.make_async_copy(pairs_hbm, pairs_ref, sems.at[0]),
        pltpu.make_async_copy(count_hbm, count_ref, sems.at[1]),
    ]
    for copy in copies:
        copy.start()
    out_ref[...] = jnp.zeros_like(out_ref)
    for copy in copies:
        copy.wait()
    shifts, _, slots = pairs_ref.shape
    for s in range(shifts):
        out_ref[s : s + 1, 0:slots] = pairs_ref[s, 0:1, :] * 8 + pairs_ref[s, 1:2, :]
    out_ref[COUNTS : COUNTS + 1, 0:shifts] = count_ref[...]


def rows_of(block):
    return pl.ds(pl.multiple_of(block * BLOCK, BLOCK), BLOCK)


def kernel_values(p, q):
    dots = lax.dot_general(p, q, (((1,), (1,)), ((), ())), preferred_element_type=jnp.float32)
    return jnp.exp(sharpness * (dots * (1.0 / q.shape[1]) - 1.0))


def add_terms(u_ref, q_ref, acc_ref, kacc_ref, mine, other):
    q = q_ref[rows_of(other), :]
    kernel = kernel_values(u_ref[rows_of(mine), :], q)
    kacc_ref[rows_of(mine), :] += kernel
    acc_ref[rows_of(mine), :] += jnp.dot(
        kernel.astype(jnp.bfloat16), q, preferred_element_type=jnp.float32
    )


def gather_tables(tables, tab_ref, sems):
    return [
        pltpu.make_async_copy(t, tab_ref.at[i * 16 : (i + 1) * 16, :], sems.at[i])
        for i, t in enumerate(tables)
    ]


def plan_and_pack_kernel(counts, pos_ref, t0, t1, t2, t3, unit_ref, sib_ref, plan_ref, class_ref, *refs):
    pieces, (tab_ref, sems, pack_sems) = refs[:-3], refs[-3:]
    plan_kernel(pos_ref, t0, t1, t2, t3, plan_ref, class_ref, tab_ref, sems)
    first_pack_kernel(counts, pos_ref, plan_ref, unit_ref, sib_ref, *pieces, pack_sems)


def plan_kernel(pos_ref, t0, t1, t2, t3, plan_ref, class_ref, tab_ref, sems):
    copies = gather_tables((t0, t1, t2, t3), tab_ref, sems)
    for copy in copies:
        copy.start()
    me = pos_ref[0]
    for i in range(8):
        plan_ref[LOAD + i] = 0
        plan_ref[F_COUNT + i] = 0
        plan_ref[D_COUNT + i] = 0
    for i in range(BLOCKS):
        plan_ref[NEED + i] = 0
    for copy in copies:
        copy.wait()

    def of_owner(o, touched):
        row = (o ^ me) * 8
        for s in range(1, 5):
            q = (o + s) & 7
            to_q, to_o = lax.shift_left(1, q >> 1), lax.shift_left(1, o >> 1)

            def of_pair(t, touched):
                pair = tab_ref[row + s, t]
                for block, chip in ((o * BPD + (pair >> 3), to_q), (q * BPD + (pair & 7), to_o)):
                    before = plan_ref[NEED + block]
                    plan_ref[NEED + block] = before | chip
                    plan_ref[TOUCHED + touched] = block
                    touched = touched + (before == 0).astype(jnp.int32)
                return touched

            touched = lax.fori_loop(0, tab_ref[row + COUNTS, s], of_pair, touched)
        return touched

    touched = lax.fori_loop(0, OWNERS, of_owner, 0)

    def needs(block):
        mask, chip = plan_ref[NEED + block], block >> 4
        bit = lambda hop: lax.shift_right_logical(mask, (chip + hop) & 3) & 1
        return chip, bit(1), bit(3), bit(2)

    def append(count, table, at, block, wanted):
        held = plan_ref[count + at]
        plan_ref[table + at * STRIDE + held] = block
        plan_ref[count + at] = held + wanted

    def one_hop(i, fars):
        block = plan_ref[TOUCHED + i]
        chip, up, down, far = needs(block)
        at = 2 * chip
        plan_ref[LOAD + at] = plan_ref[LOAD + at] + up
        plan_ref[LOAD + at + 1] = plan_ref[LOAD + at + 1] + down
        append(D_COUNT, D_LIST, at, block, up & (1 - far))
        append(D_COUNT, D_LIST, at + 1, block, down & (1 - far))
        plan_ref[FAR + fars] = block
        return fars + far

    fars = lax.fori_loop(0, touched, one_hop, 0)

    @functools.partial(loop, fars)
    def _(i):
        block = plan_ref[FAR + i]
        chip, up, down, _ = needs(block)
        costs, loads = [], []
        for way, near, hop in ((0, up, 1), (1, down, 3)):
            at, after = 2 * chip + way, 2 * ((chip + hop) & 3) + way
            here, there = plan_ref[LOAD + at] + 1 - near, plan_ref[LOAD + after] + 1
            most = jnp.maximum(jnp.maximum(here, there), 2 * plan_ref[F_COUNT + at] + 2)
            costs.append(most * 64 + here + there + 32 * (1 - near))
            loads.append((at, after, here, there))
        goes_down = costs[0] > costs[1]
        at, after, here, there = (jnp.where(goes_down, b, a) for a, b in zip(*loads))
        plan_ref[LOAD + at] = here
        plan_ref[LOAD + after] = there
        append(F_COUNT, F_LIST, at, block, 1)
        append(D_COUNT, D_LIST, at ^ 1, block, jnp.where(goes_down, up, down))

    twice = [plan_ref[F_COUNT + i] for i in range(8)]
    once = [plan_ref[D_COUNT + i] for i in range(8)]
    longest = functools.reduce(jnp.maximum, twice)
    chosen, chosen_size = len(SIZES) - 1, SIZES[-1]
    for k in range(len(SIZES) - 2, -1, -1):
        size = SIZES[k]
        needs = []
        for i in range(8):
            before = (i + (6 if i % 2 == 0 else 2)) % 8
            needs.append(twice[before] + jnp.maximum(twice[i] + once[i] - size, 0))
        fits = jnp.maximum(longest, functools.reduce(jnp.maximum, needs)) <= size
        chosen = jnp.where(fits, k, chosen)
        chosen_size = jnp.where(fits, size, chosen_size)
    class_ref[0] = chosen
    plan_ref[SIZE] = chosen_size


def places_kernel(pos_ref, plan_ref, t0, t1, t2, t3, out_ref, tab_ref, sems):
    copies = gather_tables((t0, t1, t2, t3), tab_ref, sems)
    for copy in copies:
        copy.start()
    for copy in copies:
        copy.wait()
    me = pos_ref[0]
    y, core = me >> 1, me & 1
    size = plan_ref[SIZE]
    for i in range(24):
        out_ref[TASKS + i] = 0

    def put(block, stage, way, position):
        other = way ^ core
        rest = ((stage == 0) & (size == sum(PACKED)) & (position >= PACKED[0])).astype(jnp.int32)
        place = (2 * other + rest) * 256 + position - PACKED[0] * rest
        out_ref[PLACE + block] = stage * (1 + other) * 65536 + place

    for way in (0, 1):
        near = 2 * ((y + (3 if way == 0 else 1)) & 3) + way
        far = 2 * ((y + 2) & 3) + way
        twice, passing = plan_ref[F_COUNT + near], plan_ref[F_COUNT + far]

        @functools.partial(loop, twice)
        def _(i):
            put(plan_ref[F_LIST + near * STRIDE + i], 0, way, i)

        @functools.partial(loop, plan_ref[D_COUNT + near])
        def _(i):
            late = (twice + i >= size).astype(jnp.int32)
            put(plan_ref[D_LIST + near * STRIDE + i], late, way, twice + i + late * (passing - size))

        @functools.partial(loop, passing)
        def _(i):
            put(plan_ref[F_LIST + far * STRIDE + i], 1, way, i)

    def add_task(own, block):
        place = out_ref[PLACE + block]
        row = (place >> 16) * BPD + own
        count = out_ref[TASKS + row]
        out_ref[TASK + row * ROW + count] = place & 65535
        out_ref[TASKS + row] = count + 1

    for s in range(1, 5):
        above, below = (me + s) & 7, (me - s) & 7

        @pl.when((above >> 1) != y)
        def _():
            @functools.partial(loop, tab_ref[COUNTS, s])
            def _(t):
                pair = tab_ref[s, t]
                add_task(pair >> 3, above * BPD + (pair & 7))

        @pl.when((below >> 1) != y)
        def _():
            row = (below ^ me) * 8

            @functools.partial(loop, tab_ref[row + COUNTS, s])
            def _(t):
                pair = tab_ref[row + s, t]
                add_task(pair & 7, below * BPD + (pair >> 3))


def start_from(id_, core, unit_ref, sib_ref, dst, sem):
    here = rows_of(id_ & 7)
    mine = ((id_ >> 3) & 1) == core

    @pl.when(mine)
    def _():
        pltpu.make_async_copy(unit_ref.at[here, :], dst, sem).start()

    @pl.when(jnp.logical_not(mine))
    def _():
        pltpu.make_async_copy(sib_ref.at[here, :], dst, sem).start()


def listed(plan_ref, row, i, chip):
    twice, once = plan_ref[F_COUNT + row], plan_ref[D_COUNT + row]
    from_f = plan_ref[F_LIST + row * STRIDE + jnp.clip(i, 0, 15)]
    from_d = plan_ref[D_LIST + row * STRIDE + jnp.clip(i - twice, 0, 15)]
    found = jnp.where(i < twice, from_f, from_d)
    return jnp.where(i < twice + once, found, chip * ON_CHIP)


def place_ref(ref, j):
    return ref.at[j * BLOCK : (j + 1) * BLOCK, :]


def slots_of(counts, refs):
    return [place_ref(ref, j) for ref, count in zip(refs, counts) for j in range(count)]


def first_pack_kernel(counts, pos_ref, plan_ref, unit_ref, sib_ref, *refs):
    y, core = pos_ref[0] >> 1, pos_ref[0] & 1
    slots = slots_of(counts, refs[:-1])
    for n, dst in enumerate(slots):
        block = listed(plan_ref, 2 * y + core, n, y)
        start_from(block, core, unit_ref, sib_ref, dst, refs[-1].at[n])
    for n, dst in enumerate(slots):
        pltpu.make_async_copy(place_ref(unit_ref, 0), dst, refs[-1].at[n]).wait()


def second_pack_kernel(counts, pos_ref, plan_ref, unit_ref, sib_ref, *refs):
    got, (piece_ref, sems) = slots_of(counts, refs[:-2]), refs[-2:]
    size = sum(counts)
    y, core = pos_ref[0] >> 1, pos_ref[0] & 1
    passing = plan_ref[F_COUNT + 2 * ((y + 3 + 2 * core) & 3) + core]
    for n in range(size):

        @pl.when(n < passing)
        def _():
            pltpu.make_async_copy(got[n], place_ref(piece_ref, n), sems.at[n]).start()

        @pl.when(n >= passing)
        def _():
            block = listed(plan_ref, 2 * y + core, n - passing + size, y)
            start_from(block, core, unit_ref, sib_ref, place_ref(piece_ref, n), sems.at[n])

    for n in range(size):
        pltpu.make_async_copy(place_ref(unit_ref, 0), place_ref(piece_ref, n), sems.at[n]).wait()


def own_kernel(pos_ref, tab_ref, surplus_ref, u_ref, sib_ref, acc_ref, kacc_ref, live_ref):
    core = pos_ref[0] & 1

    @functools.partial(loop, BPD * BPD)
    def _(i):
        live_ref[i] = 0.0

    def mark(a, b):
        live_ref[a * BPD + b] = 1.0
        live_ref[b * BPD + a] = 1.0

    @functools.partial(loop, tab_ref[COUNTS, 0])
    def _(t):
        pair = tab_ref[0, t]
        mark(pair >> 3, pair & 7)

    @functools.partial(loop, surplus_ref.shape[0])
    def _(t):
        @pl.when(surplus_ref[t, 2] == 1)
        def _():
            mark(surplus_ref[t, 0], surplus_ref[t, 1])

    step = OWN_STEP

    @functools.partial(loop, BPD // step)
    def _(part):
        here = pl.ds(pl.multiple_of(part * step * BLOCK, step * BLOCK), step * BLOCK)
        kernel = kernel_values(u_ref[here, :], u_ref[...])
        rows = []
        for i in range(step):
            parts = [
                kernel[i * BLOCK : (i + 1) * BLOCK, j * BLOCK : (j + 1) * BLOCK]
                * live_ref[(part * step + i) * BPD + j]
                for j in range(BPD)
            ]
            kacc_ref[rows_of(part * step + i), :] = sum(parts)
            rows.append(jnp.concatenate(parts, axis=1).astype(jnp.bfloat16))
        acc_ref[here, :] = jnp.dot(
            jnp.concatenate(rows, axis=0), u_ref[...], preferred_element_type=jnp.float32
        )

    @functools.partial(loop, tab_ref[core * 8 + COUNTS, 1])
    def _(t):
        pair = tab_ref[core * 8 + 1, t]
        a, b = pair >> 3, pair & 7
        mine, other = jnp.where(core == 0, a, b), jnp.where(core == 0, b, a)
        add_terms(u_ref, sib_ref, acc_ref, kacc_ref, mine, other)


def each_task(part, task_ref, own, pieces, q_ref, body):
    row = part * BPD + own
    count = task_ref[TASKS + row]

    @functools.partial(loop, (count + 1) >> 1)
    def _(i):
        second = jnp.minimum(2 * i + 1, count - 1)
        for half, t in enumerate((2 * i, second)):
            place = task_ref[TASK + row * ROW + t]
            for n, piece in pieces:

                @pl.when((place >> 8) == n)
                def _():
                    q_ref[half * BLOCK : (half + 1) * BLOCK, :] = piece[rows_of(place & 255), :]

        body(q_ref[...], jnp.where(2 * i + 1 < count, 1.0, 0.0))


def two_kernels(p, q, weight):
    kernel = kernel_values(p, q)
    first, second = kernel[:, :BLOCK], kernel[:, BLOCK:] * weight
    low = jnp.concatenate([first, second], axis=1).astype(jnp.bfloat16)
    return first + second, jnp.dot(low, q, preferred_element_type=jnp.float32)


def numbered(here, there):
    return [*enumerate(here), *enumerate(there, 2)]


def part_kernel(part, here, task_ref, u_ref, acc_in, kacc_in, *refs):
    pieces, (acc_ref, kacc_ref, q_ref) = numbered(refs[:here], refs[here:-3]), refs[-3:]
    acc_ref[...] = acc_in[...]
    kacc_ref[...] = kacc_in[...]

    @functools.partial(loop, BPD)
    def _(own):
        here = rows_of(own)

        def add(q, weight):
            kernel, terms = two_kernels(u_ref[here, :], q, weight)
            kacc_ref[here, :] += kernel
            acc_ref[here, :] += terms

        each_task(part, task_ref, own, pieces, q_ref, add)


def last_kernel(task_ref, u_ref, acc_in, kacc_in, *refs):
    got, (out_ref, log_ref, acc_ref, kacc_ref, q_ref, done_ref, sems) = refs[:-7], refs[-7:]
    pieces = numbered((), got)
    rows = lax.broadcasted_iota(jnp.int32, (BLOCK, BLOCK), 0)
    diagonal = rows == lax.broadcasted_iota(jnp.int32, (BLOCK, BLOCK), 1)

    def out_copy(own):
        here = rows_of(own)
        return pltpu.make_async_copy(done_ref.at[here, :], out_ref.at[here, :], sems.at[own])

    @functools.partial(loop, BPD)
    def _(own):
        here = rows_of(own)
        acc_ref[...] = acc_in[here, :]
        kacc_ref[...] = kacc_in[here, :]

        def add(q, weight):
            kernel, terms = two_kernels(u_ref[here, :], q, weight)
            kacc_ref[...] += kernel
            acc_ref[...] += terms

        each_task(2, task_ref, own, pieces, q_ref, add)
        density = jnp.sum(kacc_ref[...], axis=1, keepdims=True)
        done_ref[here, :] = (
            u_ref[here, :].astype(jnp.float32) - acc_ref[...] * (1.0 / density)
        ).astype(jnp.bfloat16)
        out_copy(own).start()
        across = jnp.sum(jnp.where(diagonal, density, 0.0), axis=0, keepdims=True)
        log_ref[pl.ds(own, 1), :] = jnp.log(across)

    for own in range(BPD):
        out_copy(own).wait()


SMEM = pl.BlockSpec(memory_space=pltpu.SMEM)
VMEM = pl.BlockSpec(memory_space=pltpu.VMEM)
ANY = pl.BlockSpec(memory_space=pl.ANY)
HBM = pl.BlockSpec(memory_space=pltpu.HBM)


def params():
    return pltpu.CompilerParams(vmem_limit_bytes=26 * 2**20)


COST = pl.CostEstimate(flops=1, bytes_accessed=1, transcendentals=0)


def pieces_of(counts, width):
    return tuple(jax.ShapeDtypeStruct((count * BLOCK, width), jnp.bfloat16) for count in counts)


def pack(kernel, name, counts, out, *operands):
    return pl.pallas_call(
        functools.partial(kernel, counts),
        in_specs=[SMEM, SMEM] + [ANY] * (len(operands) - 2),
        out_specs=(VMEM,) * len(out),
        out_shape=pieces_of(out, operands[2].shape[1]),
        scratch_shapes=[pltpu.SemaphoreType.DMA((sum(counts),))],
        compiler_params=params(),
        name=name,
    )(*operands)


def exchange_and_score(size, packed, pos, plan, tables, surplus, unit, sib):
    rows, width = unit.shape
    sums = (
        jax.ShapeDtypeStruct((rows, width), jnp.float32),
        jax.ShapeDtypeStruct((rows, BLOCK), jnp.float32),
    )

    counts = first_pieces(size)
    if size > sum(PACKED):
        packed = pack(first_pack_kernel, "first_pack", counts, counts, pos, plan, unit, sib)
    got = [both_ways(x) for x in packed[: len(counts)]]
    places = pl.pallas_call(
        places_kernel,
        in_specs=[SMEM, SMEM] + [VMEM] * 4,
        out_specs=SMEM,
        out_shape=jax.ShapeDtypeStruct((PLACES,), jnp.int32),
        scratch_shapes=[pltpu.SMEM((OWNERS * 8, 128), jnp.int32), pltpu.SemaphoreType.DMA((4,))],
        cost_estimate=COST,
        compiler_params=params(),
        name="places",
    )(pos, plan, *tables)
    acc, kacc = pl.pallas_call(
        own_kernel,
        in_specs=[SMEM, SMEM, SMEM, VMEM, VMEM],
        out_specs=(VMEM, VMEM),
        out_shape=sums,
        scratch_shapes=[pltpu.SMEM((BPD * BPD,), jnp.float32)],
        compiler_params=params(),
        cost_estimate=COST,
        name="own_pairs",
    )(pos, tables[0], surplus, unit, sib)
    *got, acc = lax.optimization_barrier((*got, acc))
    sent = pack(second_pack_kernel, "second_pack", counts, (size,), pos, plan, unit, sib, *got)
    far = [both_ways(x) for x in sent]

    def add_part(part, acc, kacc, here, there):
        return pl.pallas_call(
            functools.partial(part_kernel, part, len(here)),
            in_specs=[SMEM] + [VMEM] * (3 + len(here) + len(there)),
            out_specs=(VMEM, VMEM),
            out_shape=sums,
            scratch_shapes=[pltpu.VMEM((2 * BLOCK, width), jnp.bfloat16)],
            compiler_params=params(),
            cost_estimate=COST,
            name=f"part{part}",
        )(places, unit, acc, kacc, *here, *there)

    acc, kacc = add_part(0, acc, kacc, got, [to_sibling(x) for x in got])
    *far, acc = lax.optimization_barrier((*far, acc))
    sib_far = [to_sibling(x) for x in far]
    acc, kacc = add_part(1, acc, kacc, far, [])
    *sib_far, acc = lax.optimization_barrier((*sib_far, acc))
    return pl.pallas_call(
        last_kernel,
        in_specs=[SMEM] + [VMEM] * (3 + len(far)),
        out_specs=(ANY, VMEM),
        out_shape=(
            jax.ShapeDtypeStruct((rows, width), jnp.bfloat16),
            jax.ShapeDtypeStruct((BPD, BLOCK), jnp.float32),
        ),
        scratch_shapes=[
            pltpu.VMEM((BLOCK, width), jnp.float32),
            pltpu.VMEM((BLOCK, BLOCK), jnp.float32),
            pltpu.VMEM((2 * BLOCK, width), jnp.bfloat16),
            pltpu.VMEM((rows, width), jnp.bfloat16),
            pltpu.SemaphoreType.DMA((BPD,)),
        ],
        compiler_params=params(),
        cost_estimate=COST,
        name="last_part",
    )(places, unit, acc, kacc, *sib_far)


def shards(embeddings, home_pairs, home_count, surplus_pairs):
    rows, width = embeddings.shape
    pairs, count = home_pairs[0, 0], home_count[0, 0]
    shifts = pairs.shape[0]
    pos = lax.axis_index("owner").astype(jnp.int32).reshape(1)

    step = 128
    unit = pl.pallas_call(
        normalize_kernel,
        grid=(rows // step,),
        in_specs=[pl.BlockSpec((step, width), lambda i: (i, 0))],
        out_specs=pl.BlockSpec((step, width), lambda i: (i, 0)),
        out_shape=jax.ShapeDtypeStruct(embeddings.shape, jnp.bfloat16),
        cost_estimate=COST,
        compiler_params=params(),
        name="normalize",
    )(embeddings)

    table = pl.pallas_call(
        table_kernel,
        in_specs=[HBM, HBM],
        scratch_shapes=[
            pltpu.VMEM((shifts, 2, pairs.shape[1]), jnp.int32),
            pltpu.VMEM((1, shifts), jnp.int32),
            pltpu.SemaphoreType.DMA((2,)),
        ],
        out_specs=VMEM,
        out_shape=jax.ShapeDtypeStruct((8, 128), jnp.int32),
        compiler_params=params(),
        cost_estimate=COST,
        name="table",
    )(jnp.swapaxes(pairs, 1, 2), count[None])

    def turned(x, bits):
        return lax.ppermute(x, "owner", [(o, o ^ bits) for o in range(OWNERS)])

    came, unit = lax.optimization_barrier((turned(table, 1), unit))
    sib = to_sibling(unit)
    tables = jnp.concatenate([table, came], axis=0)
    tables = [tables] + [turned(tables, bits) for bits in (2, 4, 6)]

    out = pieces_of(PACKED, width)
    plan, chosen, *packed = pl.pallas_call(
        functools.partial(plan_and_pack_kernel, PACKED),
        in_specs=[SMEM] + [VMEM] * 4 + [ANY] * 2,
        out_specs=(SMEM, SMEM) + (VMEM,) * len(out),
        out_shape=(
            jax.ShapeDtypeStruct((PLAN,), jnp.int32),
            jax.ShapeDtypeStruct((1,), jnp.int32),
            *out,
        ),
        scratch_shapes=[
            pltpu.SMEM((OWNERS * 8, 128), jnp.int32),
            pltpu.SemaphoreType.DMA((4,)),
            pltpu.SemaphoreType.DMA((sum(PACKED),)),
        ],
        compiler_params=params(),
        name="plan",
    )(pos, *tables, unit, sib)

    centered, log_density = lax.switch(
        chosen[0],
        [functools.partial(exchange_and_score, size) for size in SIZES],
        packed, pos, plan, tables, surplus_pairs[0, 0], unit, sib,
    )
    return centered, log_density.reshape(rows)


def solution(mesh):
    return jax.shard_map(
        shards,
        mesh=mesh,
        in_specs=(
            P(("group", "owner"), None),
            P("group", "owner", None, None, None),
            P("group", "owner", None),
            P("group", "owner", None, None),
        ),
        out_specs=(P(("group", "owner"), None), P(("group", "owner"))),
        check_vma=False,
    )
```

```python
import functools

import jax
import jax.numpy as jnp
from jax import lax
from jax.experimental import pallas as pl
from jax.experimental.pallas import tpu as pltpu
from jax.sharding import PartitionSpec as P

BLOCK = 128
BPD = 8
CHIPS = 4
OWNERS = 8
BLOCKS = OWNERS * BPD
ON_CHIP = 2 * BPD
sharpness = 4.0
epsilon = 1e-06
SIZES = (5, 6, 8, 16)
PACKED = (3, 2, 1)


def first_pieces(size):
    return {5: PACKED[:2], 6: PACKED}.get(size, (size,))


OWN_STEP = 2
COUNTS = 5

STRIDE = 32
F_COUNT, D_COUNT, LOAD, SIZE, NEED, TOUCHED, FAR, F_LIST, D_LIST = 0, 8, 16, 24, 32, 96, 161, 256, 512
PLAN = 768
TASKS, TASK, PLACE = 0, 24, 1560
ROW = 64
PLACES = 1664


def loop(count, body):
    def step(i, carry):
        body(i)
        return carry

    lax.fori_loop(0, count, step, 0)


def both_ways(x):
    route = [(o, ((o // 2 + (1 if o % 2 == 0 else -1)) % CHIPS) * 2 + o % 2) for o in range(OWNERS)]
    return lax.ppermute(x, "owner", route)


def to_sibling(x):
    return lax.ppermute(x, "owner", [(o, o ^ 1) for o in range(OWNERS)])


def normalize_kernel(x_ref, u_ref):
    wide = x_ref[...].astype(jnp.float32)
    mean = jnp.mean(wide * wide, axis=-1, keepdims=True)
    u_ref[...] = (wide * lax.rsqrt(mean + epsilon)).astype(jnp.bfloat16)


def table_kernel(pairs_hbm, count_hbm, out_ref, pairs_ref, count_ref, sems):
    copies = [
        pltpu.make_async_copy(pairs_hbm, pairs_ref, sems.at[0]),
        pltpu.make_async_copy(count_hbm, count_ref, sems.at[1]),
    ]
    for copy in copies:
        copy.start()
    out_ref[...] = jnp.zeros_like(out_ref)
    for copy in copies:
        copy.wait()
    shifts, _, slots = pairs_ref.shape
    for s in range(shifts):
        out_ref[s : s + 1, 0:slots] = pairs_ref[s, 0:1, :] * 8 + pairs_ref[s, 1:2, :]
    out_ref[COUNTS : COUNTS + 1, 0:shifts] = count_ref[...]


def rows_of(block):
    return pl.ds(pl.multiple_of(block * BLOCK, BLOCK), BLOCK)


def kernel_values(p, q):
    dots = lax.dot_general(p, q, (((1,), (1,)), ((), ())), preferred_element_type=jnp.float32)
    return jnp.exp(sharpness * (dots * (1.0 / q.shape[1]) - 1.0))


def add_terms(u_ref, q_ref, acc_ref, kacc_ref, mine, other):
    q = q_ref[rows_of(other), :]
    kernel = kernel_values(u_ref[rows_of(mine), :], q)
    kacc_ref[rows_of(mine), :] += kernel
    acc_ref[rows_of(mine), :] += jnp.dot(
        kernel.astype(jnp.bfloat16), q, preferred_element_type=jnp.float32
    )


def gather_tables(tables, tab_ref, sems):
    return [
        pltpu.make_async_copy(t, tab_ref.at[i * 16 : (i + 1) * 16, :], sems.at[i])
        for i, t in enumerate(tables)
    ]


def plan_and_pack_kernel(counts, pos_ref, t0, t1, t2, t3, unit_ref, sib_ref, plan_ref, class_ref, *refs):
    pieces, (tab_ref, sems, pack_sems) = refs[:-3], refs[-3:]
    plan_kernel(pos_ref, t0, t1, t2, t3, plan_ref, class_ref, tab_ref, sems)
    first_pack_kernel(counts, pos_ref, plan_ref, unit_ref, sib_ref, *pieces, pack_sems)


def plan_kernel(pos_ref, t0, t1, t2, t3, plan_ref, class_ref, tab_ref, sems):
    copies = gather_tables((t0, t1, t2, t3), tab_ref, sems)
    for copy in copies:
        copy.start()
    me = pos_ref[0]
    for i in range(8):
        plan_ref[LOAD + i] = 0
        plan_ref[F_COUNT + i] = 0
        plan_ref[D_COUNT + i] = 0
    for i in range(BLOCKS):
        plan_ref[NEED + i] = 0
    for copy in copies:
        copy.wait()

    def of_owner(o, touched):
        row = (o ^ me) * 8
        for s in range(1, 5):
            q = (o + s) & 7
            to_q, to_o = lax.shift_left(1, q >> 1), lax.shift_left(1, o >> 1)

            def of_pair(t, touched):
                pair = tab_ref[row + s, t]
                for block, chip in ((o * BPD + (pair >> 3), to_q), (q * BPD + (pair & 7), to_o)):
                    before = plan_ref[NEED + block]
                    plan_ref[NEED + block] = before | chip
                    plan_ref[TOUCHED + touched] = block
                    touched = touched + (before == 0).astype(jnp.int32)
                return touched

            touched = lax.fori_loop(0, tab_ref[row + COUNTS, s], of_pair, touched)
        return touched

    touched = lax.fori_loop(0, OWNERS, of_owner, 0)

    def needs(block):
        mask, chip = plan_ref[NEED + block], block >> 4
        bit = lambda hop: lax.shift_right_logical(mask, (chip + hop) & 3) & 1
        return chip, bit(1), bit(3), bit(2)

    def append(count, table, at, block, wanted):
        held = plan_ref[count + at]
        plan_ref[table + at * STRIDE + held] = block
        plan_ref[count + at] = held + wanted

    def one_hop(i, fars):
        block = plan_ref[TOUCHED + i]
        chip, up, down, far = needs(block)
        at = 2 * chip
        plan_ref[LOAD + at] = plan_ref[LOAD + at] + up
        plan_ref[LOAD + at + 1] = plan_ref[LOAD + at + 1] + down
        append(D_COUNT, D_LIST, at, block, up & (1 - far))
        append(D_COUNT, D_LIST, at + 1, block, down & (1 - far))
        plan_ref[FAR + fars] = block
        return fars + far

    fars = lax.fori_loop(0, touched, one_hop, 0)

    @functools.partial(loop, fars)
    def _(i):
        block = plan_ref[FAR + i]
        chip, up, down, _ = needs(block)
        costs, loads = [], []
        for way, near, hop in ((0, up, 1), (1, down, 3)):
            at, after = 2 * chip + way, 2 * ((chip + hop) & 3) + way
            here, there = plan_ref[LOAD + at] + 1 - near, plan_ref[LOAD + after] + 1
            most = jnp.maximum(jnp.maximum(here, there), 2 * plan_ref[F_COUNT + at] + 2)
            costs.append(most * 64 + here + there + 32 * (1 - near))
            loads.append((at, after, here, there))
        goes_down = costs[0] > costs[1]
        at, after, here, there = (jnp.where(goes_down, b, a) for a, b in zip(*loads))
        plan_ref[LOAD + at] = here
        plan_ref[LOAD + after] = there
        append(F_COUNT, F_LIST, at, block, 1)
        append(D_COUNT, D_LIST, at ^ 1, block, jnp.where(goes_down, up, down))

    twice = [plan_ref[F_COUNT + i] for i in range(8)]
    once = [plan_ref[D_COUNT + i] for i in range(8)]
    longest = functools.reduce(jnp.maximum, twice)
    chosen, chosen_size = len(SIZES) - 1, SIZES[-1]
    for k in range(len(SIZES) - 2, -1, -1):
        size = SIZES[k]
        needs = []
        for i in range(8):
            before = (i + (6 if i % 2 == 0 else 2)) % 8
            needs.append(twice[before] + jnp.maximum(twice[i] + once[i] - size, 0))
        fits = jnp.maximum(longest, functools.reduce(jnp.maximum, needs)) <= size
        chosen = jnp.where(fits, k, chosen)
        chosen_size = jnp.where(fits, size, chosen_size)
    class_ref[0] = chosen
    plan_ref[SIZE] = chosen_size


def places_kernel(pos_ref, plan_ref, t0, t1, t2, t3, out_ref, tab_ref, sems):
    copies = gather_tables((t0, t1, t2, t3), tab_ref, sems)
    for copy in copies:
        copy.start()
    for copy in copies:
        copy.wait()
    me = pos_ref[0]
    y, core = me >> 1, me & 1
    size = plan_ref[SIZE]
    for i in range(24):
        out_ref[TASKS + i] = 0

    split = size <= sum(PACKED)

    def put(block, stage, way, position):
        other = way ^ core
        piece, begin = 0, 0
        for n in (1, 2):
            after = split & (stage == 0) & (position >= sum(PACKED[:n]))
            piece, begin = jnp.where(after, n, piece), jnp.where(after, sum(PACKED[:n]), begin)
        out_ref[PLACE + block] = stage * (1 + other) * 65536 + (3 * other + piece) * 256 + position - begin

    for way in (0, 1):
        near = 2 * ((y + (3 if way == 0 else 1)) & 3) + way
        far = 2 * ((y + 2) & 3) + way
        twice, passing = plan_ref[F_COUNT + near], plan_ref[F_COUNT + far]

        @functools.partial(loop, twice)
        def _(i):
            put(plan_ref[F_LIST + near * STRIDE + i], 0, way, i)

        @functools.partial(loop, plan_ref[D_COUNT + near])
        def _(i):
            late = (twice + i >= size).astype(jnp.int32)
            put(plan_ref[D_LIST + near * STRIDE + i], late, way, twice + i + late * (passing - size))

        @functools.partial(loop, passing)
        def _(i):
            put(plan_ref[F_LIST + far * STRIDE + i], 1, way, i)

    def add_task(own, block):
        place = out_ref[PLACE + block]
        row = (place >> 16) * BPD + own
        count = out_ref[TASKS + row]
        out_ref[TASK + row * ROW + count] = place & 65535
        out_ref[TASKS + row] = count + 1

    for s in range(1, 5):
        above, below = (me + s) & 7, (me - s) & 7

        @pl.when((above >> 1) != y)
        def _():
            @functools.partial(loop, tab_ref[COUNTS, s])
            def _(t):
                pair = tab_ref[s, t]
                add_task(pair >> 3, above * BPD + (pair & 7))

        @pl.when((below >> 1) != y)
        def _():
            row = (below ^ me) * 8

            @functools.partial(loop, tab_ref[row + COUNTS, s])
            def _(t):
                pair = tab_ref[row + s, t]
                add_task(pair & 7, below * BPD + (pair >> 3))


def start_from(id_, core, unit_ref, sib_ref, dst, sem):
    here = rows_of(id_ & 7)
    mine = ((id_ >> 3) & 1) == core

    @pl.when(mine)
    def _():
        pltpu.make_async_copy(unit_ref.at[here, :], dst, sem).start()

    @pl.when(jnp.logical_not(mine))
    def _():
        pltpu.make_async_copy(sib_ref.at[here, :], dst, sem).start()


def listed(plan_ref, row, i, chip):
    twice, once = plan_ref[F_COUNT + row], plan_ref[D_COUNT + row]
    from_f = plan_ref[F_LIST + row * STRIDE + jnp.clip(i, 0, 15)]
    from_d = plan_ref[D_LIST + row * STRIDE + jnp.clip(i - twice, 0, 15)]
    found = jnp.where(i < twice, from_f, from_d)
    return jnp.where(i < twice + once, found, chip * ON_CHIP)


def place_ref(ref, j):
    return ref.at[j * BLOCK : (j + 1) * BLOCK, :]


def slots_of(counts, refs):
    return [place_ref(ref, j) for ref, count in zip(refs, counts) for j in range(count)]


def first_pack_kernel(counts, pos_ref, plan_ref, unit_ref, sib_ref, *refs):
    y, core = pos_ref[0] >> 1, pos_ref[0] & 1
    slots = slots_of(counts, refs[:-1])
    for n, dst in enumerate(slots):
        block = listed(plan_ref, 2 * y + core, n, y)
        start_from(block, core, unit_ref, sib_ref, dst, refs[-1].at[n])
    for n, dst in enumerate(slots):
        pltpu.make_async_copy(place_ref(unit_ref, 0), dst, refs[-1].at[n]).wait()


def second_pack_kernel(counts, pos_ref, plan_ref, unit_ref, sib_ref, *refs):
    got, (piece_ref, sems) = slots_of(counts, refs[:-2]), refs[-2:]
    size = sum(counts)
    y, core = pos_ref[0] >> 1, pos_ref[0] & 1
    passing = plan_ref[F_COUNT + 2 * ((y + 3 + 2 * core) & 3) + core]
    for n in range(size):

        @pl.when(n < passing)
        def _():
            pltpu.make_async_copy(got[n], place_ref(piece_ref, n), sems.at[n]).start()

        @pl.when(n >= passing)
        def _():
            block = listed(plan_ref, 2 * y + core, n - passing + size, y)
            start_from(block, core, unit_ref, sib_ref, place_ref(piece_ref, n), sems.at[n])

    for n in range(size):
        pltpu.make_async_copy(place_ref(unit_ref, 0), place_ref(piece_ref, n), sems.at[n]).wait()


def own_kernel(pos_ref, tab_ref, surplus_ref, u_ref, sib_ref, acc_ref, kacc_ref, live_ref):
    core = pos_ref[0] & 1

    @functools.partial(loop, BPD * BPD)
    def _(i):
        live_ref[i] = 0.0

    def mark(a, b):
        live_ref[a * BPD + b] = 1.0
        live_ref[b * BPD + a] = 1.0

    @functools.partial(loop, tab_ref[COUNTS, 0])
    def _(t):
        pair = tab_ref[0, t]
        mark(pair >> 3, pair & 7)

    @functools.partial(loop, surplus_ref.shape[0])
    def _(t):
        @pl.when(surplus_ref[t, 2] == 1)
        def _():
            mark(surplus_ref[t, 0], surplus_ref[t, 1])

    step = OWN_STEP

    @functools.partial(loop, BPD // step)
    def _(part):
        here = pl.ds(pl.multiple_of(part * step * BLOCK, step * BLOCK), step * BLOCK)
        kernel = kernel_values(u_ref[here, :], u_ref[...])
        rows = []
        for i in range(step):
            parts = [
                kernel[i * BLOCK : (i + 1) * BLOCK, j * BLOCK : (j + 1) * BLOCK]
                * live_ref[(part * step + i) * BPD + j]
                for j in range(BPD)
            ]
            kacc_ref[rows_of(part * step + i), :] = sum(parts)
            rows.append(jnp.concatenate(parts, axis=1).astype(jnp.bfloat16))
        acc_ref[here, :] = jnp.dot(
            jnp.concatenate(rows, axis=0), u_ref[...], preferred_element_type=jnp.float32
        )

    @functools.partial(loop, tab_ref[core * 8 + COUNTS, 1])
    def _(t):
        pair = tab_ref[core * 8 + 1, t]
        a, b = pair >> 3, pair & 7
        mine, other = jnp.where(core == 0, a, b), jnp.where(core == 0, b, a)
        add_terms(u_ref, sib_ref, acc_ref, kacc_ref, mine, other)


def each_task(part, task_ref, own, pieces, q_ref, body):
    row = part * BPD + own
    count = task_ref[TASKS + row]

    @functools.partial(loop, (count + 1) >> 1)
    def _(i):
        second = jnp.minimum(2 * i + 1, count - 1)
        for half, t in enumerate((2 * i, second)):
            place = task_ref[TASK + row * ROW + t]
            for n, piece in pieces:

                @pl.when((place >> 8) == n)
                def _():
                    q_ref[half * BLOCK : (half + 1) * BLOCK, :] = piece[rows_of(place & 255), :]

        body(q_ref[...], jnp.where(2 * i + 1 < count, 1.0, 0.0))


def two_kernels(p, q, weight):
    kernel = kernel_values(p, q)
    first, second = kernel[:, :BLOCK], kernel[:, BLOCK:] * weight
    low = jnp.concatenate([first, second], axis=1).astype(jnp.bfloat16)
    return first + second, jnp.dot(low, q, preferred_element_type=jnp.float32)


def numbered(here, there):
    return [*enumerate(here), *enumerate(there, 3)]


def part_kernel(part, here, task_ref, u_ref, acc_in, kacc_in, *refs):
    pieces, (acc_ref, kacc_ref, q_ref) = numbered(refs[:here], refs[here:-3]), refs[-3:]
    acc_ref[...] = acc_in[...]
    kacc_ref[...] = kacc_in[...]

    @functools.partial(loop, BPD)
    def _(own):
        here = rows_of(own)

        def add(q, weight):
            kernel, terms = two_kernels(u_ref[here, :], q, weight)
            kacc_ref[here, :] += kernel
            acc_ref[here, :] += terms

        each_task(part, task_ref, own, pieces, q_ref, add)


def last_kernel(task_ref, u_ref, acc_in, kacc_in, *refs):
    got, (out_ref, log_ref, acc_ref, kacc_ref, q_ref, done_ref, sems) = refs[:-7], refs[-7:]
    pieces = numbered((), got)
    rows = lax.broadcasted_iota(jnp.int32, (BLOCK, BLOCK), 0)
    diagonal = rows == lax.broadcasted_iota(jnp.int32, (BLOCK, BLOCK), 1)

    def out_copy(own):
        here = rows_of(own)
        return pltpu.make_async_copy(done_ref.at[here, :], out_ref.at[here, :], sems.at[own])

    @functools.partial(loop, BPD)
    def _(own):
        here = rows_of(own)
        acc_ref[...] = acc_in[here, :]
        kacc_ref[...] = kacc_in[here, :]

        def add(q, weight):
            kernel, terms = two_kernels(u_ref[here, :], q, weight)
            kacc_ref[...] += kernel
            acc_ref[...] += terms

        each_task(2, task_ref, own, pieces, q_ref, add)
        density = jnp.sum(kacc_ref[...], axis=1, keepdims=True)
        done_ref[here, :] = (
            u_ref[here, :].astype(jnp.float32) - acc_ref[...] * (1.0 / density)
        ).astype(jnp.bfloat16)
        out_copy(own).start()
        across = jnp.sum(jnp.where(diagonal, density, 0.0), axis=0, keepdims=True)
        log_ref[pl.ds(own, 1), :] = jnp.log(across)

    for own in range(BPD):
        out_copy(own).wait()


SMEM = pl.BlockSpec(memory_space=pltpu.SMEM)
VMEM = pl.BlockSpec(memory_space=pltpu.VMEM)
ANY = pl.BlockSpec(memory_space=pl.ANY)
HBM = pl.BlockSpec(memory_space=pltpu.HBM)


def params():
    return pltpu.CompilerParams(vmem_limit_bytes=26 * 2**20)


COST = pl.CostEstimate(flops=1, bytes_accessed=1, transcendentals=0)


def pieces_of(counts, width):
    return tuple(jax.ShapeDtypeStruct((count * BLOCK, width), jnp.bfloat16) for count in counts)


def pack(kernel, name, counts, out, *operands):
    return pl.pallas_call(
        functools.partial(kernel, counts),
        in_specs=[SMEM, SMEM] + [ANY] * (len(operands) - 2),
        out_specs=(VMEM,) * len(out),
        out_shape=pieces_of(out, operands[2].shape[1]),
        scratch_shapes=[pltpu.SemaphoreType.DMA((sum(counts),))],
        compiler_params=params(),
        name=name,
    )(*operands)


def exchange_and_score(size, packed, pos, plan, tables, surplus, unit, sib):
    rows, width = unit.shape
    sums = (
        jax.ShapeDtypeStruct((rows, width), jnp.float32),
        jax.ShapeDtypeStruct((rows, BLOCK), jnp.float32),
    )

    counts = first_pieces(size)
    if size > sum(PACKED):
        packed = pack(first_pack_kernel, "first_pack", counts, counts, pos, plan, unit, sib)
    got = [both_ways(x) for x in packed[: len(counts)]]
    places = pl.pallas_call(
        places_kernel,
        in_specs=[SMEM, SMEM] + [VMEM] * 4,
        out_specs=SMEM,
        out_shape=jax.ShapeDtypeStruct((PLACES,), jnp.int32),
        scratch_shapes=[pltpu.SMEM((OWNERS * 8, 128), jnp.int32), pltpu.SemaphoreType.DMA((4,))],
        cost_estimate=COST,
        compiler_params=params(),
        name="places",
    )(pos, plan, *tables)
    acc, kacc = pl.pallas_call(
        own_kernel,
        in_specs=[SMEM, SMEM, SMEM, VMEM, VMEM],
        out_specs=(VMEM, VMEM),
        out_shape=sums,
        scratch_shapes=[pltpu.SMEM((BPD * BPD,), jnp.float32)],
        compiler_params=params(),
        cost_estimate=COST,
        name="own_pairs",
    )(pos, tables[0], surplus, unit, sib)
    *got, acc = lax.optimization_barrier((*got, acc))
    sent = pack(second_pack_kernel, "second_pack", counts, (size,), pos, plan, unit, sib, *got)
    far = [both_ways(x) for x in sent]
    *got, _ = lax.optimization_barrier((*got, *sent))

    def add_part(part, acc, kacc, here, there):
        return pl.pallas_call(
            functools.partial(part_kernel, part, len(here)),
            in_specs=[SMEM] + [VMEM] * (3 + len(here) + len(there)),
            out_specs=(VMEM, VMEM),
            out_shape=sums,
            scratch_shapes=[pltpu.VMEM((2 * BLOCK, width), jnp.bfloat16)],
            compiler_params=params(),
            cost_estimate=COST,
            name=f"part{part}",
        )(places, unit, acc, kacc, *here, *there)

    acc, kacc = add_part(0, acc, kacc, got, [to_sibling(x) for x in got])
    *far, acc = lax.optimization_barrier((*far, acc))
    sib_far = [to_sibling(x) for x in far]
    acc, kacc = add_part(1, acc, kacc, far, [])
    *sib_far, acc = lax.optimization_barrier((*sib_far, acc))
    return pl.pallas_call(
        last_kernel,
        in_specs=[SMEM] + [VMEM] * (3 + len(far)),
        out_specs=(ANY, VMEM),
        out_shape=(
            jax.ShapeDtypeStruct((rows, width), jnp.bfloat16),
            jax.ShapeDtypeStruct((BPD, BLOCK), jnp.float32),
        ),
        scratch_shapes=[
            pltpu.VMEM((BLOCK, width), jnp.float32),
            pltpu.VMEM((BLOCK, BLOCK), jnp.float32),
            pltpu.VMEM((2 * BLOCK, width), jnp.bfloat16),
            pltpu.VMEM((rows, width), jnp.bfloat16),
            pltpu.SemaphoreType.DMA((BPD,)),
        ],
        compiler_params=params(),
        cost_estimate=COST,
        name="last_part",
    )(places, unit, acc, kacc, *sib_far)


def shards(embeddings, home_pairs, home_count, surplus_pairs):
    rows, width = embeddings.shape
    pairs, count = home_pairs[0, 0], home_count[0, 0]
    shifts = pairs.shape[0]
    pos = lax.axis_index("owner").astype(jnp.int32).reshape(1)

    step = 128
    unit = pl.pallas_call(
        normalize_kernel,
        grid=(rows // step,),
        in_specs=[pl.BlockSpec((step, width), lambda i: (i, 0))],
        out_specs=pl.BlockSpec((step, width), lambda i: (i, 0)),
        out_shape=jax.ShapeDtypeStruct(embeddings.shape, jnp.bfloat16),
        cost_estimate=COST,
        compiler_params=params(),
        name="normalize",
    )(embeddings)

    table = pl.pallas_call(
        table_kernel,
        in_specs=[HBM, HBM],
        scratch_shapes=[
            pltpu.VMEM((shifts, 2, pairs.shape[1]), jnp.int32),
            pltpu.VMEM((1, shifts), jnp.int32),
            pltpu.SemaphoreType.DMA((2,)),
        ],
        out_specs=VMEM,
        out_shape=jax.ShapeDtypeStruct((8, 128), jnp.int32),
        compiler_params=params(),
        cost_estimate=COST,
        name="table",
    )(jnp.swapaxes(pairs, 1, 2), count[None])

    def turned(x, bits):
        return lax.ppermute(x, "owner", [(o, o ^ bits) for o in range(OWNERS)])

    came, unit = lax.optimization_barrier((turned(table, 1), unit))
    sib = to_sibling(unit)
    tables = jnp.concatenate([table, came], axis=0)
    tables = [tables] + [turned(tables, bits) for bits in (2, 4, 6)]

    out = pieces_of(PACKED, width)
    plan, chosen, *packed = pl.pallas_call(
        functools.partial(plan_and_pack_kernel, PACKED),
        in_specs=[SMEM] + [VMEM] * 4 + [ANY] * 2,
        out_specs=(SMEM, SMEM) + (VMEM,) * len(out),
        out_shape=(
            jax.ShapeDtypeStruct((PLAN,), jnp.int32),
            jax.ShapeDtypeStruct((1,), jnp.int32),
            *out,
        ),
        scratch_shapes=[
            pltpu.SMEM((OWNERS * 8, 128), jnp.int32),
            pltpu.SemaphoreType.DMA((4,)),
            pltpu.SemaphoreType.DMA((sum(PACKED),)),
        ],
        compiler_params=params(),
        name="plan",
    )(pos, *tables, unit, sib)

    centered, log_density = lax.switch(
        chosen[0],
        [functools.partial(exchange_and_score, size) for size in SIZES],
        packed, pos, plan, tables, surplus_pairs[0, 0], unit, sib,
    )
    return centered, log_density.reshape(rows)


def solution(mesh):
    return jax.shard_map(
        shards,
        mesh=mesh,
        in_specs=(
            P(("group", "owner"), None),
            P("group", "owner", None, None, None),
            P("group", "owner", None),
            P("group", "owner", None, None),
        ),
        out_specs=(P(("group", "owner"), None), P(("group", "owner"))),
        check_vma=False,
    )
```
